128 devices in a mesh: seq: 8 (over y, core), own: 16 (over x, z).
Axes of the slice: x: 4, y: 4, z: 4, core: 2. Of those that a mesh axis runs over, the one named last changes fastest.
Arguments:
- d_out: bfloat16 [32, 2048, 512], P('own', 'seq'), may hold values from -6 to 6
- weight_in: bfloat16 [512, 2048], replicated, may hold values from -0.25 to 0.25
- weight_out: bfloat16 [512, 512], replicated, may hold values from -0.25 to 0.25
- hot_table: bfloat16 [512, 512], replicated, may hold values from -6 to 6
- cold_table: bfloat16 [262144, 512], P(('seq', 'own')), may hold values from -6 to 6
- cold_ids: int32 [16384, 4], P(('seq', 'own')), may hold values from 0 to 2047
- cold_counts: int32 [16384], P(('seq', 'own')), may hold values from 2 to 4
- event_slots: int32 [32, 2048], P('own', 'seq'), may hold values from 0 to 1023, as said below
- lengths: int32 [32], P('own'), may hold values from 512 to 2048, as said below
Outputs:
- grad_w_in: float32 [512, 2048], replicated
- grad_w_out: float32 [512, 512], replicated
- hot_grad: float32 [512, 512], replicated
- cold_grad: float32 [262144, 512], P(('seq', 'own'))
The draws below stay inside these ranges and needn't reach their ends.
Inputs may be any that keep to these rules, and one draw needn't show every extreme that they name: `cold_ids`: row ids inside one owner's shard. `event_slots`: a position at or above 512 names a valid slot of the request rows of the device that holds it. `lengths`: some user has all 2048 events in every draw.
All inputs are finite; a program needn't handle non-finite values.
Results may differ from the reference program's by a relative error of at most 0.0065.
Values may be sent and summed in bfloat16 or wider, within the bound.
A program may use at most 192 MiB of HBM per device.

```python
import jax
import jax.numpy as jnp
from jax import lax

HEADS = 4
HEAD_DIM = 128
D = 512
USERS_DEV = 2
SEQ_DEV = 256
HOT = 512
ROWS_DEV = 2048
SLOTS = 4
USERS = 32
LENGTH = 2048
ROWS = 262144
N_SEQ = 8
N_OWN = 16
DEVICES = 128


def shared_counts(key):
    key = jax.random.fold_in(key, 5)
    counts = jax.random.randint(key, (DEVICES * DEVICES,), SLOTS // 2, SLOTS + 1)
    counts = counts.at[DEVICES * DEVICES - 1].set(SLOTS)
    counts = counts.at[0].set(SLOTS // 2)
    return counts.astype(jnp.int32)


def draw_cold_counts(key, part):
    counts = shared_counts(key)
    return counts


def draw_event_slots(key, part):
    counts = shared_counts(key)
    key = jax.random.fold_in(key, 7)
    key_hot, key_row, key_owner, key_slot = jax.random.split(key, 4)
    shape = (USERS, LENGTH)
    hot_flag = jax.random.randint(key_hot, shape, 0, 4) == 0
    hot_row = jax.random.randint(key_row, shape, 0, HOT)
    owner = jax.random.randint(key_owner, shape, 0, DEVICES)
    user_idx = jnp.arange(USERS, dtype=jnp.int32)[:, None]
    time_idx = jnp.arange(LENGTH, dtype=jnp.int32)[None, :]
    device = time_idx // SEQ_DEV * (DEVICES // (LENGTH // SEQ_DEV)) + user_idx // USERS_DEV
    limit = counts[device * DEVICES + owner]
    within = jax.random.randint(key_slot, shape, 0, limit)
    cold = HOT + owner * SLOTS + within
    slots = jnp.where(hot_flag, hot_row, cold)
    slots = slots.at[0, 0].set(0)
    slots = slots.at[USERS - 1, LENGTH - 1].set(HOT + DEVICES * SLOTS - 1)
    return slots.astype(jnp.int32)


def draw_lengths(key, part):
    key = jax.random.fold_in(key, 11)
    values = jax.random.randint(key, (USERS,), LENGTH // 4, LENGTH + 1)
    values = values.at[0].set(LENGTH)
    values = values.at[1].set(LENGTH // 4)
    return values.astype(jnp.int32)


def with_ends(drawn, own_key, low, largest):
    extent = drawn.shape
    spot = [jax.random.randint(jax.random.fold_in(own_key, axis), (), 0, extent[axis]) for axis in range(len(extent))]
    drawn = drawn.at[tuple(spot)].set(low)
    longest = extent.index(max(extent))
    spot[longest] = (spot[longest] + 1) % extent[longest]
    return drawn.at[tuple(spot)].set(largest)


def steps_of(own_key, shape, cuts, smallest, largest):
    def one(dim, parts):
        heights = jax.random.uniform(jax.random.fold_in(jax.random.fold_in(own_key, 6), dim), (parts,), jnp.float32, smallest / len(cuts), largest / len(cuts))
        return jnp.repeat(jnp.exp(heights), shape[dim] // parts).reshape((-1,) + (1,) * (len(shape) - dim - 1))

    level = one(*cuts[0])
    for cut in cuts[1:]:
        level = level * one(*cut)
    return level


def noise(stream_key, extent, scale, reach, cuts=(), kind=jnp.bfloat16):
    drawn = jax.random.normal(stream_key, extent, jnp.float32) * scale
    if len(cuts) > 0:
        drawn = steps_of(stream_key, extent, cuts, -0.22, 0.18) * drawn
    return jnp.clip(drawn, min=-reach, max=reach).astype(kind)


def setup_inputs(seed: int = 0) -> dict:
    splits = jax.random.split(jax.random.key(seed), 10)
    return {
        "d_out": noise(splits[0], (USERS, LENGTH, D), 1.0, 6.0, ((0, 16), (1, 8))),
        "weight_in": noise(splits[1], (D, 4 * D), D ** -0.5, 0.25),
        "weight_out": noise(splits[2], (D, D), D ** -0.5, 0.25),
        "hot_table": noise(splits[3], (HOT, D), 1.0, 6.0),
        "cold_table": noise(splits[4], (ROWS, D), 1.0, 6.0, ((0, 128),)),
        "cold_ids": with_ends(jax.random.randint(splits[5], (DEVICES * DEVICES, SLOTS), 0, ROWS_DEV), jax.random.fold_in(splits[5], 1), 0, ROWS_DEV - 1).astype(jnp.int32),
        "cold_counts": draw_cold_counts(jax.random.fold_in(splits[9], 71), 0),
        "event_slots": draw_event_slots(jax.random.fold_in(splits[9], 71), 0),
        "lengths": draw_lengths(jax.random.fold_in(splits[9], 71), 0),
    }


def silu_slope(values):
    sigma = jax.nn.sigmoid(values)
    return sigma * (1.0 + values * (1.0 - sigma))

def reference(d_out, weight_in, weight_out, hot_table, cold_table, cold_ids, cold_counts, event_slots, lengths):
    dev_count = N_SEQ * N_OWN
    width = HEADS * HEAD_DIM
    scale = HEAD_DIM ** (-0.5)
    full_len = SEQ_DEV * N_SEQ
    requests = cold_ids.reshape(dev_count, dev_count, SLOTS)
    owners = jnp.arange(dev_count, dtype=jnp.int32)
    global_rows = requests + (owners * ROWS_DEV)[None, :, None]
    valid = jnp.arange(SLOTS, dtype=jnp.int32)[None, None, :] < cold_counts.reshape(dev_count, dev_count)[:, :, None]
    user_idx = jnp.arange(USERS_DEV * N_OWN, dtype=jnp.int32)[:, None]
    time_idx = jnp.arange(full_len, dtype=jnp.int32)[None, :]
    device = time_idx // SEQ_DEV * N_OWN + user_idx // USERS_DEV
    is_hot = event_slots < HOT
    hot_index = jnp.clip(event_slots, 0, HOT - 1)
    cold_slot = jnp.clip(event_slots - HOT, 0, dev_count * SLOTS - 1)
    owner = cold_slot // SLOTS
    within = cold_slot % SLOTS
    row_ids = global_rows[device, owner, within]
    live_slot = valid[device, owner, within] & jnp.logical_not(is_hot)
    cold_rows = jnp.where(live_slot[..., None], cold_table[row_ids], jnp.zeros((), cold_table.dtype))
    embedded = jnp.where(is_hot[..., None], hot_table[hot_index], cold_rows)
    live_rows = time_idx < lengths[:, None]
    cotangent = jnp.where(live_rows[..., None], d_out, jnp.zeros((), d_out.dtype))
    positions = jnp.arange(full_len, dtype=jnp.int32)

    def per_user(carry, inputs):
        tokens, grad_in, length = inputs
        inv_len = 1.0 / length.astype(jnp.float32)
        mask = ((positions[None, :] <= positions[:, None]) & (positions[None, :] < length)).astype(jnp.float32)[None]
        hidden_pre = jnp.dot(tokens, weight_in, preferred_element_type=jnp.float32)
        projected = jax.nn.silu(hidden_pre).astype(jnp.bfloat16)
        gate_part = projected[:, :width].astype(jnp.float32)
        query_heads = projected[:, width:2 * width].astype(jnp.float32).reshape(full_len, HEADS, HEAD_DIM)
        key_heads = projected[:, 2 * width:3 * width].astype(jnp.float32).reshape(full_len, HEADS, HEAD_DIM)
        value_heads = projected[:, 3 * width:].astype(jnp.float32).reshape(full_len, HEADS, HEAD_DIM)
        scores = jnp.einsum('thd,shd->hts', query_heads, key_heads) * scale
        weights = (jax.nn.silu(scores) * mask * inv_len).astype(jnp.bfloat16)
        attended = jnp.einsum('hts,shd->thd', weights.astype(jnp.float32), value_heads).reshape(full_len, width)
        centered = attended - lax.optimization_barrier(jnp.mean(attended, axis=-1, keepdims=True))
        rstd = lax.rsqrt(lax.optimization_barrier(jnp.mean(centered * centered, axis=-1, keepdims=True)) + 1e-05)
        normed = centered * rstd
        gated = (normed * gate_part).astype(jnp.bfloat16)
        grad_w_out = jnp.dot(gated.T, grad_in, preferred_element_type=jnp.float32)
        grad_gated = jnp.dot(grad_in, weight_out.T, preferred_element_type=jnp.float32)
        grad_gate = grad_gated * normed
        grad_normed = grad_gated * gate_part
        grad_att = ((grad_normed - lax.optimization_barrier(jnp.mean(grad_normed, axis=-1, keepdims=True)) - normed * lax.optimization_barrier(jnp.mean(grad_normed * normed, axis=-1, keepdims=True))) * rstd).astype(jnp.bfloat16)
        grad_heads = grad_att.astype(jnp.float32).reshape(full_len, HEADS, HEAD_DIM)
        grad_weights = jnp.einsum('thd,shd->hts', grad_heads, value_heads)
        grad_scores = (grad_weights * silu_slope(scores) * mask * inv_len).astype(jnp.bfloat16).astype(jnp.float32)
        grad_query = jnp.einsum('hts,shd->thd', grad_scores, key_heads) * scale
        grad_key = jnp.einsum('hts,thd->shd', grad_scores, query_heads) * scale
        grad_val = jnp.einsum('hts,thd->shd', weights.astype(jnp.float32), grad_heads)
        grad_proj = jnp.concatenate([grad_gate, grad_query.reshape(full_len, width), grad_key.reshape(full_len, width), grad_val.reshape(full_len, width)], axis=-1)
        grad_hidden = (grad_proj * silu_slope(hidden_pre)).astype(jnp.bfloat16)
        grad_w_in = jnp.dot(tokens.T, grad_hidden, preferred_element_type=jnp.float32)
        grad_embed = jnp.dot(grad_hidden, weight_in.T, preferred_element_type=jnp.float32) + grad_in.astype(jnp.float32)
        return ((carry[0] + grad_w_in, carry[1] + grad_w_out), grad_embed)
    start = (jnp.zeros((width, 4 * width), jnp.float32), jnp.zeros((width, width), jnp.float32))
    (grad_w_in, grad_w_out), grad_embed = lax.scan(per_user, start, (embedded, cotangent, lengths))
    flat = grad_embed.reshape(-1, width)
    hot_grad = jax.ops.segment_sum(jnp.where(is_hot.reshape(-1, 1), flat, jnp.zeros((), flat.dtype)), hot_index.reshape(-1), num_segments=HOT)
    cold_grad = jax.ops.segment_sum(jnp.where(live_slot.reshape(-1, 1), flat, jnp.zeros((), flat.dtype)), row_ids.reshape(-1), num_segments=ROWS_DEV * dev_count)
    return (grad_w_in, grad_w_out, hot_grad, cold_grad)
```

```python
import functools

import jax
import jax.numpy as jnp
from jax import lax
from jax.experimental import pallas as pl
from jax.experimental.pallas import tpu as pltpu
from jax.sharding import PartitionSpec as P

F32 = jnp.float32
BF16 = jnp.bfloat16
MESH = pl.DeviceIdType.MESH
SCALE = 128 ** (-0.5)
AG_ORDERS = (("z", "x", "y"), ("x", "y", "z"), ("y", "z", "x"))
AG_WIDTHS = (256, 256, 128)


def mm(a, b):
    return jnp.dot(a, b, preferred_element_type=F32)


def mm_nt(a, b):
    return lax.dot_general(a, b, (((1,), (1,)), ((), ())), preferred_element_type=F32)


def iota(shape, dim):
    return lax.broadcasted_iota(jnp.int32, shape, dim)


class Exchange:
    def __init__(self, n, me, device, src, dst, send_sem, recv_sem):
        self.n, self.me, self.device, self.src, self.dst = n, me, device, src, dst
        self.send_sem, self.recv_sem = send_sem, recv_sem

    def _out(self, p):
        return pltpu.make_async_remote_copy(
            src_ref=self.src(p),
            dst_ref=self.dst(self.me),
            send_sem=self.send_sem.at[p],
            recv_sem=self.recv_sem.at[self.me],
            device_id=self.device(p),
            device_id_type=MESH,
        )

    def _in(self, p):
        return pltpu.make_async_remote_copy(
            src_ref=self.src(p),
            dst_ref=self.dst(p),
            send_sem=self.send_sem.at[p],
            recv_sem=self.recv_sem.at[p],
            device_id=self.device(p),
            device_id_type=MESH,
        )

    def peer(self, k):
        return lax.rem(self.me + k, self.n)

    def _each(self, f):
        if self.n <= 4:
            for k in range(1, self.n):
                f(self.peer(k))
        else:
            pl.loop(1, self.n)(lambda k: f(self.peer(k)))

    def start(self):
        self._each(lambda p: self._out(p).start())

    def wait_recv(self):
        self._each(lambda p: self._in(p).wait_recv())

    def wait_send(self):
        self._each(lambda p: self._out(p).wait_send())


def main_kernel(
    ids_ref, code_col, code_row, valid_row, valid_col, len_ref, inv_ref, dout_ref, wout_ref, hot_ref, table_ref,
    win_ref,
    agw0, agw1, agw2, agh, ret, asked,
    id_a, id_b, got, rows, perm, fetched, e_loc, e_all, c_all,
    wh, wht, wh_sem, slope_pre, u_t, q_t, k_t, v_t, q_n, k_n, v_n,
    w_st, sl_st, att, gg, gat, ga_t, ga_n, gq, gk, gv, g_t,
    stat1, stat2, sib_s, sib_r, y_s, y_r, grad, w_send, w_recv, wu_s, wu_r, h_send, h_recv, hu_s, hu_r,
    s_send, q_recv, p_send,
    sem16, sem8, sem4, sem_ag, sem_sib,
):
    s, o = lax.axis_index("seq"), lax.axis_index("own")
    y, c = s // 2, lax.rem(s, 2)
    u, h = s // 4, lax.rem(s, 4)
    x, z = o // 4, lax.rem(o, 4)
    sib = (2 * y + 1 - c, o)
    agws = (agw0, agw1, agw2)

    barrier = pltpu.get_barrier_semaphore()

    @pl.loop(1, 16)
    def _(k):
        pl.semaphore_signal(barrier, inc=1, device_id=(s, lax.rem(o + k, 16)), device_id_type=MESH)

    @pl.loop(1, 8)
    def _(k):
        pl.semaphore_signal(barrier, inc=1, device_id=(lax.rem(s + k, 8), o), device_id_type=MESH)

    def load_w(b):
        return pltpu.make_async_copy(
            win_ref.at[:, pl.ds(pl.multiple_of(b * 512 + h * 128, 128), 128)],
            wh.at[:, pl.ds(b * 128, 128)],
            wh_sem.at[b],
        )

    for b in range(4):
        load_w(b).start()

    def own_x(i, src, dst):
        return Exchange(16, o, lambda p: (s, p), src, dst, sem16.at[i, 0], sem16.at[i, 1])

    def seq_x(i, src, dst):
        return Exchange(8, s, lambda p: (p, o), src, dst, sem8.at[i, 0], sem8.at[i, 1])

    def y_x(i, src, dst):
        return Exchange(4, y, lambda p: (2 * p + c, o), src, dst, sem4.at[i, 0], sem4.at[i, 1])

    def head_x(i, src, dst):
        return Exchange(4, h, lambda p: (4 * u + p, o), src, dst, sem4.at[i, 0], sem4.at[i, 1])

    def to_sib(src, dst, ssem, rsem):
        return pltpu.make_async_remote_copy(
            src_ref=src, dst_ref=dst, send_sem=ssem, recv_sem=rsem, device_id=sib, device_id_type=MESH
        )

    ids_x1 = own_x(0, lambda p: ids_ref.at[p], lambda p: id_a.at[p])
    ids_x2 = seq_x(0, lambda p: id_a.at[:, p], lambda p: id_b.at[p])
    rows_x1 = seq_x(1, lambda p: got.at[:, p], lambda p: rows.at[p])
    rows_x2 = own_x(1, lambda p: perm.at[p], lambda p: fetched.at[p])
    cot_x = y_x(0, lambda p: dout_ref.at[p // 2], lambda p: c_all.at[2 * p + c])
    emb_x = y_x(1, lambda p: e_loc.at[p // 2], lambda p: e_all.at[2 * p + c])
    stat1_x = head_x(2, lambda p: stat1.at[h], lambda p: stat1.at[p])
    stat2_x = head_x(3, lambda p: stat2.at[h], lambda p: stat2.at[p])
    grad_x = y_x(4, lambda p: y_s.at[p], lambda p: y_r.at[p])
    w_x = own_x(2, lambda p: w_send.at[p], lambda p: w_recv.at[p])
    hot_x1 = own_x(3, lambda p: h_send.at[p], lambda p: h_recv.at[p])
    hot_x2 = seq_x(2, lambda p: hu_s.at[p], lambda p: hu_r.at[p])
    ret_x1 = own_x(4, lambda p: s_send.at[p], lambda p: q_recv.at[p])
    ret_x2 = seq_x(3, lambda p: p_send.at[p], lambda p: ret.at[:, p])

    def sib_block(buf, i, yy):
        blk = buf.at[2 * yy + c]
        return to_sib(blk, blk, sem_sib.at[i, 0, yy], sem_sib.at[i, 1, yy])

    def sib_block_in(buf, i, yy):
        blk = buf.at[2 * yy + 1 - c]
        return to_sib(blk, blk, sem_sib.at[i, 0, yy], sem_sib.at[i, 1, yy])

    pl.semaphore_wait(barrier, 22)

    ids_x1.start()
    id_a[o] = ids_ref[o]
    cot_x.start()
    c_all[s] = dout_ref[u]
    sib_block(c_all, 0, y).start()
    for b in range(4):
        load_w(b).wait()
    wht[...] = wh[...].T
    ids_x1.wait_recv()
    ids_x2.start()
    id_b[s] = id_a[:, s, :]
    ids_x2.wait_recv()

    asked_ids = id_b[...].reshape(128, 128)
    for i in range(4):
        onehot = (iota((128, 2048), 1) == asked_ids[:, i : i + 1]).astype(F32).astype(BF16)
        got[i] = mm(onehot, table_ref[...]).astype(BF16).reshape(8, 16, 512)
    rows_x1.start()
    rows[s] = got[:, s]
    asked[...] = asked_ids.T[0:8, :]
    for d in (1, 3, 2):
        yy = lax.rem(y + d, 4)
        cot_x._in(yy).wait_recv()
        sib_block(c_all, 0, yy).start()
    rows_x1.wait_recv()
    r = iota((512, 512), 0)
    pick = (iota((512, 512), 1) == lax.rem(r, 32) * 16 + r // 32).astype(F32).astype(BF16)
    perm[...] = mm(pick, rows[...].reshape(512, 512)).astype(BF16).reshape(16, 32, 512)
    rows_x2.start()
    fetched[o] = perm[o]
    emb = []
    for b in range(4):
        hit = (code_col[...] == iota((512, 128), 1) + b * 128).astype(F32).astype(BF16)
        part = mm(hit, hot_ref[b * 128 : (b + 1) * 128, :])
        emb = part if b == 0 else emb + part
    rows_x2.wait_recv()
    for b in range(4):
        ok = jnp.logical_and(
            code_col[...] == iota((512, 128), 1) + (512 + b * 128), valid_row[:, b * 128 : (b + 1) * 128] > 0
        )
        emb += mm(ok.astype(F32).astype(BF16), fetched[4 * b : 4 * b + 4].reshape(128, 512))
    e_loc[...] = emb.astype(BF16).reshape(2, 256, 512)
    emb_x.start()
    e_all[s] = e_loc[u]
    sib_block(e_all, 1, y).start()

    def project(blk):
        cols = pl.ds(pl.multiple_of(blk * 256, 256), 256)
        pre = mm_nt(wht[...], e_all[blk])
        sig = 0.5 + 0.5 * jnp.tanh(0.5 * pre)
        act = pre * sig
        slope_pre[:, cols] = sig + act * (1.0 - sig)
        act = act.astype(BF16)
        u_t[:, cols] = act[0:128]
        q_t[:, cols] = act[128:256]
        k_t[:, cols] = act[256:384]
        keep = (blk * 256 + iota((1, 256), 1) < len_ref[u]).astype(F32)
        val = (act[384:512].astype(F32) * keep).astype(BF16)
        v_t[:, cols] = val
        q_n[cols, :] = act[128:256].T
        k_n[cols, :] = act[256:384].T
        v_n[cols, :] = val.T

    project(s)
    for d in (1, 3, 2):
        yy = lax.rem(y + d, 4)
        emb_x._in(yy).wait_recv()
        sib_block(e_all, 1, yy).start()
        project(2 * yy + c)
    for d in (0, 1, 3, 2):
        yy = lax.rem(y + d, 4)
        sib_block_in(e_all, 1, yy).wait_recv()
        project(2 * yy + 1 - c)

    att[...] = jnp.zeros_like(att)

    def forward(i, j, diag):
        keys = pl.multiple_of(j * 512, 512)
        qs = pl.ds(pl.multiple_of(i * 512, 512), 512)
        at = i * (i + 1) // 2 + j
        for m in range(4):
            half = mm(k_n[pl.ds(keys + m * 128, 128), :], q_t[:, qs]) * (0.5 * SCALE)
            t = jnp.tanh(half)
            a = 1.0 + t
            w = half * a
            slope = a * ((1.0 + 2.0 * half) - w)
            if diag:
                ok = iota((128, 512), 0) + m * 128 <= iota((128, 512), 1)
                w = jnp.where(ok, w, 0.0)
                slope = jnp.where(ok, slope, 0.0)
            w_st[at, m * 128 : (m + 1) * 128, :] = w.astype(BF16)
            sl_st[at, m * 128 : (m + 1) * 128, :] = slope.astype(BF16)
        att[:, qs] += mm(v_t[:, pl.ds(keys, 512)], w_st[at])

    @pl.loop(0, 4)
    def _(i):
        @pl.loop(0, i)
        def _(j):
            forward(i, j, False)

        forward(i, i, True)

    inv = inv_ref[u]
    mine = att[...] * inv
    m1 = jnp.sum(mine, axis=0, keepdims=True) * (1.0 / 128)
    dev = mine - m1
    stat1[h, 0:1, :] = m1
    stat1[h, 1:2, :] = jnp.sum(dev * dev, axis=0, keepdims=True)
    stat1_x.start()
    for d in range(4):
        sib_block_in(c_all, 0, lax.rem(y + d, 4)).wait_recv()
    live = (iota((1, 2048), 1) < len_ref[u]).astype(F32)
    wo = wout_ref[pl.ds(pl.multiple_of(h * 128, 128), 128), :]
    gg[...] = mm_nt(wo, c_all[...].reshape(2048, 512)) * live
    stat1_x.wait_recv()
    all1 = stat1[...]
    mean = jnp.sum(all1[:, 0, :], axis=0, keepdims=True) * 0.25
    off = all1[:, 0, :] - mean
    var = (jnp.sum(all1[:, 1, :], axis=0, keepdims=True) + 128.0 * jnp.sum(off * off, axis=0, keepdims=True)) * (
        1.0 / 512
    )
    rstd = lax.rsqrt(var + 1e-05)
    normed = (att[...] * inv - mean) * rstd
    att[...] = normed
    gate = u_t[...].astype(F32)
    gn = gg[...] * gate
    stat2[h, 0:1, :] = jnp.sum(gn, axis=0, keepdims=True)
    stat2[h, 1:2, :] = jnp.sum(gn * normed, axis=0, keepdims=True)
    stat2_x.start()
    gat[...] = (normed * gate * live).astype(BF16)
    gw_out = mm(gat[...], c_all[...].reshape(2048, 512))
    for b in range(4):
        w_send[4 * b : 4 * b + 4, :, 512:640] = gw_out[:, b * 128 : (b + 1) * 128].astype(BF16).reshape(4, 32, 128)
    g_t[0:128, :] = (gg[...] * att[...] * slope_pre[0:128, :]).astype(BF16)
    stat2_x.wait_recv()
    all2 = stat2[...]
    mean1 = jnp.sum(all2[:, 0, :], axis=0, keepdims=True) * (1.0 / 512)
    mean2 = jnp.sum(all2[:, 1, :], axis=0, keepdims=True) * (1.0 / 512)
    ga = (gg[...] * u_t[...].astype(F32) - mean1 - att[...] * mean2) * (rstd * inv)
    ga_t[...] = ga.astype(BF16)
    for b in range(8):
        ga_n[b * 256 : (b + 1) * 256, :] = ga_t[:, b * 256 : (b + 1) * 256].T

    gq[...] = jnp.zeros_like(gq)
    gk[...] = jnp.zeros_like(gk)
    gv[...] = jnp.zeros_like(gv)

    def backward(i, j):
        keys = pl.multiple_of(j * 512, 512)
        qs = pl.ds(pl.multiple_of(i * 512, 512), 512)
        at = i * (i + 1) // 2 + j
        for m in range(4):
            gw = mm(v_n[pl.ds(keys + m * 128, 128), :], ga_t[:, qs])
            ds = gw * sl_st[at, m * 128 : (m + 1) * 128, :].astype(F32)
            sl_st[at, m * 128 : (m + 1) * 128, :] = ds.astype(BF16)
        gk[pl.ds(keys, 512), :] += mm(sl_st[at], q_n[qs, :])
        gv[pl.ds(keys, 512), :] += mm(w_st[at], ga_n[qs, :])
        gq[:, qs] += mm(k_t[:, pl.ds(keys, 512)], sl_st[at])

    @pl.loop(0, 4)
    def _(i):
        @pl.loop(0, i + 1)
        def _(j):
            backward(i, j)

    keep = (iota((1, 2048), 1) < len_ref[u]).astype(F32)
    g_t[128:256, :] = (gq[...] * (0.5 * SCALE) * slope_pre[128:256, :]).astype(BF16)
    for b in range(8):
        cols = slice(b * 256, (b + 1) * 256)
        g_t[256:384, cols] = (gk[cols, :].T * (0.5 * SCALE) * slope_pre[256:384, cols]).astype(BF16)
        g_t[384:512, cols] = (gv[cols, :].T * keep[:, cols] * slope_pre[384:512, cols]).astype(BF16)

    def partial(blk):
        return mm(wh[...], g_t[:, pl.ds(pl.multiple_of(blk * 256, 256), 256)])

    def sib_grad(yy):
        return to_sib(sib_s.at[yy], sib_r.at[yy], sem_sib.at[2, 0, yy], sem_sib.at[2, 1, yy])

    for d in (2, 1, 3, 0):
        yy = lax.rem(y + d, 4)
        sib_s[yy] = partial(2 * yy + 1 - c).astype(BF16)
        sib_grad(yy).start()
    for d in (2, 1, 3, 0):
        yy = lax.rem(y + d, 4)
        total = partial(2 * yy + c)
        sib_grad(yy).wait_recv()
        total = (total + sib_r[yy].astype(F32)).astype(BF16)
        if d == 0:
            y_r[yy] = total
        else:
            y_s[yy] = total
            grad_x._out(yy).start()

    gw_in = mm(g_t[...], e_all[...].reshape(2048, 512))
    w_send[:, :, 0:512] = gw_in.T.astype(BF16).reshape(16, 32, 512)
    w_x.start()
    w_recv[o] = w_send[o]

    grad_x.wait_recv()
    for uu in range(2):
        grad[:, uu * 256 : (uu + 1) * 256] = (y_r[2 * uu].astype(F32) + y_r[2 * uu + 1].astype(F32)).astype(BF16)
    cots = []
    for uu in range(2):
        here = (s * 256 + iota((256, 1), 0) < len_ref[uu]).astype(F32)
        cots.append((dout_ref[uu].astype(F32) * here).astype(BF16))
    cot = jnp.concatenate(cots, axis=0)
    for b in (1, 0):
        blocks = []
        for l in range(4):
            hit = iota((512, 128), 0) + b * 512 == code_row[:, l * 128 : (l + 1) * 128]
            if b == 1:
                hit = jnp.logical_and(hit, valid_col[...] > 0)
            blocks.append(hit.astype(F32).astype(BF16))
        onehot = jnp.concatenate(blocks, axis=1)
        sums = (mm_nt(onehot, grad[...]) + mm(onehot, cot)).astype(BF16).reshape(16, 32, 512)
        if b == 1:
            s_send[...] = sums
            ret_x1.start()
            q_recv[o] = s_send[o]
        else:
            h_send[...] = sums
            hot_x1.start()
            h_recv[o] = h_send[o]

    w_x.wait_recv()
    total = jnp.sum(w_recv[...].astype(F32), axis=0)
    wu_s[...] = total.astype(BF16).reshape(2, 16, 640)
    partner = (lax.rem(s + 4, 8), o)
    wu = pltpu.make_async_remote_copy(
        src_ref=wu_s.at[1 - u],
        dst_ref=wu_r,
        send_sem=sem_sib.at[3, 0, 0],
        recv_sem=sem_sib.at[3, 1, 0],
        device_id=partner,
        device_id_type=MESH,
    )
    wu.start()

    place = {"y": y, "x": x, "z": z}
    device = {
        "y": lambda p: (2 * p + c, o),
        "x": lambda p: (s, 4 * p + z),
        "z": lambda p: (s, 4 * x + p),
    }

    def gather_x(buf, i, order, stage):
        axis = order[stage]

        def block(p):
            at = dict(place)
            at[axis] = p
            for done in order[:stage]:
                at[done] = slice(None)
            return buf.at[c, at["y"], at["x"], at["z"]]

        return Exchange(
            4, place[axis], device[axis], lambda p: block(place[axis]), block,
            sem_ag.at[i, stage, 0], sem_ag.at[i, stage, 1],
        )

    def sib_gather(buf, i, core):
        return to_sib(buf.at[core], buf.at[core], sem_sib.at[4, 0, i], sem_sib.at[4, 1, i])

    w_gathers = [[gather_x(agws[i], i, AG_ORDERS[i], stage) for stage in range(3)] for i in range(3)]
    h_gather = [gather_x(agh, 3, AG_ORDERS[0], stage) for stage in range(3)]

    ret_x1.wait_recv()
    r = iota((512, 512), 0)
    pick = (iota((512, 512), 1) == lax.rem(r, 16) * 32 + r // 16).astype(F32).astype(BF16)
    p_send[...] = mm(pick, q_recv[...].reshape(512, 512)).astype(BF16).reshape(8, 4, 16, 512)
    ret_x2.start()
    ret[:, s] = p_send[s]

    wu.wait_recv()
    mine = (total[0:16] * (1.0 - u.astype(F32)) + total[16:32] * u.astype(F32)) + wu_r[...].astype(F32)
    mine = mine.astype(BF16)
    agw0[c, y, x, z] = mine[:, 0:256]
    agw1[c, y, x, z] = mine[:, 256:512]
    agw2[c, y, x, z] = mine[:, 512:640]
    for i in range(3):
        w_gathers[i][0].start()

    hot_x1.wait_recv()
    total = jnp.sum(h_recv[...].astype(F32), axis=0).astype(BF16)
    for i in range(8):
        hu_s[i] = total[16 * (i // 4) : 16 * (i // 4) + 16, 128 * (i % 4) : 128 * (i % 4) + 128]
    hot_x2.start()
    hu_r[s] = hu_s[s]

    for i in range(3):
        w_gathers[i][0].wait_recv()
        w_gathers[i][1].start()
    hot_x2.wait_recv()
    agh[c, y, x, z] = jnp.sum(hu_r[...].astype(F32), axis=0).astype(BF16)
    h_gather[0].start()
    for i in range(3):
        w_gathers[i][1].wait_recv()
        w_gathers[i][2].start()
    h_gather[0].wait_recv()
    h_gather[1].start()
    h_gather[1].wait_recv()
    h_gather[2].start()
    for i in range(3):
        w_gathers[i][2].wait_recv()
        sib_gather(agws[i], i, c).start()
    h_gather[2].wait_recv()
    sib_gather(agh, 3, c).start()
    ret_x2.wait_recv()
    for i in range(4):
        sib_gather((*agws, agh)[i], i, 1 - c).wait_recv()

    for step in (ids_x1, ids_x2, rows_x1, rows_x2, cot_x, emb_x, stat1_x, stat2_x, grad_x, w_x):
        step.wait_send()
    for step in (hot_x1, hot_x2, ret_x1, ret_x2, *h_gather, *w_gathers[0], *w_gathers[1], *w_gathers[2]):
        step.wait_send()
    for yy in range(4):
        sib_block(c_all, 0, yy).wait_send()
        sib_block(e_all, 1, yy).wait_send()
        sib_grad(yy).wait_send()
    wu.wait_send()
    for i in range(4):
        sib_gather((*agws, agh)[i], i, c).wait_send()


def finish_kernel(a0, a1, a2, ah, ret, asked, gin, gout, ghot, gcold):
    g = pl.program_id(0)
    for yy in range(4):
        for core in range(2):
            user, head = yy // 2, (yy % 2) * 2 + core
            seq = 2 * yy + core
            for zz in range(2):
                top = 32 * zz + 16 * user
                b0 = a0[core, yy, 0, zz].astype(F32)
                b1 = a1[core, yy, 0, zz].astype(F32)
                for b in range(4):
                    part = (b0, b1)[b // 2][:, (b % 2) * 128 : (b % 2) * 128 + 128]
                    gin[top : top + 16, b * 512 + head * 128 : b * 512 + head * 128 + 128] = part
                low = pl.multiple_of(head * 128 + 32 * (2 * lax.rem(g, 2) + zz) + 16 * user, 16)
                gout[pl.ds(low, 16), pl.ds(pl.multiple_of(g // 2 * 128, 128), 128)] = a2[core, yy, 0, zz].astype(F32)
                hot_top = 32 * zz + 16 * (seq // 4)
                ghot[hot_top : hot_top + 16, 128 * (seq % 4) : 128 * (seq % 4) + 128] = ah[core, yy, 0, zz].astype(F32)
    hits = [
        (iota((256, 128), 0) + g * 256 == asked[i : i + 1, :]).astype(F32).astype(BF16) for i in range(4)
    ]
    gcold[...] = mm(jnp.concatenate(hits, axis=1), ret[...].reshape(512, 512))


def on_device(
    d_out, weight_in, weight_out, hot_table, cold_table, cold_ids, cold_counts, event_slots, lengths
):
    ids = jnp.pad(cold_ids.reshape(8, 16, 4).transpose(1, 0, 2), ((0, 0), (0, 0), (0, 124)))
    slot = event_slots.reshape(512)
    cold = slot - 512
    owner, part = cold // 4, cold % 4
    code = jnp.where(slot < 512, slot, 512 + owner % 16 * 32 + owner // 16 * 4 + part)
    code_col = jnp.broadcast_to(code[:, None], (512, 128))
    code_row = code.reshape(1, 512)
    valid = jnp.arange(4, dtype=jnp.int32)[None, None, :] < cold_counts.reshape(8, 16).T[:, :, None]
    valid = valid.astype(jnp.int32).reshape(512)
    valid_row = valid.reshape(1, 512)
    valid_col = jnp.broadcast_to(valid[:, None], (512, 128))
    inv = 1.0 / lengths.astype(F32)

    vmem = pl.BlockSpec(memory_space=pltpu.VMEM)
    smem = pl.BlockSpec(memory_space=pltpu.SMEM)
    big = lambda *shape: pltpu.VMEM(shape, BF16)
    wide = lambda *shape: pltpu.VMEM(shape, F32)
    sems = pltpu.SemaphoreType.DMA
    outs = [jax.ShapeDtypeStruct((2, 4, 4, 4, 16, w), BF16) for w in (*AG_WIDTHS, 128)] + [
        jax.ShapeDtypeStruct((4, 8, 16, 512), BF16),
        jax.ShapeDtypeStruct((8, 128), jnp.int32),
    ]
    scratch = [
        pltpu.VMEM((16, 8, 128), jnp.int32),
        pltpu.VMEM((8, 16, 128), jnp.int32),
        big(4, 8, 16, 512),
        big(8, 4, 16, 512),
        big(16, 32, 512),
        big(16, 32, 512),
        big(2, 256, 512),
        big(8, 256, 512),
        big(8, 256, 512),
        big(512, 512),
        big(512, 512),
        sems((4,)),
        wide(512, 2048),
        big(128, 2048),
        big(128, 2048),
        big(128, 2048),
        big(128, 2048),
        big(2048, 128),
        big(2048, 128),
        big(2048, 128),
        big(10, 512, 512),
        big(10, 512, 512),
        wide(128, 2048),
        wide(128, 2048),
        big(128, 2048),
        big(128, 2048),
        big(2048, 128),
        wide(128, 2048),
        wide(2048, 128),
        wide(2048, 128),
        big(512, 2048),
        wide(4, 2, 2048),
        wide(4, 2, 2048),
        big(4, 512, 256),
        big(4, 512, 256),
        big(4, 512, 256),
        big(4, 512, 256),
        big(512, 512),
        big(16, 32, 640),
        big(16, 32, 640),
        big(2, 16, 640),
        big(16, 640),
        big(16, 32, 512),
        big(16, 32, 512),
        big(8, 16, 128),
        big(8, 16, 128),
        big(16, 32, 512),
        big(16, 32, 512),
        big(8, 4, 16, 512),
        sems((5, 2, 16)),
        sems((4, 2, 8)),
        sems((5, 2, 4)),
        sems((4, 3, 2, 4)),
        sems((5, 2, 4)),
    ]
    a0, a1, a2, ah, ret, asked = pl.pallas_call(
        main_kernel,
        out_shape=outs,
        in_specs=[vmem] * 5 + [smem] * 2 + [vmem] * 4 + [pl.BlockSpec(memory_space=pl.ANY)],
        out_specs=[vmem] * 6,
        scratch_shapes=scratch,
        compiler_params=pltpu.CompilerParams(
            collective_id=0, has_side_effects=True, vmem_limit_bytes=60 * 1024 * 1024
        ),
        name="layer",
    )(
        ids, code_col, code_row, valid_row, valid_col, lengths, inv,
        d_out, weight_out, hot_table, cold_table, weight_in,
    )

    def ag_spec(w):
        return pl.BlockSpec((2, 4, 1, 2, 16, w), lambda g: (0, 0, g // 2, lax.rem(g, 2), 0, 0))

    return pl.pallas_call(
        finish_kernel,
        grid=(8,),
        out_shape=[
            jax.ShapeDtypeStruct((512, 2048), F32),
            jax.ShapeDtypeStruct((512, 512), F32),
            jax.ShapeDtypeStruct((512, 512), F32),
            jax.ShapeDtypeStruct((2048, 512), F32),
        ],
        in_specs=[ag_spec(w) for w in (*AG_WIDTHS, 128)]
        + [
            pl.BlockSpec((4, 8, 16, 512), lambda g: (0, 0, 0, 0)),
            pl.BlockSpec((8, 128), lambda g: (0, 0)),
        ],
        out_specs=[
            pl.BlockSpec((64, 2048), lambda g: (g, 0)),
            pl.BlockSpec((512, 512), lambda g: (0, 0)),
            pl.BlockSpec((64, 512), lambda g: (g, 0)),
            pl.BlockSpec((256, 512), lambda g: (g, 0)),
        ],
        compiler_params=pltpu.CompilerParams(vmem_limit_bytes=32 * 1024 * 1024),
        name="finish",
    )(a0, a1, a2, ah, ret, asked)


def solution(mesh):
    placed = (
        P("own", "seq", None),
        P(),
        P(),
        P(),
        P(("seq", "own"), None),
        P(("seq", "own"), None),
        P(("seq", "own")),
        P("own", "seq"),
        P("own"),
    )
    return jax.shard_map(
        on_device,
        mesh=mesh,
        in_specs=placed,
        out_specs=(P(), P(), P(), P(("seq", "own"), None)),
        check_vma=False,
    )
```

```python
import functools

import jax
import jax.numpy as jnp
from jax import lax
from jax.experimental import pallas as pl
from jax.experimental.pallas import tpu as pltpu
from jax.sharding import PartitionSpec as P

F32 = jnp.float32
BF16 = jnp.bfloat16
MESH = pl.DeviceIdType.MESH
SCALE = 128 ** (-0.5)
AG_ORDERS = (("z", "x", "y"), ("x", "y", "z"), ("y", "z", "x"))
CHUNKS = 2
CW = 512 // CHUNKS


def mm(a, b):
    return jnp.dot(a, b, preferred_element_type=F32)


def mm_nt(a, b):
    return lax.dot_general(a, b, (((1,), (1,)), ((), ())), preferred_element_type=F32)


def iota(shape, dim):
    return lax.broadcasted_iota(jnp.int32, shape, dim)


def onehot(hit):
    return hit.astype(F32).astype(BF16)


class Exchange:
    def __init__(self, n, me, device, src, dst, send_sem, recv_sem):
        self.n, self.me, self.device, self.src, self.dst = n, me, device, src, dst
        self.send_sem, self.recv_sem = send_sem, recv_sem

    def _out(self, p):
        return pltpu.make_async_remote_copy(
            src_ref=self.src(p),
            dst_ref=self.dst(self.me),
            send_sem=self.send_sem.at[p],
            recv_sem=self.recv_sem.at[self.me],
            device_id=self.device(p),
            device_id_type=MESH,
        )

    def _in(self, p):
        return pltpu.make_async_remote_copy(
            src_ref=self.src(p),
            dst_ref=self.dst(p),
            send_sem=self.send_sem.at[p],
            recv_sem=self.recv_sem.at[p],
            device_id=self.device(p),
            device_id_type=MESH,
        )

    def peer(self, k):
        return lax.rem(self.me + k, self.n)

    def _each(self, f):
        if self.n <= 4:
            for k in range(1, self.n):
                f(self.peer(k))
        else:
            pl.loop(1, self.n)(lambda k: f(self.peer(k)))

    def start(self, pending):
        pending.append(self.wait_send)
        self._each(lambda p: self._out(p).start())

    def start_to(self, p, pending):
        pending.append(lambda: self._out(p).wait_send())
        self._out(p).start()

    def wait_from(self, p):
        self._in(p).wait_recv()

    def wait_recv(self):
        self._each(lambda p: self._in(p).wait_recv())

    def wait_send(self):
        self._each(lambda p: self._out(p).wait_send())


def main_kernel(
    idst_ref, counts_ref, ev_ref, len_ref, dout_ref, wout_ref, hot_ref, table_ref, win_ref,
    ag0, ag1, ag2, ret, asked,
    id_pad, id_loc, id_a, id_b, ev_loc, ev_all, code_col, valid_col,
    got, rows, perm, fetched, e_loc, e_all, c_all,
    wh, wht, wh_sem, slope_pre, u_t, q_t, k_t, v_t, q_n, k_n, v_n,
    w_st, sl_st, att, gg, gat, ga_t, ga_n, gq, gk, gv, g_t, stat,
    sib_s, sib_r, own_p, y_s, y_r, grad, w_send, w_recv, wu_s, wu_r, hu_s, hu_r,
    s_send, q_recv, p_send,
    sem16, sem8, sem4, sem_ag, sem_sib,
):
    s, o = lax.axis_index("seq"), lax.axis_index("own")
    y, c = s // 2, lax.rem(s, 2)
    u, h = s // 4, lax.rem(s, 4)
    x, z = o // 4, lax.rem(o, 4)
    sib = (2 * y + 1 - c, o)
    ags = (ag0, ag1, ag2)
    chunks = range(CHUNKS)
    pending = []

    barrier = pltpu.get_barrier_semaphore()

    @pl.loop(1, 16)
    def _(k):
        pl.semaphore_signal(barrier, inc=1, device_id=(s, lax.rem(o + k, 16)), device_id_type=MESH)

    @pl.loop(1, 8)
    def _(k):
        pl.semaphore_signal(barrier, inc=1, device_id=(lax.rem(s + k, 8), o), device_id_type=MESH)

    def load_w(b):
        return pltpu.make_async_copy(
            win_ref.at[:, pl.ds(pl.multiple_of(b * 512 + h * 128, 128), 128)],
            wh.at[:, pl.ds(b * 128, 128)],
            wh_sem.at[b],
        )

    for b in range(4):
        load_w(b).start()

    def own_x(i, src, dst):
        return Exchange(16, o, lambda p: (s, p), src, dst, sem16.at[i, 0], sem16.at[i, 1])

    def seq_x(i, src, dst):
        return Exchange(8, s, lambda p: (p, o), src, dst, sem8.at[i, 0], sem8.at[i, 1])

    def y_x(i, src, dst):
        return Exchange(4, y, lambda p: (2 * p + c, o), src, dst, sem4.at[i, 0], sem4.at[i, 1])

    def head_x(i, src, dst):
        return Exchange(4, h, lambda p: (4 * u + p, o), src, dst, sem4.at[i, 0], sem4.at[i, 1])

    def to_sib(src, dst, i, j):
        return pltpu.make_async_remote_copy(
            src_ref=src, dst_ref=dst, send_sem=sem_sib.at[i, 0, j], recv_sem=sem_sib.at[i, 1, j],
            device_id=sib, device_id_type=MESH,
        )

    def start_sib(copy):
        pending.append(copy.wait_send)
        copy.start()

    ids_x1 = own_x(0, lambda p: id_loc.at[:, p], lambda p: id_a.at[p])
    ids_x2 = seq_x(0, lambda p: id_a.at[:, p], lambda p: id_b.at[p])
    ev_x = seq_x(1, lambda p: ev_loc.at[p // 4], lambda p: ev_all.at[p])
    hot_x = seq_x(2, lambda p: hu_s.at[p], lambda p: hu_r.at[p])
    rows_x1 = [seq_x(3 + k, lambda p, k=k: got.at[k, :, p], lambda p, k=k: rows.at[k, p]) for k in chunks]
    ret_x2 = [
        seq_x(3 + CHUNKS + k, lambda p, k=k: p_send.at[k, p], lambda p, k=k: ret.at[k, :, p]) for k in chunks
    ]
    w_x = own_x(1, lambda p: w_send.at[p], lambda p: w_recv.at[p])
    rows_x2 = [own_x(2 + k, lambda p, k=k: perm.at[k, p], lambda p, k=k: fetched.at[k, p]) for k in chunks]
    ret_x1 = [
        own_x(2 + CHUNKS + k, lambda p, k=k: s_send.at[k, p], lambda p, k=k: q_recv.at[k, p]) for k in chunks
    ]
    cot_x = y_x(0, lambda p: dout_ref.at[p // 2], lambda p: c_all.at[2 * p + c])
    stat_x = head_x(1, lambda p: stat.at[h], lambda p: stat.at[p])
    emb_x = [
        y_x(2 + k, lambda p, k=k: e_loc.at[k, p // 2], lambda p, k=k: e_all.at[k, 2 * p + c]) for k in chunks
    ]
    grad_x = [y_x(2 + CHUNKS + k, lambda p, k=k: y_s.at[k, p], lambda p, k=k: y_r.at[k, p]) for k in chunks]

    def sib_block(buf, i, yy):
        return to_sib(buf.at[2 * yy + c], buf.at[2 * yy + c], i, yy)

    def sib_block_in(buf, i, yy):
        return to_sib(buf.at[2 * yy + 1 - c], buf.at[2 * yy + 1 - c], i, yy)

    id_pad[...] = jnp.zeros_like(id_pad)
    id_pad[0:4, :] = idst_ref[...]
    id_loc[...] = id_pad[...].T.reshape(8, 16, 128)

    pl.semaphore_wait(barrier, 22)

    ids_x1.start(pending)
    id_a[o] = id_loc[:, o, :]
    for d in (1, 3):
        cot_x.start_to(lax.rem(y + d, 4), pending)
    c_all[s] = dout_ref[u]

    codes = []
    for uu in range(2):
        e = ev_ref[uu : uu + 1, :]
        cold = e - 512
        code = jnp.where(e < 512, e, 512 + ((cold >> 2) & 15) * 32 + (cold >> 6) * 4 + (cold & 3))
        ev_loc[uu] = jnp.broadcast_to(code, (8, 256))
        codes.append(code)
    code_row = jnp.concatenate(codes, axis=1)
    code_col[...] = jnp.broadcast_to(code_row, (128, 512)).T
    counts = counts_ref[...].astype(F32).astype(BF16)
    l = iota((128, 512), 1)
    pick = onehot(iota((128, 512), 0) == ((l >> 2) & 7) * 16 + (l >> 5))
    valid_row = (iota((8, 512), 1) & 3).astype(F32) < mm(jnp.broadcast_to(counts, (8, 128)), pick)
    valid_row = valid_row[0:1]
    l = iota((512, 128), 0)
    pick = onehot(iota((512, 128), 1) == ((l >> 2) & 7) * 16 + (l >> 5))
    valid_col[...] = (
        (l & 3).astype(F32) < mm_nt(pick, jnp.broadcast_to(counts, (128, 128)))
    ).astype(F32)
    for b in range(4):
        load_w(b).wait()
    wht[...] = wh[...].T

    ids_x1.wait_recv()
    ids_x2.start(pending)
    id_b[s] = id_a[:, s, :]
    ids_x2.wait_recv()

    asked_ids = id_b[...].reshape(128, 128)
    for i in range(4):
        hit = onehot(iota((128, 2048), 1) == asked_ids[:, i : i + 1])
        found = mm(hit, table_ref[...]).astype(BF16)
        for k in chunks:
            got[k, i] = found[:, k * CW : (k + 1) * CW].reshape(8, 16, CW)
    for k in chunks:
        rows_x1[k].start(pending)
        rows[k, s] = got[k, :, s]
    ev_x.start(pending)
    ev_all[s] = ev_loc[u]
    asked[...] = asked_ids.T[0:8, :]
    start_sib(sib_block(c_all, 0, y))
    hot_hits = [onehot(code_col[...] == iota((512, 128), 1) + b * 128) for b in range(4)]
    emb = mm(jnp.concatenate(hot_hits, axis=1), hot_ref[...])
    r = iota((512, 512), 0)
    pick = onehot(iota((512, 512), 1) == (r & 31) * 16 + (r >> 5))
    for k in chunks:
        rows_x1[k].wait_recv()
        perm[k] = mm(pick, rows[k].reshape(512, CW)).astype(BF16).reshape(16, 32, CW)
        rows_x2[k].start(pending)
        fetched[k, o] = perm[k, o]
    cot_x.start_to(lax.rem(y + 2, 4), pending)
    for d in (1, 3):
        cot_x.wait_from(lax.rem(y + d, 4))
        start_sib(sib_block(c_all, 0, lax.rem(y + d, 4)))
    cold_hits = [
        onehot(jnp.logical_and(
            code_col[...] == iota((512, 128), 1) + (512 + b * 128), valid_row[:, b * 128 : (b + 1) * 128]
        ))
        for b in range(4)
    ]
    cold_hits = jnp.concatenate(cold_hits, axis=1)
    for k in chunks:
        rows_x2[k].wait_recv()
        part = emb[:, k * CW : (k + 1) * CW] + mm(cold_hits, fetched[k].reshape(512, CW))
        e_loc[k] = part.astype(BF16).reshape(2, 256, CW)
        emb_x[k].start(pending)
        e_all[k, s] = e_loc[k, u]
        start_sib(sib_block(e_all.at[k], 2 + k, y))

    def project(blk):
        cols = pl.ds(pl.multiple_of(blk * 256, 256), 256)
        pre = mm_nt(wht[...], jnp.concatenate([e_all[k, blk] for k in chunks], axis=1))
        sig = 0.5 + 0.5 * jnp.tanh(0.5 * pre)
        act = pre * sig
        slope_pre[:, cols] = sig + act * (1.0 - sig)
        act = act.astype(BF16)
        u_t[:, cols] = act[0:128]
        q_t[:, cols] = act[128:256]
        k_t[:, cols] = act[256:384]
        keep = (blk * 256 + iota((1, 256), 1) < len_ref[u]).astype(F32)
        val = (act[384:512].astype(F32) * keep).astype(BF16)
        v_t[:, cols] = val
        q_n[cols, :] = act[128:256].T
        k_n[cols, :] = act[256:384].T
        v_n[cols, :] = val.T

    cot_x.wait_from(lax.rem(y + 2, 4))
    start_sib(sib_block(c_all, 0, lax.rem(y + 2, 4)))
    project(s)
    for k in chunks:
        for d in (1, 3, 2):
            yy = lax.rem(y + d, 4)
            emb_x[k].wait_from(yy)
            start_sib(sib_block(e_all.at[k], 2 + k, yy))
            if k == CHUNKS - 1:
                project(2 * yy + c)
    for d in (0, 1, 3, 2):
        yy = lax.rem(y + d, 4)
        for k in chunks:
            sib_block_in(e_all.at[k], 2 + k, yy).wait_recv()
        project(2 * yy + 1 - c)

    att[...] = jnp.zeros_like(att)

    def forward(i, j, diag):
        keys = pl.multiple_of(j * 512, 512)
        qs = pl.ds(pl.multiple_of(i * 512, 512), 512)
        at = i * (i + 1) // 2 + j
        for m in range(4):
            half = mm(k_n[pl.ds(keys + m * 128, 128), :], q_t[:, qs]) * (0.5 * SCALE)
            t = jnp.tanh(half)
            a = 1.0 + t
            w = half * a
            slope = a * ((1.0 + 2.0 * half) - w)
            if diag:
                ok = iota((128, 512), 0) + m * 128 <= iota((128, 512), 1)
                w = jnp.where(ok, w, 0.0)
                slope = jnp.where(ok, slope, 0.0)
            w_st[at, m * 128 : (m + 1) * 128, :] = w.astype(BF16)
            sl_st[at, m * 128 : (m + 1) * 128, :] = slope.astype(BF16)
        att[:, qs] += mm(v_t[:, pl.ds(keys, 512)], w_st[at])

    @pl.loop(0, 4)
    def _(i):
        @pl.loop(0, i)
        def _(j):
            forward(i, j, False)

        forward(i, i, True)

    for d in range(4):
        sib_block_in(c_all, 0, lax.rem(y + d, 4)).wait_recv()
    live = (iota((1, 2048), 1) < len_ref[u]).astype(F32)
    wo = wout_ref[pl.ds(pl.multiple_of(h * 128, 128), 128), :]
    gg[...] = mm_nt(wo, c_all[...].reshape(2048, 512)) * live
    inv = 1.0 / jnp.full((1, 2048), len_ref[u], jnp.int32).astype(F32)
    mine = att[...] * inv
    m1 = jnp.sum(mine, axis=0, keepdims=True) * (1.0 / 128)
    dev = mine - m1
    gn = gg[...] * u_t[...].astype(F32)
    stat[h, 0:1, :] = m1
    stat[h, 1:2, :] = jnp.sum(dev * dev, axis=0, keepdims=True)
    stat[h, 2:3, :] = jnp.sum(gn, axis=0, keepdims=True)
    stat[h, 3:4, :] = jnp.sum(gn * dev, axis=0, keepdims=True)
    stat_x.start(pending)
    stat_x.wait_recv()
    both = stat[...]
    mean = jnp.sum(both[:, 0, :], axis=0, keepdims=True) * 0.25
    off = both[:, 0, :] - mean
    var = (jnp.sum(both[:, 1, :], axis=0, keepdims=True) + 128.0 * jnp.sum(off * off, axis=0, keepdims=True)) * (
        1.0 / 512
    )
    rstd = lax.rsqrt(var + 1e-05)
    mean1 = jnp.sum(both[:, 2, :], axis=0, keepdims=True) * (1.0 / 512)
    mean2 = jnp.sum(both[:, 3, :] + off * both[:, 2, :], axis=0, keepdims=True) * (rstd * (1.0 / 512))
    normed = (att[...] * inv - mean) * rstd
    att[...] = normed
    gn = gg[...] * u_t[...].astype(F32)
    ga_t[...] = ((gn - mean1 - normed * mean2) * (rstd * inv)).astype(BF16)
    for b in range(8):
        ga_n[b * 256 : (b + 1) * 256, :] = ga_t[:, b * 256 : (b + 1) * 256].T

    gq[...] = jnp.zeros_like(gq)
    gk[...] = jnp.zeros_like(gk)
    gv[...] = jnp.zeros_like(gv)

    def backward(i, j):
        keys = pl.multiple_of(j * 512, 512)
        qs = pl.ds(pl.multiple_of(i * 512, 512), 512)
        at = i * (i + 1) // 2 + j
        for m in range(4):
            gw = mm(v_n[pl.ds(keys + m * 128, 128), :], ga_t[:, qs])
            ds = gw * sl_st[at, m * 128 : (m + 1) * 128, :].astype(F32)
            sl_st[at, m * 128 : (m + 1) * 128, :] = ds.astype(BF16)
        gk[pl.ds(keys, 512), :] += mm(sl_st[at], q_n[qs, :])
        gv[pl.ds(keys, 512), :] += mm(w_st[at], ga_n[qs, :])
        gq[:, qs] += mm(k_t[:, pl.ds(keys, 512)], sl_st[at])

    @pl.loop(0, 4)
    def _(i):
        @pl.loop(0, i + 1)
        def _(j):
            backward(i, j)

    keep = (iota((1, 2048), 1) < len_ref[u]).astype(F32)
    g_t[0:128, :] = (gg[...] * att[...] * slope_pre[0:128, :]).astype(BF16)
    g_t[128:256, :] = (gq[...] * (0.5 * SCALE) * slope_pre[128:256, :]).astype(BF16)
    for b in range(8):
        cols = slice(b * 256, (b + 1) * 256)
        g_t[256:384, cols] = (gk[cols, :].T * (0.5 * SCALE) * slope_pre[256:384, cols]).astype(BF16)
        g_t[384:512, cols] = (gv[cols, :].T * keep[:, cols] * slope_pre[384:512, cols]).astype(BF16)

    def partial(k, blk):
        return mm(wh[k * CW : (k + 1) * CW, :], g_t[:, pl.ds(pl.multiple_of(blk * 256, 256), 256)])

    def sib_grad(k, yy):
        return to_sib(sib_s.at[k, yy], sib_r.at[k, yy], 2 + CHUNKS + k, yy)

    for k in chunks:
        for d in (2, 1, 3, 0):
            yy = lax.rem(y + d, 4)
            sib_s[k, yy] = partial(k, 2 * yy + 1 - c).astype(BF16)
            start_sib(sib_grad(k, yy))
        for d in (2, 1, 3, 0):
            yy = lax.rem(y + d, 4)
            total = partial(k, 2 * yy + c)
            own_p[k, yy] = total.astype(BF16)
            sib_grad(k, yy).wait_recv()
            total = (total + sib_r[k, yy].astype(F32)).astype(BF16)
            if d == 0:
                y_r[k, yy] = total
            else:
                y_s[k, yy] = total
                grad_x[k].start_to(yy, pending)

    gat[...] = (att[...] * u_t[...].astype(F32) * live).astype(BF16)
    gw_out = mm(gat[...], c_all[...].reshape(2048, 512))
    for b in range(4):
        w_send[4 * b : 4 * b + 4, :, 512:640] = gw_out[:, b * 128 : (b + 1) * 128].astype(BF16).reshape(4, 32, 128)
    for k in chunks:
        gw_in = mm(g_t[...], e_all[k].reshape(2048, CW))
        n = CW // 32
        w_send[k * n : (k + 1) * n, :, 0:512] = gw_in.T.astype(BF16).reshape(n, 32, 512)
    ev_x.wait_recv()
    for k in chunks:
        sums = jnp.zeros((512, CW), F32)
        for yy in range(4):
            for same in range(2):
                blk = 2 * yy + (c if same else 1 - c)
                hit = onehot(iota((512, 256), 0) == ev_all[blk, 0:1, :])
                sums += mm_nt(hit, (own_p if same else sib_s)[k, yy])
        for b in range(2):
            blk = 2 * h + b
            hit = jnp.logical_and(
                iota((512, 256), 0) == ev_all[blk, 0:1, :], blk * 256 + iota((1, 256), 1) < len_ref[u]
            )
            sums += mm(onehot(hit), c_all[blk, :, k * CW : (k + 1) * CW])
        w_send[:, :, 640 + k * CW : 640 + (k + 1) * CW] = sums.astype(BF16).reshape(16, 32, CW)
    w_x.start(pending)
    w_recv[o] = w_send[o]

    cots = []
    for uu in range(2):
        here = (s * 256 + iota((256, 1), 0) < len_ref[uu]).astype(F32)
        cots.append((dout_ref[uu].astype(F32) * here).astype(BF16))
    cot = jnp.concatenate(cots, axis=0)
    hits = []
    for uu in range(2):
        hit = iota((512, 256), 0) + 512 == ev_loc[uu, 0:1, :]
        hits.append(onehot(jnp.logical_and(hit, jnp.concatenate([valid_col[...]] * 2, axis=1) > 0)))
    hits = jnp.concatenate(hits, axis=1)
    for k in chunks:
        grad_x[k].wait_recv()
        for uu in range(2):
            grad[:, uu * 256 : (uu + 1) * 256] = (
                y_r[k, 2 * uu].astype(F32) + y_r[k, 2 * uu + 1].astype(F32)
            ).astype(BF16)
        sums = mm_nt(hits, grad[...]) + mm(hits, cot[:, k * CW : (k + 1) * CW])
        s_send[k] = sums.astype(BF16).reshape(16, 32, CW)
        ret_x1[k].start(pending)
        q_recv[k, o] = s_send[k, o]

    w_x.wait_recv()
    total = jnp.sum(w_recv[...].astype(F32), axis=0)
    wu_s[...] = total[:, 0:640].astype(BF16).reshape(2, 16, 640)
    for i in range(8):
        left = 640 + 128 * (i % 4)
        hu_s[i] = total[16 * (i // 4) : 16 * (i // 4) + 16, left : left + 128].astype(BF16)
    wu = pltpu.make_async_remote_copy(
        src_ref=wu_s.at[1 - u],
        dst_ref=wu_r,
        send_sem=sem_sib.at[1, 0, 0],
        recv_sem=sem_sib.at[1, 1, 0],
        device_id=(lax.rem(s + 4, 8), o),
        device_id_type=MESH,
    )
    start_sib(wu)
    hot_x.start(pending)
    hu_r[s] = hu_s[s]

    r = iota((512, 512), 0)
    pick = onehot(iota((512, 512), 1) == (r & 15) * 32 + (r >> 4))
    for k in chunks:
        ret_x1[k].wait_recv()
        p_send[k] = mm(pick, q_recv[k].reshape(512, CW)).astype(BF16).reshape(8, 4, 16, CW)
        ret_x2[k].start(pending)
        ret[k, :, s] = p_send[k, s]

    place = {"y": y, "x": x, "z": z}
    device = {
        "y": lambda p: (2 * p + c, o),
        "x": lambda p: (s, 4 * p + z),
        "z": lambda p: (s, 4 * x + p),
    }

    def slab(i, core, known):
        at = dict(place)
        at.update(known)
        return ags[i].at[core, at["y"], at["x"], at["z"]]

    def gather_x(i, stage):
        order = AG_ORDERS[i]
        axis = order[stage]
        whole = {a: slice(None) for a in order[:stage]}
        block = lambda p: slab(i, c, {**whole, axis: p})
        return Exchange(
            4, place[axis], device[axis], lambda p: block(place[axis]), block,
            sem_ag.at[i, stage, 0], sem_ag.at[i, stage, 1],
        )

    def last_slab(i, core, p):
        order = AG_ORDERS[i]
        blk = slab(i, core, {order[0]: slice(None), order[1]: slice(None), order[2]: p})
        return to_sib(blk, blk, 2 + 2 * CHUNKS + i, p)

    gathers = [[gather_x(i, stage) for stage in range(3)] for i in range(3)]
    wu.wait_recv()
    pick_u = u.astype(F32)
    mine = total[0:16, 0:640] * (1.0 - pick_u) + total[16:32, 0:640] * pick_u + wu_r[...].astype(F32)
    mine = mine.astype(BF16)
    ag0[c, y, x, z] = mine[:, 0:256]
    ag1[c, y, x, z] = mine[:, 256:512]
    for i in range(2):
        gathers[i][0].start(pending)
    hot_x.wait_recv()
    ag2[c, y, x, z] = jnp.concatenate(
        [mine[:, 512:640], jnp.sum(hu_r[...].astype(F32), axis=0).astype(BF16)], axis=1
    )
    gathers[2][0].start(pending)
    for stage in range(2):
        for i in range(3):
            gathers[i][stage].wait_recv()
            gathers[i][stage + 1].start(pending)
    for i in range(3):
        start_sib(last_slab(i, c, place[AG_ORDERS[i][2]]))
    for d in (1, 3, 2):
        for i in range(3):
            p = lax.rem(place[AG_ORDERS[i][2]] + d, 4)
            gathers[i][2].wait_from(p)
            start_sib(last_slab(i, c, p))
    for k in chunks:
        ret_x2[k].wait_recv()
    for i in range(3):
        for p in range(4):
            last_slab(i, 1 - c, p).wait_recv()

    for wait in pending:
        wait()


def finish_kernel(a0, a1, a2, ret, asked, gin, gout, ghot, gcold):
    g = pl.program_id(0)
    for yy in range(4):
        for core in range(2):
            user, head = yy // 2, (yy % 2) * 2 + core
            seq = 2 * yy + core
            for zz in range(2):
                top = 32 * zz + 16 * user
                b0 = a0[core, yy, 0, zz].astype(F32)
                b1 = a1[core, yy, 0, zz].astype(F32)
                b2 = a2[core, yy, 0, zz].astype(F32)
                for b in range(4):
                    part = (b0, b1)[b // 2][:, (b % 2) * 128 : (b % 2) * 128 + 128]
                    gin[top : top + 16, b * 512 + head * 128 : b * 512 + head * 128 + 128] = part
                low = pl.multiple_of(head * 128 + 32 * (2 * lax.rem(g, 2) + zz) + 16 * user, 16)
                gout[pl.ds(low, 16), pl.ds(pl.multiple_of(g // 2 * 128, 128), 128)] = b2[:, 0:128]
                hot_top = 32 * zz + 16 * (seq // 4)
                ghot[hot_top : hot_top + 16, 128 * (seq % 4) : 128 * (seq % 4) + 128] = b2[:, 128:256]
    hits = jnp.concatenate([onehot(iota((256, 128), 0) + g * 256 == asked[i : i + 1, :]) for i in range(4)], axis=1)
    for k in range(CHUNKS):
        gcold[:, k * CW : (k + 1) * CW] = mm(hits, ret[k].reshape(512, CW))


def on_device(
    d_out, weight_in, weight_out, hot_table, cold_table, cold_ids, cold_counts, event_slots, lengths
):
    vmem = pl.BlockSpec(memory_space=pltpu.VMEM)
    smem = pl.BlockSpec(memory_space=pltpu.SMEM)
    big = lambda *shape: pltpu.VMEM(shape, BF16)
    wide = lambda *shape: pltpu.VMEM(shape, F32)
    sems = pltpu.SemaphoreType.DMA
    outs = [jax.ShapeDtypeStruct((2, 4, 4, 4, 16, 256), BF16)] * 3 + [
        jax.ShapeDtypeStruct((CHUNKS, 4, 8, 16, CW), BF16),
        jax.ShapeDtypeStruct((8, 128), jnp.int32),
    ]
    ints = lambda *shape: pltpu.VMEM(shape, jnp.int32)
    scratch = [
        ints(128, 128),
        ints(8, 16, 128),
        ints(16, 8, 128),
        ints(8, 16, 128),
        ints(2, 8, 256),
        ints(8, 8, 256),
        ints(512, 128),
        wide(512, 128),
        big(CHUNKS, 4, 8, 16, CW),
        big(CHUNKS, 8, 4, 16, CW),
        big(CHUNKS, 16, 32, CW),
        big(CHUNKS, 16, 32, CW),
        big(CHUNKS, 2, 256, CW),
        big(CHUNKS, 8, 256, CW),
        big(8, 256, 512),
        big(512, 512),
        big(512, 512),
        sems((4,)),
        wide(512, 2048),
        big(128, 2048),
        big(128, 2048),
        big(128, 2048),
        big(128, 2048),
        big(2048, 128),
        big(2048, 128),
        big(2048, 128),
        big(10, 512, 512),
        big(10, 512, 512),
        wide(128, 2048),
        wide(128, 2048),
        big(128, 2048),
        big(128, 2048),
        big(2048, 128),
        wide(128, 2048),
        wide(2048, 128),
        wide(2048, 128),
        big(512, 2048),
        wide(4, 4, 2048),
        big(CHUNKS, 4, CW, 256),
        big(CHUNKS, 4, CW, 256),
        big(CHUNKS, 4, CW, 256),
        big(CHUNKS, 4, CW, 256),
        big(CHUNKS, 4, CW, 256),
        big(CW, 512),
        big(16, 32, 1152),
        big(16, 32, 1152),
        big(2, 16, 640),
        big(16, 640),
        big(8, 16, 128),
        big(8, 16, 128),
        big(CHUNKS, 16, 32, CW),
        big(CHUNKS, 16, 32, CW),
        big(CHUNKS, 8, 4, 16, CW),
        sems((2 + 2 * CHUNKS, 2, 16)),
        sems((3 + 2 * CHUNKS, 2, 8)),
        sems((2 + 2 * CHUNKS, 2, 4)),
        sems((3, 3, 2, 4)),
        sems((5 + 2 * CHUNKS, 2, 4)),
    ]
    a0, a1, a2, ret, asked = pl.pallas_call(
        main_kernel,
        out_shape=outs,
        in_specs=[vmem] * 3 + [smem] + [vmem] * 4 + [pl.BlockSpec(memory_space=pl.ANY)],
        out_specs=[vmem] * 5,
        scratch_shapes=scratch,
        compiler_params=pltpu.CompilerParams(
            collective_id=0, has_side_effects=True, vmem_limit_bytes=60 * 1024 * 1024
        ),
        name="layer",
    )(
        cold_ids.T, cold_counts.reshape(1, 128), event_slots, lengths,
        d_out, weight_out, hot_table, cold_table, weight_in,
    )

    part = pl.BlockSpec((2, 4, 1, 2, 16, 256), lambda g: (0, 0, g // 2, lax.rem(g, 2), 0, 0))
    return pl.pallas_call(
        finish_kernel,
        grid=(8,),
        out_shape=[
            jax.ShapeDtypeStruct((512, 2048), F32),
            jax.ShapeDtypeStruct((512, 512), F32),
            jax.ShapeDtypeStruct((512, 512), F32),
            jax.ShapeDtypeStruct((2048, 512), F32),
        ],
        in_specs=[part] * 3
        + [
            pl.BlockSpec((CHUNKS, 4, 8, 16, CW), lambda g: (0, 0, 0, 0, 0)),
            pl.BlockSpec((8, 128), lambda g: (0, 0)),
        ],
        out_specs=[
            pl.BlockSpec((64, 2048), lambda g: (g, 0)),
            pl.BlockSpec((512, 512), lambda g: (0, 0)),
            pl.BlockSpec((64, 512), lambda g: (g, 0)),
            pl.BlockSpec((256, 512), lambda g: (g, 0)),
        ],
        compiler_params=pltpu.CompilerParams(vmem_limit_bytes=60 * 1024 * 1024),
        name="finish",
    )(a0, a1, a2, ret, asked)


def solution(mesh):
    placed = (
        P("own", "seq", None),
        P(),
        P(),
        P(),
        P(("seq", "own"), None),
        P(("seq", "own"), None),
        P(("seq", "own")),
        P("own", "seq"),
        P("own"),
    )
    return jax.shard_map(
        on_device,
        mesh=mesh,
        in_specs=placed,
        out_specs=(P(), P(), P(), P(("seq", "own"), None)),
        check_vma=False,
    )
```

```python
import functools

import jax
import jax.numpy as jnp
from jax import lax
from jax.experimental import pallas as pl
from jax.experimental.pallas import tpu as pltpu
from jax.sharding import PartitionSpec as P

F32 = jnp.float32
BF16 = jnp.bfloat16
MESH = pl.DeviceIdType.MESH
SCALE = 128 ** (-0.5)
AG_ORDERS = (("z", "x", "y"), ("x", "y", "z"), ("y", "z", "x"))
HEAD = 2
HW = 512 // HEAD
CHUNKS = 2
CW = 512 // CHUNKS
HALF = 256 // CHUNKS


def mm(a, b):
    return jnp.dot(a, b, preferred_element_type=F32)


def mm_nt(a, b):
    return lax.dot_general(a, b, (((1,), (1,)), ((), ())), preferred_element_type=F32)


def iota(shape, dim):
    return lax.broadcasted_iota(jnp.int32, shape, dim)


def onehot(hit):
    return hit.astype(F32).astype(BF16)


class Exchange:
    def __init__(self, n, me, device, src, dst, send_sem, recv_sem):
        self.n, self.me, self.device, self.src, self.dst = n, me, device, src, dst
        self.send_sem, self.recv_sem = send_sem, recv_sem

    def _out(self, p):
        return pltpu.make_async_remote_copy(
            src_ref=self.src(p),
            dst_ref=self.dst(self.me),
            send_sem=self.send_sem.at[p],
            recv_sem=self.recv_sem.at[self.me],
            device_id=self.device(p),
            device_id_type=MESH,
        )

    def _in(self, p):
        return pltpu.make_async_remote_copy(
            src_ref=self.src(p),
            dst_ref=self.dst(p),
            send_sem=self.send_sem.at[p],
            recv_sem=self.recv_sem.at[p],
            device_id=self.device(p),
            device_id_type=MESH,
        )

    def peer(self, k):
        return lax.rem(self.me + k, self.n)

    def _each(self, f):
        if self.n <= 16:
            for k in range(1, self.n):
                f(self.peer(k))
        else:
            pl.loop(1, self.n)(lambda k: f(self.peer(k)))

    def start(self, pending):
        pending.append(self.wait_send)
        self._each(lambda p: self._out(p).start())

    def start_to(self, p, pending):
        pending.append(lambda: self._out(p).wait_send())
        self._out(p).start()

    def wait_from(self, p):
        self._in(p).wait_recv()

    def wait_recv(self):
        self._each(lambda p: self._in(p).wait_recv())

    def wait_send(self):
        self._each(lambda p: self._out(p).wait_send())


def main_kernel(
    idst_ref, counts_ref, ev_ref, len_ref, dout_any, wout_any, hot_any, table_any, win_ref,
    ag0, ag1, ag2, ret, asked,
    id_pad, id_loc, id_a, id_b, ev_loc, ev_all, code_col, valid_col,
    got, rows, perm, fetched, e_loc, e_all, c_all,
    wh, wht, wh_sem, slope_pre, u_t, q_t, k_t, v_t, q_n, k_n, v_n,
    w_st, sl_st, att, gg, gat, ga_t, ga_n, gq, gk, gv, g_t, stat,
    sib_s, sib_r, tot, g_r, grad, w1_send, w1_recv, w2_send, w2_recv, wu_s, wu_r, hu_s, hu_r,
    s_send, q_recv, p_send, dout_ref, wout_ref, hot_ref, table_ref, load_sem,
    sem16, sem8, sem4, sem_ag, sem_sib,
):
    s, o = lax.axis_index("seq"), lax.axis_index("own")
    y, c = s // 2, lax.rem(s, 2)
    u, h = s // 4, lax.rem(s, 4)
    x, z = o // 4, lax.rem(o, 4)
    sib = (2 * y + 1 - c, o)
    ags = (ag0, ag1, ag2)
    chunks = range(CHUNKS)
    heads = range(HEAD)
    pending = []

    barrier = pltpu.get_barrier_semaphore()

    @pl.loop(1, 16)
    def _(k):
        pl.semaphore_signal(barrier, inc=1, device_id=(s, lax.rem(o + k, 16)), device_id_type=MESH)

    @pl.loop(1, 8)
    def _(k):
        pl.semaphore_signal(barrier, inc=1, device_id=(lax.rem(s + k, 8), o), device_id_type=MESH)

    def load_w(b):
        return pltpu.make_async_copy(
            win_ref.at[:, pl.ds(pl.multiple_of(b * 512 + h * 128, 128), 128)],
            wh.at[:, pl.ds(b * 128, 128)],
            wh_sem.at[b],
        )

    loads = [
        pltpu.make_async_copy(a, b, load_sem.at[i])
        for i, (a, b) in enumerate(
            ((table_any, table_ref), (dout_any, dout_ref), (hot_any, hot_ref), (wout_any, wout_ref))
        )
    ]
    for copy in loads:
        copy.start()
    for b in range(4):
        load_w(b).start()

    def own_x(i, src, dst):
        return Exchange(16, o, lambda p: (s, p), src, dst, sem16.at[i, 0], sem16.at[i, 1])

    def seq_x(i, src, dst):
        return Exchange(8, s, lambda p: (p, o), src, dst, sem8.at[i, 0], sem8.at[i, 1])

    def y_x(i, src, dst):
        return Exchange(4, y, lambda p: (2 * p + c, o), src, dst, sem4.at[i, 0], sem4.at[i, 1])

    def head_x(i, src, dst):
        return Exchange(4, h, lambda p: (4 * u + p, o), src, dst, sem4.at[i, 0], sem4.at[i, 1])

    def to_sib(src, dst, i, j):
        return pltpu.make_async_remote_copy(
            src_ref=src, dst_ref=dst, send_sem=sem_sib.at[i, 0, j], recv_sem=sem_sib.at[i, 1, j],
            device_id=sib, device_id_type=MESH,
        )

    def start_sib(copy):
        pending.append(copy.wait_send)
        copy.start()

    ids_x1 = own_x(0, lambda p: id_loc.at[:, p], lambda p: id_a.at[p])
    ids_x2 = seq_x(0, lambda p: id_a.at[:, p], lambda p: id_b.at[p])
    ev_x = seq_x(1, lambda p: ev_loc.at[p // 4], lambda p: ev_all.at[p])
    rows_x1 = [seq_x(2 + k, lambda p, k=k: got.at[k, :, p], lambda p, k=k: rows.at[k, p]) for k in heads]
    ret_x2 = [
        seq_x(2 + HEAD + k, lambda p, k=k: p_send.at[k, p], lambda p, k=k: ret.at[k, :, p]) for k in chunks
    ]
    w1_x = own_x(1, lambda p: w1_send.at[p], lambda p: w1_recv.at[p])
    w2_x = own_x(2, lambda p: w2_send.at[p], lambda p: w2_recv.at[p])
    rows_x2 = [own_x(3 + k, lambda p, k=k: perm.at[k, p], lambda p, k=k: fetched.at[k, p]) for k in heads]
    ret_x1 = [
        own_x(3 + HEAD + k, lambda p, k=k: s_send.at[k, p], lambda p, k=k: q_recv.at[k, p]) for k in chunks
    ]
    cot_x = y_x(0, lambda p: dout_ref.at[p // 2], lambda p: c_all.at[2 * p + c])
    stat_x = head_x(1, lambda p: stat.at[h], lambda p: stat.at[p])
    emb_x = [
        y_x(2 + k, lambda p, k=k: e_loc.at[k, p // 2], lambda p, k=k: e_all.at[k, 2 * p + c]) for k in heads
    ]
    hot_x = y_x(2 + HEAD, lambda p: hu_s.at[p], lambda p: hu_r.at[p])

    def positions(k, p):
        return tot.at[k, :, pl.ds(pl.multiple_of(p * 256, 256), 256)]

    grad_x = [
        seq_x(2 + HEAD + CHUNKS + k, lambda p, k=k: positions(k, p), lambda p, k=k: g_r.at[k, p]) for k in chunks
    ]

    def sib_block(buf, i, yy):
        return to_sib(buf.at[2 * yy + c], buf.at[2 * yy + c], i, yy)

    def sib_block_in(buf, i, yy):
        return to_sib(buf.at[2 * yy + 1 - c], buf.at[2 * yy + 1 - c], i, yy)

    id_pad[...] = jnp.zeros_like(id_pad)
    id_pad[0:4, :] = idst_ref[...]
    id_loc[...] = id_pad[...].T.reshape(8, 16, 128)

    pl.semaphore_wait(barrier, 22)

    ids_x1.start(pending)
    id_a[o] = id_loc[:, o, :]

    codes = []
    for uu in range(2):
        e = ev_ref[uu : uu + 1, :]
        cold = e - 512
        code = jnp.where(e < 512, e, 512 + ((cold >> 2) & 15) * 32 + (cold >> 6) * 4 + (cold & 3))
        ev_loc[uu] = jnp.broadcast_to(code, (8, 256))
        codes.append(code)
    code_row = jnp.concatenate(codes, axis=1)
    code_col[...] = jnp.broadcast_to(code_row, (128, 512)).T
    counts = counts_ref[...].astype(F32).astype(BF16)
    l = iota((128, 512), 1)
    pick = onehot(iota((128, 512), 0) == ((l >> 2) & 7) * 16 + (l >> 5))
    valid_row = (iota((8, 512), 1) & 3).astype(F32) < mm(jnp.broadcast_to(counts, (8, 128)), pick)
    valid_row = valid_row[0:1]
    l = iota((512, 128), 0)
    pick = onehot(iota((512, 128), 1) == ((l >> 2) & 7) * 16 + (l >> 5))
    valid_col[...] = (
        (l & 3).astype(F32) < mm_nt(pick, jnp.broadcast_to(counts, (128, 128)))
    ).astype(F32)
    for b in range(4):
        load_w(b).wait()
    wht[...] = wh[...].T
    for copy in loads:
        copy.wait()
    c_all[s] = dout_ref[u]

    ids_x1.wait_recv()
    ids_x2.start(pending)
    id_b[s] = id_a[:, s, :]
    ids_x2.wait_recv()

    asked_ids = id_b[...].reshape(128, 128)
    for i in range(4):
        hit = onehot(iota((128, 2048), 1) == asked_ids[:, i : i + 1])
        found = mm(hit, table_ref[...]).astype(BF16)
        for k in heads:
            got[k, i] = found[:, k * HW : (k + 1) * HW].reshape(8, 16, HW)
    for k in heads:
        rows_x1[k].start(pending)
        rows[k, s] = got[k, :, s]
    ev_x.start(pending)
    ev_all[s] = ev_loc[u]
    asked[...] = asked_ids.T[0:8, :]
    start_sib(sib_block(c_all, 0, y))
    hot_hits = [onehot(code_col[...] == iota((512, 128), 1) + b * 128) for b in range(4)]
    emb = mm(jnp.concatenate(hot_hits, axis=1), hot_ref[...])
    r = iota((512, 512), 0)
    pick = onehot(iota((512, 512), 1) == (r & 31) * 16 + (r >> 5))
    for k in heads:
        rows_x1[k].wait_recv()
        perm[k] = mm(pick, rows[k].reshape(512, HW)).astype(BF16).reshape(16, 32, HW)
        rows_x2[k].start(pending)
        fetched[k, o] = perm[k, o]
    for d in (1, 3):
        cot_x.start_to(lax.rem(y + d, 4), pending)
    cold_hits = [
        onehot(jnp.logical_and(
            code_col[...] == iota((512, 128), 1) + (512 + b * 128), valid_row[:, b * 128 : (b + 1) * 128]
        ))
        for b in range(4)
    ]
    cold_hits = jnp.concatenate(cold_hits, axis=1)
    for k in heads:
        rows_x2[k].wait_recv()
        part = emb[:, k * HW : (k + 1) * HW] + mm(cold_hits, fetched[k].reshape(512, HW))
        e_loc[k] = part.astype(BF16).reshape(2, 256, HW)
        emb_x[k].start(pending)
        e_all[k, s] = e_loc[k, u]
        start_sib(sib_block(e_all.at[k], 2 + k, y))

    def project(blk):
        cols = pl.ds(pl.multiple_of(blk * 256, 256), 256)
        pre = mm_nt(wht[...], jnp.concatenate([e_all[k, blk] for k in heads], axis=1))
        sig = 0.5 + 0.5 * jnp.tanh(0.5 * pre)
        act = pre * sig
        slope_pre[:, cols] = sig + act * (1.0 - sig)
        act = act.astype(BF16)
        u_t[:, cols] = act[0:128]
        q_t[:, cols] = act[128:256]
        k_t[:, cols] = act[256:384]
        keep = (blk * 256 + iota((1, 256), 1) < len_ref[u]).astype(F32)
        val = (act[384:512].astype(F32) * keep).astype(BF16)
        v_t[:, cols] = val
        q_n[cols, :] = act[128:256].T
        k_n[cols, :] = act[256:384].T
        v_n[cols, :] = val.T

    for d in (1, 3):
        cot_x.wait_from(lax.rem(y + d, 4))
        start_sib(sib_block(c_all, 0, lax.rem(y + d, 4)))
    project(s)
    for k in heads:
        for d in (1, 3, 2):
            yy = lax.rem(y + d, 4)
            emb_x[k].wait_from(yy)
            start_sib(sib_block(e_all.at[k], 2 + k, yy))
            if k == HEAD - 1:
                project(2 * yy + c)
    cot_x.start_to(lax.rem(y + 2, 4), pending)
    for d in (0, 1, 3, 2):
        yy = lax.rem(y + d, 4)
        for k in heads:
            sib_block_in(e_all.at[k], 2 + k, yy).wait_recv()
        project(2 * yy + 1 - c)

    att[...] = jnp.zeros_like(att)

    def forward(i, j, diag):
        keys = pl.multiple_of(j * 512, 512)
        qs = pl.ds(pl.multiple_of(i * 512, 512), 512)
        at = i * (i + 1) // 2 + j
        for m in range(4):
            half = mm(k_n[pl.ds(keys + m * 128, 128), :], q_t[:, qs]) * (0.5 * SCALE)
            t = jnp.tanh(half)
            a = 1.0 + t
            w = half * a
            slope = a * ((1.0 + 2.0 * half) - w)
            if diag:
                ok = iota((128, 512), 0) + m * 128 <= iota((128, 512), 1)
                w = jnp.where(ok, w, 0.0)
                slope = jnp.where(ok, slope, 0.0)
            w_st[at, m * 128 : (m + 1) * 128, :] = w.astype(BF16)
            sl_st[at, m * 128 : (m + 1) * 128, :] = slope.astype(BF16)
        att[:, qs] += mm(v_t[:, pl.ds(keys, 512)], w_st[at])

    @pl.loop(0, 4)
    def _(i):
        @pl.loop(0, i)
        def _(j):
            forward(i, j, False)

        forward(i, i, True)

    cot_x.wait_from(lax.rem(y + 2, 4))
    start_sib(sib_block(c_all, 0, lax.rem(y + 2, 4)))
    for d in range(4):
        sib_block_in(c_all, 0, lax.rem(y + d, 4)).wait_recv()
    live = (iota((1, 2048), 1) < len_ref[u]).astype(F32)
    wo = wout_ref[pl.ds(pl.multiple_of(h * 128, 128), 128), :]
    gg[...] = mm_nt(wo, c_all[...].reshape(2048, 512)) * live
    inv = 1.0 / jnp.full((1, 2048), len_ref[u], jnp.int32).astype(F32)
    mine = att[...] * inv
    m1 = jnp.sum(mine, axis=0, keepdims=True) * (1.0 / 128)
    dev = mine - m1
    gn = gg[...] * u_t[...].astype(F32)
    stat[h, 0:1, :] = m1
    stat[h, 1:2, :] = jnp.sum(dev * dev, axis=0, keepdims=True)
    stat[h, 2:3, :] = jnp.sum(gn, axis=0, keepdims=True)
    stat[h, 3:4, :] = jnp.sum(gn * dev, axis=0, keepdims=True)
    stat_x.start(pending)
    stat_x.wait_recv()
    both = stat[...]
    mean = jnp.sum(both[:, 0, :], axis=0, keepdims=True) * 0.25
    off = both[:, 0, :] - mean
    var = (jnp.sum(both[:, 1, :], axis=0, keepdims=True) + 128.0 * jnp.sum(off * off, axis=0, keepdims=True)) * (
        1.0 / 512
    )
    rstd = lax.rsqrt(var + 1e-05)
    mean1 = jnp.sum(both[:, 2, :], axis=0, keepdims=True) * (1.0 / 512)
    mean2 = jnp.sum(both[:, 3, :] + off * both[:, 2, :], axis=0, keepdims=True) * (rstd * (1.0 / 512))
    normed = (att[...] * inv - mean) * rstd
    att[...] = normed
    gn = gg[...] * u_t[...].astype(F32)
    ga_t[...] = ((gn - mean1 - normed * mean2) * (rstd * inv)).astype(BF16)
    for b in range(8):
        ga_n[b * 256 : (b + 1) * 256, :] = ga_t[:, b * 256 : (b + 1) * 256].T

    def to_rows(rows_by_cols):
        n = rows_by_cols.shape[1]
        return rows_by_cols.astype(BF16).reshape(-1, 32, n)

    gat[...] = (att[...] * u_t[...].astype(F32) * live).astype(BF16)
    gw_out = mm(gat[...], c_all[...].reshape(2048, 512))
    for b in range(4):
        w1_send[4 * b : 4 * b + 4, :, 0:128] = to_rows(gw_out[:, b * 128 : (b + 1) * 128])
    g_t[0:128, :] = (gg[...] * att[...] * slope_pre[0:128, :]).astype(BF16)
    n = HW // 32
    for k in heads:
        w1_send[k * n : (k + 1) * n, :, 128:256] = to_rows(mm(g_t[0:128, :], e_all[k].reshape(2048, HW)).T)
    w1_x.start(pending)
    w1_recv[o] = w1_send[o]

    gq[...] = jnp.zeros_like(gq)
    gk[...] = jnp.zeros_like(gk)
    gv[...] = jnp.zeros_like(gv)

    def backward(i, j):
        keys = pl.multiple_of(j * 512, 512)
        qs = pl.ds(pl.multiple_of(i * 512, 512), 512)
        at = i * (i + 1) // 2 + j
        for m in range(4):
            gw = mm(v_n[pl.ds(keys + m * 128, 128), :], ga_t[:, qs])
            ds = gw * sl_st[at, m * 128 : (m + 1) * 128, :].astype(F32)
            sl_st[at, m * 128 : (m + 1) * 128, :] = ds.astype(BF16)
        gk[pl.ds(keys, 512), :] += mm(sl_st[at], q_n[qs, :])
        gv[pl.ds(keys, 512), :] += mm(w_st[at], ga_n[qs, :])
        gq[:, qs] += mm(k_t[:, pl.ds(keys, 512)], sl_st[at])

    @pl.loop(0, 4)
    def _(i):
        @pl.loop(0, i + 1)
        def _(j):
            backward(i, j)

    keep = (iota((1, 2048), 1) < len_ref[u]).astype(F32)
    g_t[128:256, :] = (gq[...] * (0.5 * SCALE) * slope_pre[128:256, :]).astype(BF16)
    for b in range(8):
        cols = slice(b * 256, (b + 1) * 256)
        g_t[256:384, cols] = (gk[cols, :].T * (0.5 * SCALE) * slope_pre[256:384, cols]).astype(BF16)
        g_t[384:512, cols] = (gv[cols, :].T * keep[:, cols] * slope_pre[384:512, cols]).astype(BF16)

    def partial(k, half):
        return mm(wh[pl.ds(pl.multiple_of(half * 256 + k * HALF, HALF), HALF), :], g_t[...])

    def sib_grad(k):
        return to_sib(sib_s.at[k], sib_r.at[k], 2 + HEAD, k)

    for k in chunks:
        sib_s[k] = partial(k, 1 - c).astype(BF16)
        start_sib(sib_grad(k))
    for k in chunks:
        total = partial(k, c)
        sib_grad(k).wait_recv()
        tot[k] = (total + sib_r[k].astype(F32)).astype(BF16)
        grad_x[k].start(pending)
        g_r[k, s] = positions(k, s)[...]

    for k in heads:
        w2_send[k * n : (k + 1) * n, :, 0:384] = to_rows(mm(g_t[128:512, :], e_all[k].reshape(2048, HW)).T)
    ev_x.wait_recv()
    sums = jnp.zeros((512, 256), F32)
    for blk in range(8):
        hit = onehot(iota((512, 256), 0) == ev_all[blk, 0:1, :])
        sums += mm_nt(hit, jnp.concatenate([tot[k, :, blk * 256 : (blk + 1) * 256] for k in chunks], axis=0))
    for b in range(4):
        blk = 4 * lax.rem(y, 2) + b
        hit = jnp.logical_and(
            iota((512, 256), 0) == ev_all[blk, 0:1, :], blk * 256 + iota((1, 256), 1) < len_ref[u]
        )
        sums += mm(onehot(hit), c_all[blk, :, pl.ds(pl.multiple_of(c * 256, 256), 256)])
    w2_send[:, :, 384:640] = to_rows(sums)
    w2_x.start(pending)
    w2_recv[o] = w2_send[o]

    cots = []
    for uu in range(2):
        here = (s * 256 + iota((256, 1), 0) < len_ref[uu]).astype(F32)
        cots.append((dout_ref[uu].astype(F32) * here).astype(BF16))
    cot = jnp.concatenate(cots, axis=0)
    hits = []
    for uu in range(2):
        hit = iota((512, 256), 0) + 512 == ev_loc[uu, 0:1, :]
        hits.append(onehot(jnp.logical_and(hit, jnp.concatenate([valid_col[...]] * 2, axis=1) > 0)))
    hits = jnp.concatenate(hits, axis=1)
    for k in chunks:
        grad_x[k].wait_recv()
        here = []
        for half in range(2):
            rows_k = slice(half * HALF, (half + 1) * HALF)
            for uu in range(2):
                grad[rows_k, uu * 256 : (uu + 1) * 256] = (
                    g_r[k, 4 * uu + half].astype(F32) + g_r[k, 4 * uu + 2 + half].astype(F32)
                ).astype(BF16)
            here.append(cot[:, half * 256 + k * HALF : half * 256 + (k + 1) * HALF])
        sums = mm_nt(hits, grad[...]) + mm(hits, jnp.concatenate(here, axis=1))
        s_send[k] = to_rows(sums)
        ret_x1[k].start(pending)
        q_recv[k, o] = s_send[k, o]

    w1_x.wait_recv()
    total1 = jnp.sum(w1_recv[...].astype(F32), axis=0)
    w2_x.wait_recv()
    total2 = jnp.sum(w2_recv[...].astype(F32), axis=0)
    total = jnp.concatenate([total1[:, 128:256], total2[:, 0:384], total1[:, 0:128]], axis=1)
    wu_s[...] = total.astype(BF16).reshape(2, 16, 640)
    for i in range(4):
        left = 384 + 128 * (i % 2)
        hu_s[i] = total2[16 * (i // 2) : 16 * (i // 2) + 16, left : left + 128].astype(BF16)
    wu = pltpu.make_async_remote_copy(
        src_ref=wu_s.at[1 - u],
        dst_ref=wu_r,
        send_sem=sem_sib.at[1, 0, 0],
        recv_sem=sem_sib.at[1, 1, 0],
        device_id=(lax.rem(s + 4, 8), o),
        device_id_type=MESH,
    )
    start_sib(wu)
    hot_x.start(pending)
    hu_r[y] = hu_s[y]

    r = iota((512, 512), 0)
    pick = onehot(iota((512, 512), 1) == (r & 15) * 32 + (r >> 4))

    def second_hop(k):
        ret_x1[k].wait_recv()
        p_send[k] = mm(pick, q_recv[k].reshape(512, CW)).astype(BF16).reshape(8, 4, 16, CW)
        ret_x2[k].start(pending)
        ret[k, :, s] = p_send[k, s]

    second_hop(0)

    place = {"y": y, "x": x, "z": z}
    device = {
        "y": lambda p: (2 * p + c, o),
        "x": lambda p: (s, 4 * p + z),
        "z": lambda p: (s, 4 * x + p),
    }

    def slab(i, core, known):
        at = dict(place)
        at.update(known)
        return ags[i].at[core, at["y"], at["x"], at["z"]]

    def gather_x(i, stage):
        order = AG_ORDERS[i]
        axis = order[stage]
        whole = {a: slice(None) for a in order[:stage]}
        block = lambda p: slab(i, c, {**whole, axis: p})
        return Exchange(
            4, place[axis], device[axis], lambda p: block(place[axis]), block,
            sem_ag.at[i, stage, 0], sem_ag.at[i, stage, 1],
        )

    def last_slab(i, core, p):
        order = AG_ORDERS[i]
        blk = slab(i, core, {order[0]: slice(None), order[1]: slice(None), order[2]: p})
        return to_sib(blk, blk, 3 + HEAD + i, p)

    gathers = [[gather_x(i, stage) for stage in range(3)] for i in range(3)]
    wu.wait_recv()
    pick_u = u.astype(F32)
    mine = total[0:16] * (1.0 - pick_u) + total[16:32] * pick_u + wu_r[...].astype(F32)
    mine = mine.astype(BF16)
    ag0[c, y, x, z] = mine[:, 0:256]
    ag1[c, y, x, z] = mine[:, 256:512]
    for i in range(2):
        gathers[i][0].start(pending)
    hot_x.wait_recv()
    ag2[c, y, x, z] = jnp.concatenate(
        [mine[:, 512:640], jnp.sum(hu_r[...].astype(F32), axis=0).astype(BF16)], axis=1
    )
    gathers[2][0].start(pending)
    for k in range(1, CHUNKS):
        second_hop(k)
    for stage in range(2):
        for i in range(3):
            gathers[i][stage].wait_recv()
            gathers[i][stage + 1].start(pending)
    for i in range(3):
        start_sib(last_slab(i, c, place[AG_ORDERS[i][2]]))
    for d in (1, 3, 2):
        for i in range(3):
            p = lax.rem(place[AG_ORDERS[i][2]] + d, 4)
            gathers[i][2].wait_from(p)
            start_sib(last_slab(i, c, p))
    for k in chunks:
        ret_x2[k].wait_recv()
    for i in range(3):
        for p in range(4):
            last_slab(i, 1 - c, p).wait_recv()

    for wait in pending:
        wait()


def finish_kernel(a0, a1, a2, ret, asked, gin, gout, ghot, gcold):
    g = pl.program_id(0)
    for yy in range(4):
        for core in range(2):
            user, head = yy // 2, (yy % 2) * 2 + core
            for zz in range(2):
                top = 32 * zz + 16 * user
                b0 = a0[core, yy, 0, zz].astype(F32)
                b1 = a1[core, yy, 0, zz].astype(F32)
                b2 = a2[core, yy, 0, zz].astype(F32)
                for b in range(4):
                    part = (b0, b1)[b // 2][:, (b % 2) * 128 : (b % 2) * 128 + 128]
                    gin[top : top + 16, b * 512 + head * 128 : b * 512 + head * 128 + 128] = part
                low = pl.multiple_of(head * 128 + 32 * (2 * lax.rem(g, 2) + zz) + 16 * user, 16)
                gout[pl.ds(low, 16), pl.ds(pl.multiple_of(g // 2 * 128, 128), 128)] = b2[:, 0:128]
                hot_top = 32 * zz + 16 * (yy // 2)
                left = 256 * core + 128 * (yy % 2)
                ghot[hot_top : hot_top + 16, left : left + 128] = b2[:, 128:256]
    hits = jnp.concatenate([onehot(iota((256, 128), 0) + g * 256 == asked[i : i + 1, :]) for i in range(4)], axis=1)
    for k in range(CHUNKS):
        sums = mm(hits, ret[k].reshape(512, CW))
        for half in range(2):
            left = half * 256 + k * HALF
            gcold[:, left : left + HALF] = sums[:, half * HALF : (half + 1) * HALF]


def on_device(
    d_out, weight_in, weight_out, hot_table, cold_table, cold_ids, cold_counts, event_slots, lengths
):
    vmem = pl.BlockSpec(memory_space=pltpu.VMEM)
    smem = pl.BlockSpec(memory_space=pltpu.SMEM)
    big = lambda *shape: pltpu.VMEM(shape, BF16)
    wide = lambda *shape: pltpu.VMEM(shape, F32)
    sems = pltpu.SemaphoreType.DMA
    outs = [jax.ShapeDtypeStruct((2, 4, 4, 4, 16, 256), BF16)] * 3 + [
        jax.ShapeDtypeStruct((CHUNKS, 4, 8, 16, CW), BF16),
        jax.ShapeDtypeStruct((8, 128), jnp.int32),
    ]
    ints = lambda *shape: pltpu.VMEM(shape, jnp.int32)
    scratch = [
        ints(128, 128),
        ints(8, 16, 128),
        ints(16, 8, 128),
        ints(8, 16, 128),
        ints(2, 8, 256),
        ints(8, 8, 256),
        ints(512, 128),
        wide(512, 128),
        big(HEAD, 4, 8, 16, HW),
        big(HEAD, 8, 4, 16, HW),
        big(HEAD, 16, 32, HW),
        big(HEAD, 16, 32, HW),
        big(HEAD, 2, 256, HW),
        big(HEAD, 8, 256, HW),
        big(8, 256, 512),
        big(512, 512),
        big(512, 512),
        sems((4,)),
        wide(512, 2048),
        big(128, 2048),
        big(128, 2048),
        big(128, 2048),
        big(128, 2048),
        big(2048, 128),
        big(2048, 128),
        big(2048, 128),
        big(10, 512, 512),
        big(10, 512, 512),
        wide(128, 2048),
        wide(128, 2048),
        big(128, 2048),
        big(128, 2048),
        big(2048, 128),
        wide(128, 2048),
        wide(2048, 128),
        wide(2048, 128),
        big(512, 2048),
        wide(4, 4, 2048),
        big(CHUNKS, HALF, 2048),
        big(CHUNKS, HALF, 2048),
        big(CHUNKS, HALF, 2048),
        big(CHUNKS, 8, HALF, 256),
        big(CW, 512),
        big(16, 32, 256),
        big(16, 32, 256),
        big(16, 32, 640),
        big(16, 32, 640),
        big(2, 16, 640),
        big(16, 640),
        big(4, 16, 128),
        big(4, 16, 128),
        big(CHUNKS, 16, 32, CW),
        big(CHUNKS, 16, 32, CW),
        big(CHUNKS, 8, 4, 16, CW),
        big(2, 256, 512),
        big(512, 512),
        big(512, 512),
        big(2048, 512),
        sems((4,)),
        sems((3 + HEAD + CHUNKS, 2, 16)),
        sems((2 + HEAD + 2 * CHUNKS, 2, 8)),
        sems((3 + HEAD, 2, 4)),
        sems((3, 3, 2, 4)),
        sems((6 + HEAD, 2, 4)),
    ]
    a0, a1, a2, ret, asked = pl.pallas_call(
        main_kernel,
        out_shape=outs,
        in_specs=[vmem] * 3 + [smem] + [pl.BlockSpec(memory_space=pl.ANY)] * 5,
        out_specs=[vmem] * 5,
        scratch_shapes=scratch,
        compiler_params=pltpu.CompilerParams(
            collective_id=0, has_side_effects=True, vmem_limit_bytes=60 * 1024 * 1024
        ),
        name="layer",
    )(
        cold_ids.T, cold_counts.reshape(1, 128), event_slots, lengths,
        d_out, weight_out, hot_table, cold_table, weight_in,
    )

    part = pl.BlockSpec((2, 4, 1, 2, 16, 256), lambda g: (0, 0, g // 2, lax.rem(g, 2), 0, 0))
    return pl.pallas_call(
        finish_kernel,
        grid=(8,),
        out_shape=[
            jax.ShapeDtypeStruct((512, 2048), F32),
            jax.ShapeDtypeStruct((512, 512), F32),
            jax.ShapeDtypeStruct((512, 512), F32),
            jax.ShapeDtypeStruct((2048, 512), F32),
        ],
        in_specs=[part] * 3
        + [
            pl.BlockSpec((CHUNKS, 4, 8, 16, CW), lambda g: (0, 0, 0, 0, 0)),
            pl.BlockSpec((8, 128), lambda g: (0, 0)),
        ],
        out_specs=[
            pl.BlockSpec((64, 2048), lambda g: (g, 0)),
            pl.BlockSpec((512, 512), lambda g: (0, 0)),
            pl.BlockSpec((64, 512), lambda g: (g, 0)),
            pl.BlockSpec((256, 512), lambda g: (g, 0)),
        ],
        compiler_params=pltpu.CompilerParams(vmem_limit_bytes=60 * 1024 * 1024),
        name="finish",
    )(a0, a1, a2, ret, asked)


def solution(mesh):
    placed = (
        P("own", "seq", None),
        P(),
        P(),
        P(),
        P(("seq", "own"), None),
        P(("seq", "own"), None),
        P(("seq", "own")),
        P("own", "seq"),
        P("own"),
    )
    return jax.shard_map(
        on_device,
        mesh=mesh,
        in_specs=placed,
        out_specs=(P(), P(), P(), P(("seq", "own"), None)),
        check_vma=False,
    )
```

```python
import functools

import jax
import jax.numpy as jnp
from jax import lax
from jax.experimental import pallas as pl
from jax.experimental.pallas import tpu as pltpu
from jax.sharding import PartitionSpec as P

F32 = jnp.float32
BF16 = jnp.bfloat16
MESH = pl.DeviceIdType.MESH
SCALE = 128 ** (-0.5)
AG_ORDERS = (("z", "x", "y"), ("x", "y", "z"), ("y", "z", "x"))
HEAD = 2
HW = 512 // HEAD
CHUNKS = 2
CW = 512 // CHUNKS
HALF = 256 // CHUNKS


def mm(a, b):
    return jnp.dot(a, b, preferred_element_type=F32)


def mm_nt(a, b):
    return lax.dot_general(a, b, (((1,), (1,)), ((), ())), preferred_element_type=F32)


def iota(shape, dim):
    return lax.broadcasted_iota(jnp.int32, shape, dim)


def onehot(hit):
    return hit.astype(F32).astype(BF16)


def hops(step):
    return sum(min(d, 4 - d) for d in step[:2])


STEPS = {
    4: [(2,), (1,), (3,)],
    16: sorted(((dx, dz) for dx in range(4) for dz in range(4) if dx or dz), key=hops, reverse=True),
    8: [(2, 0), (2, 1), (1, 0), (1, 1), (3, 0), (3, 1), (0, 1)],
}


def away(n, me, step):
    if n == 4:
        return lax.rem(me + step[0], 4)
    if n == 16:
        return lax.rem(me // 4 + step[0], 4) * 4 + lax.rem(lax.rem(me, 4) + step[1], 4)
    return lax.rem(me // 2 + step[0], 4) * 2 + lax.rem(lax.rem(me, 2) + step[1], 2)


class Exchange:
    def __init__(self, n, me, device, src, dst, send_sem, recv_sem):
        self.n, self.me, self.device, self.src, self.dst = n, me, device, src, dst
        self.send_sem, self.recv_sem = send_sem, recv_sem

    def _out(self, p):
        return pltpu.make_async_remote_copy(
            src_ref=self.src(p),
            dst_ref=self.dst(self.me),
            send_sem=self.send_sem.at[p],
            recv_sem=self.recv_sem.at[self.me],
            device_id=self.device(p),
            device_id_type=MESH,
        )

    def _in(self, p):
        return pltpu.make_async_remote_copy(
            src_ref=self.src(p),
            dst_ref=self.dst(p),
            send_sem=self.send_sem.at[p],
            recv_sem=self.recv_sem.at[p],
            device_id=self.device(p),
            device_id_type=MESH,
        )

    def peers(self):
        return [away(self.n, self.me, step) for step in STEPS[self.n]]

    def _each(self, f, near_first=False):
        peers = self.peers()
        for p in peers[::-1] if near_first else peers:
            f(p)

    def start(self, pending):
        pending.append(self.wait_send)
        self._each(lambda p: self._out(p).start())

    def start_to(self, p, pending):
        pending.append(lambda: self._out(p).wait_send())
        self._out(p).start()

    def wait_from(self, p):
        self._in(p).wait_recv()

    def wait_recv(self):
        self._each(lambda p: self._in(p).wait_recv(), near_first=True)

    def wait_send(self):
        self._each(lambda p: self._out(p).wait_send())


def main_kernel(
    idst_ref, counts_ref, ev_ref, len_ref, dout_any, wout_any, hot_any, table_any, win_ref,
    ag0, ag1, ag2, ret, asked,
    id_pad, id_loc, id_a, id_b, ev_loc, ev_all, code_col, valid_col,
    got, rows, perm, fetched, e_loc, e_all, c_all,
    wh, wht, wh_sem, slope_pre, u_t, q_t, k_t, v_t, q_n, k_n, v_n,
    w_st, sl_st, att, gg, gat, ga_t, ga_n, gq, gk, gv, g_t, stat,
    sib_s, sib_r, tot, g_r, grad, w1_send, w1_recv, w2_send, w2_recv, wu_s, wu_r, hu_s, hu_r,
    s_send, q_recv, p_send, dout_ref, wout_ref, hot_ref, table_ref, load_sem,
    sem16, sem8, sem4, sem_ag, sem_sib,
):
    s, o = lax.axis_index("seq"), lax.axis_index("own")
    y, c = s // 2, lax.rem(s, 2)
    u, h = s // 4, lax.rem(s, 4)
    x, z = o // 4, lax.rem(o, 4)
    sib = (2 * y + 1 - c, o)
    ags = (ag0, ag1, ag2)
    chunks = range(CHUNKS)
    heads = range(HEAD)
    pending = []

    barrier = pltpu.get_barrier_semaphore()

    for step in STEPS[16]:
        pl.semaphore_signal(barrier, inc=1, device_id=(s, away(16, o, step)), device_id_type=MESH)
    for step in STEPS[8]:
        pl.semaphore_signal(barrier, inc=1, device_id=(away(8, s, step), o), device_id_type=MESH)

    def load_w(b):
        return pltpu.make_async_copy(
            win_ref.at[:, pl.ds(pl.multiple_of(b * 512 + h * 128, 128), 128)],
            wh.at[:, pl.ds(b * 128, 128)],
            wh_sem.at[b],
        )

    loads = [
        pltpu.make_async_copy(a, b, load_sem.at[i])
        for i, (a, b) in enumerate(
            ((table_any, table_ref), (dout_any, dout_ref), (hot_any, hot_ref), (wout_any, wout_ref))
        )
    ]
    for copy in loads:
        copy.start()
    for b in range(4):
        load_w(b).start()

    def own_x(i, src, dst):
        return Exchange(16, o, lambda p: (s, p), src, dst, sem16.at[i, 0], sem16.at[i, 1])

    def seq_x(i, src, dst):
        return Exchange(8, s, lambda p: (p, o), src, dst, sem8.at[i, 0], sem8.at[i, 1])

    def y_x(i, src, dst):
        return Exchange(4, y, lambda p: (2 * p + c, o), src, dst, sem4.at[i, 0], sem4.at[i, 1])

    def head_x(i, src, dst):
        return Exchange(4, h, lambda p: (4 * u + p, o), src, dst, sem4.at[i, 0], sem4.at[i, 1])

    def to_sib(src, dst, i, j):
        return pltpu.make_async_remote_copy(
            src_ref=src, dst_ref=dst, send_sem=sem_sib.at[i, 0, j], recv_sem=sem_sib.at[i, 1, j],
            device_id=sib, device_id_type=MESH,
        )

    def start_sib(copy):
        pending.append(copy.wait_send)
        copy.start()

    ids_x1 = own_x(0, lambda p: id_loc.at[:, p], lambda p: id_a.at[p])
    ids_x2 = seq_x(0, lambda p: id_a.at[:, p], lambda p: id_b.at[p])
    ev_x = seq_x(1, lambda p: ev_loc.at[p // 4], lambda p: ev_all.at[p])
    rows_x1 = [seq_x(2 + k, lambda p, k=k: got.at[k, :, p], lambda p, k=k: rows.at[k, p]) for k in heads]
    ret_x2 = [
        seq_x(2 + HEAD + k, lambda p, k=k: p_send.at[k, p], lambda p, k=k: ret.at[k, :, p]) for k in chunks
    ]
    w1_x = own_x(1, lambda p: w1_send.at[p], lambda p: w1_recv.at[p])
    w2_x = own_x(2, lambda p: w2_send.at[p], lambda p: w2_recv.at[p])
    rows_x2 = [own_x(3 + k, lambda p, k=k: perm.at[k, p], lambda p, k=k: fetched.at[k, p]) for k in heads]
    ret_x1 = [
        own_x(3 + HEAD + k, lambda p, k=k: s_send.at[k, p], lambda p, k=k: q_recv.at[k, p]) for k in chunks
    ]
    cot_x = y_x(0, lambda p: dout_ref.at[p // 2], lambda p: c_all.at[2 * p + c])
    stat_x = head_x(1, lambda p: stat.at[h], lambda p: stat.at[p])
    emb_x = [
        y_x(2 + k, lambda p, k=k: e_loc.at[k, p // 2], lambda p, k=k: e_all.at[k, 2 * p + c]) for k in heads
    ]
    hot_x = y_x(2 + HEAD, lambda p: hu_s.at[p], lambda p: hu_r.at[p])

    def positions(k, p):
        return tot.at[k, :, pl.ds(pl.multiple_of(p * 256, 256), 256)]

    grad_x = [
        seq_x(2 + HEAD + CHUNKS + k, lambda p, k=k: positions(k, p), lambda p, k=k: g_r.at[k, p]) for k in chunks
    ]

    def sib_block(buf, i, yy):
        return to_sib(buf.at[2 * yy + c], buf.at[2 * yy + c], i, yy)

    def sib_block_in(buf, i, yy):
        return to_sib(buf.at[2 * yy + 1 - c], buf.at[2 * yy + 1 - c], i, yy)

    id_pad[...] = jnp.zeros_like(id_pad)
    id_pad[0:4, :] = idst_ref[...]
    id_loc[...] = id_pad[...].T.reshape(8, 16, 128)

    pl.semaphore_wait(barrier, 22)

    ids_x1.start(pending)
    id_a[o] = id_loc[:, o, :]

    codes = []
    for uu in range(2):
        e = ev_ref[uu : uu + 1, :]
        cold = e - 512
        code = jnp.where(e < 512, e, 512 + ((cold >> 2) & 15) * 32 + (cold >> 6) * 4 + (cold & 3))
        ev_loc[uu] = jnp.broadcast_to(code, (8, 256))
        codes.append(code)
    code_row = jnp.concatenate(codes, axis=1)
    code_col[...] = jnp.broadcast_to(code_row, (128, 512)).T
    counts = counts_ref[...].astype(F32).astype(BF16)
    l = iota((128, 512), 1)
    pick = onehot(iota((128, 512), 0) == ((l >> 2) & 7) * 16 + (l >> 5))
    valid_row = (iota((8, 512), 1) & 3).astype(F32) < mm(jnp.broadcast_to(counts, (8, 128)), pick)
    valid_row = valid_row[0:1]
    l = iota((512, 128), 0)
    pick = onehot(iota((512, 128), 1) == ((l >> 2) & 7) * 16 + (l >> 5))
    valid_col[...] = (
        (l & 3).astype(F32) < mm_nt(pick, jnp.broadcast_to(counts, (128, 128)))
    ).astype(F32)
    for b in range(4):
        load_w(b).wait()
    wht[...] = wh[...].T
    for copy in loads:
        copy.wait()
    c_all[s] = dout_ref[u]

    ids_x1.wait_recv()
    ids_x2.start(pending)
    id_b[s] = id_a[:, s, :]
    ids_x2.wait_recv()

    asked_ids = id_b[...].reshape(128, 128)
    for i in range(4):
        hit = onehot(iota((128, 2048), 1) == asked_ids[:, i : i + 1])
        found = mm(hit, table_ref[...]).astype(BF16)
        for k in heads:
            got[k, i] = found[:, k * HW : (k + 1) * HW].reshape(8, 16, HW)
    for k in heads:
        rows_x1[k].start(pending)
        rows[k, s] = got[k, :, s]
    ev_x.start(pending)
    ev_all[s] = ev_loc[u]
    asked[...] = asked_ids.T[0:8, :]
    start_sib(sib_block(c_all, 0, y))
    hot_hits = [onehot(code_col[...] == iota((512, 128), 1) + b * 128) for b in range(4)]
    emb = mm(jnp.concatenate(hot_hits, axis=1), hot_ref[...])
    r = iota((512, 512), 0)
    pick = onehot(iota((512, 512), 1) == (r & 31) * 16 + (r >> 5))
    for k in heads:
        rows_x1[k].wait_recv()
        perm[k] = mm(pick, rows[k].reshape(512, HW)).astype(BF16).reshape(16, 32, HW)
        rows_x2[k].start(pending)
        fetched[k, o] = perm[k, o]
    for d in (1, 3):
        cot_x.start_to(lax.rem(y + d, 4), pending)
    cold_hits = [
        onehot(jnp.logical_and(
            code_col[...] == iota((512, 128), 1) + (512 + b * 128), valid_row[:, b * 128 : (b + 1) * 128]
        ))
        for b in range(4)
    ]
    cold_hits = jnp.concatenate(cold_hits, axis=1)
    for k in heads:
        rows_x2[k].wait_recv()
        part = emb[:, k * HW : (k + 1) * HW] + mm(cold_hits, fetched[k].reshape(512, HW))
        e_loc[k] = part.astype(BF16).reshape(2, 256, HW)
        emb_x[k].start(pending)
        e_all[k, s] = e_loc[k, u]
        start_sib(sib_block(e_all.at[k], 2 + k, y))

    def project(blk):
        cols = pl.ds(pl.multiple_of(blk * 256, 256), 256)
        pre = mm_nt(wht[...], jnp.concatenate([e_all[k, blk] for k in heads], axis=1))
        sig = 0.5 + 0.5 * jnp.tanh(0.5 * pre)
        act = pre * sig
        slope_pre[:, cols] = sig + act * (1.0 - sig)
        act = act.astype(BF16)
        u_t[:, cols] = act[0:128]
        q_t[:, cols] = act[128:256]
        k_t[:, cols] = act[256:384]
        keep = (blk * 256 + iota((1, 256), 1) < len_ref[u]).astype(F32)
        val = (act[384:512].astype(F32) * keep).astype(BF16)
        v_t[:, cols] = val
        q_n[cols, :] = act[128:256].T
        k_n[cols, :] = act[256:384].T
        v_n[cols, :] = val.T

    for d in (1, 3):
        cot_x.wait_from(lax.rem(y + d, 4))
        start_sib(sib_block(c_all, 0, lax.rem(y + d, 4)))
    project(s)
    for k in heads:
        for d in (1, 3, 2):
            yy = lax.rem(y + d, 4)
            emb_x[k].wait_from(yy)
            start_sib(sib_block(e_all.at[k], 2 + k, yy))
            if k == HEAD - 1:
                project(2 * yy + c)
    cot_x.start_to(lax.rem(y + 2, 4), pending)
    for d in (0, 1, 3, 2):
        yy = lax.rem(y + d, 4)
        for k in heads:
            sib_block_in(e_all.at[k], 2 + k, yy).wait_recv()
        project(2 * yy + 1 - c)

    att[...] = jnp.zeros_like(att)

    def forward(i, j, diag):
        keys = pl.multiple_of(j * 512, 512)
        qs = pl.ds(pl.multiple_of(i * 512, 512), 512)
        at = i * (i + 1) // 2 + j
        for m in range(4):
            half = mm(k_n[pl.ds(keys + m * 128, 128), :], q_t[:, qs]) * (0.5 * SCALE)
            t = jnp.tanh(half)
            a = 1.0 + t
            w = half * a
            slope = a + w * (2.0 - a)
            if diag:
                ok = iota((128, 512), 0) + m * 128 <= iota((128, 512), 1)
                w = jnp.where(ok, w, 0.0)
                slope = jnp.where(ok, slope, 0.0)
            w_st[at, m * 128 : (m + 1) * 128, :] = w.astype(BF16)
            sl_st[at, m * 128 : (m + 1) * 128, :] = slope.astype(BF16)
        att[:, qs] += mm(v_t[:, pl.ds(keys, 512)], w_st[at])

    @pl.loop(0, 4)
    def _(i):
        @pl.loop(0, i)
        def _(j):
            forward(i, j, False)

        forward(i, i, True)

    cot_x.wait_from(lax.rem(y + 2, 4))
    start_sib(sib_block(c_all, 0, lax.rem(y + 2, 4)))
    for d in range(4):
        sib_block_in(c_all, 0, lax.rem(y + d, 4)).wait_recv()
    live = (iota((1, 2048), 1) < len_ref[u]).astype(F32)
    wo = wout_ref[pl.ds(pl.multiple_of(h * 128, 128), 128), :]
    gg[...] = mm_nt(wo, c_all[...].reshape(2048, 512)) * live
    inv = 1.0 / jnp.full((1, 2048), len_ref[u], jnp.int32).astype(F32)
    mine = att[...] * inv
    m1 = jnp.sum(mine, axis=0, keepdims=True) * (1.0 / 128)
    dev = mine - m1
    gn = gg[...] * u_t[...].astype(F32)
    stat[h, 0:1, :] = m1
    stat[h, 1:2, :] = jnp.sum(dev * dev, axis=0, keepdims=True)
    stat[h, 2:3, :] = jnp.sum(gn, axis=0, keepdims=True)
    stat[h, 3:4, :] = jnp.sum(gn * dev, axis=0, keepdims=True)
    stat_x.start(pending)
    stat_x.wait_recv()
    both = stat[...]
    mean = jnp.sum(both[:, 0, :], axis=0, keepdims=True) * 0.25
    off = both[:, 0, :] - mean
    var = (jnp.sum(both[:, 1, :], axis=0, keepdims=True) + 128.0 * jnp.sum(off * off, axis=0, keepdims=True)) * (
        1.0 / 512
    )
    rstd = lax.rsqrt(var + 1e-05)
    mean1 = jnp.sum(both[:, 2, :], axis=0, keepdims=True) * (1.0 / 512)
    mean2 = jnp.sum(both[:, 3, :] + off * both[:, 2, :], axis=0, keepdims=True) * (rstd * (1.0 / 512))
    normed = (att[...] * inv - mean) * rstd
    att[...] = normed
    gn = gg[...] * u_t[...].astype(F32)
    ga_t[...] = ((gn - mean1 - normed * mean2) * (rstd * inv)).astype(BF16)
    for b in range(8):
        ga_n[b * 256 : (b + 1) * 256, :] = ga_t[:, b * 256 : (b + 1) * 256].T

    def to_rows(rows_by_cols):
        n = rows_by_cols.shape[1]
        return rows_by_cols.astype(BF16).reshape(-1, 32, n)

    gat[...] = (att[...] * u_t[...].astype(F32) * live).astype(BF16)
    gw_out = mm(gat[...], c_all[...].reshape(2048, 512))
    for b in range(4):
        w1_send[4 * b : 4 * b + 4, :, 0:128] = to_rows(gw_out[:, b * 128 : (b + 1) * 128])
    g_t[0:128, :] = (gg[...] * att[...] * slope_pre[0:128, :]).astype(BF16)
    n = HW // 32
    for k in heads:
        w1_send[k * n : (k + 1) * n, :, 128:256] = to_rows(mm(g_t[0:128, :], e_all[k].reshape(2048, HW)).T)
    w1_x.start(pending)
    w1_recv[o] = w1_send[o]

    gq[...] = jnp.zeros_like(gq)
    gk[...] = jnp.zeros_like(gk)
    gv[...] = jnp.zeros_like(gv)

    def backward(i, j):
        keys = pl.multiple_of(j * 512, 512)
        qs = pl.ds(pl.multiple_of(i * 512, 512), 512)
        at = i * (i + 1) // 2 + j
        for m in range(4):
            gw = mm(v_n[pl.ds(keys + m * 128, 128), :], ga_t[:, qs])
            ds = gw * sl_st[at, m * 128 : (m + 1) * 128, :].astype(F32)
            sl_st[at, m * 128 : (m + 1) * 128, :] = ds.astype(BF16)
        gk[pl.ds(keys, 512), :] += mm(sl_st[at], q_n[qs, :])
        gv[pl.ds(keys, 512), :] += mm(w_st[at], ga_n[qs, :])
        gq[:, qs] += mm(k_t[:, pl.ds(keys, 512)], sl_st[at])

    @pl.loop(0, 4)
    def _(i):
        @pl.loop(0, i + 1)
        def _(j):
            backward(i, j)

    keep = (iota((1, 2048), 1) < len_ref[u]).astype(F32)
    g_t[128:256, :] = (gq[...] * (0.5 * SCALE) * slope_pre[128:256, :]).astype(BF16)
    for b in range(8):
        cols = slice(b * 256, (b + 1) * 256)
        g_t[256:384, cols] = (gk[cols, :].T * (0.5 * SCALE) * slope_pre[256:384, cols]).astype(BF16)
        g_t[384:512, cols] = (gv[cols, :].T * keep[:, cols] * slope_pre[384:512, cols]).astype(BF16)

    def partial(k, half):
        return mm(wh[pl.ds(pl.multiple_of(half * 256 + k * HALF, HALF), HALF), :], g_t[...])

    def sib_grad(k):
        return to_sib(sib_s.at[k], sib_r.at[k], 2 + HEAD, k)

    for k in chunks:
        sib_s[k] = partial(k, 1 - c).astype(BF16)
        start_sib(sib_grad(k))
    for k in chunks:
        total = partial(k, c)
        sib_grad(k).wait_recv()
        tot[k] = (total + sib_r[k].astype(F32)).astype(BF16)
        grad_x[k].start(pending)
        g_r[k, s] = positions(k, s)[...]

    for k in heads:
        w2_send[k * n : (k + 1) * n, :, 0:384] = to_rows(mm(g_t[128:512, :], e_all[k].reshape(2048, HW)).T)
    ev_x.wait_recv()
    sums = jnp.zeros((512, 256), F32)
    for blk in range(8):
        hit = onehot(iota((512, 256), 0) == ev_all[blk, 0:1, :])
        sums += mm_nt(hit, jnp.concatenate([tot[k, :, blk * 256 : (blk + 1) * 256] for k in chunks], axis=0))
    for b in range(4):
        blk = 4 * lax.rem(y, 2) + b
        hit = jnp.logical_and(
            iota((512, 256), 0) == ev_all[blk, 0:1, :], blk * 256 + iota((1, 256), 1) < len_ref[u]
        )
        sums += mm(onehot(hit), c_all[blk, :, pl.ds(pl.multiple_of(c * 256, 256), 256)])
    w2_send[:, :, 384:640] = to_rows(sums)
    w2_x.start(pending)
    w2_recv[o] = w2_send[o]

    cots = []
    for uu in range(2):
        here = (s * 256 + iota((256, 1), 0) < len_ref[uu]).astype(F32)
        cots.append((dout_ref[uu].astype(F32) * here).astype(BF16))
    cot = jnp.concatenate(cots, axis=0)
    hits = []
    for uu in range(2):
        hit = iota((512, 256), 0) + 512 == ev_loc[uu, 0:1, :]
        hits.append(onehot(jnp.logical_and(hit, jnp.concatenate([valid_col[...]] * 2, axis=1) > 0)))
    hits = jnp.concatenate(hits, axis=1)
    def first_hop(k):
        grad_x[k].wait_recv()
        here = []
        for half in range(2):
            rows_k = slice(half * HALF, (half + 1) * HALF)
            for uu in range(2):
                grad[rows_k, uu * 256 : (uu + 1) * 256] = (
                    g_r[k, 4 * uu + half].astype(F32) + g_r[k, 4 * uu + 2 + half].astype(F32)
                ).astype(BF16)
            here.append(cot[:, half * 256 + k * HALF : half * 256 + (k + 1) * HALF])
        sums = mm_nt(hits, grad[...]) + mm(hits, jnp.concatenate(here, axis=1))
        s_send[k] = to_rows(sums)
        ret_x1[k].start(pending)
        q_recv[k, o] = s_send[k, o]

    first_hop(0)

    w1_x.wait_recv()
    total1 = jnp.sum(w1_recv[...].astype(F32), axis=0)
    w2_x.wait_recv()
    total2 = jnp.sum(w2_recv[...].astype(F32), axis=0)
    total = jnp.concatenate([total1[:, 128:256], total2[:, 0:384], total1[:, 0:128]], axis=1)
    wu_s[...] = total.astype(BF16).reshape(2, 16, 640)
    for i in range(4):
        left = 384 + 128 * (i % 2)
        hu_s[i] = total2[16 * (i // 2) : 16 * (i // 2) + 16, left : left + 128].astype(BF16)
    wu = pltpu.make_async_remote_copy(
        src_ref=wu_s.at[1 - u],
        dst_ref=wu_r,
        send_sem=sem_sib.at[1, 0, 0],
        recv_sem=sem_sib.at[1, 1, 0],
        device_id=(lax.rem(s + 4, 8), o),
        device_id_type=MESH,
    )
    start_sib(wu)
    hot_x.start(pending)
    hu_r[y] = hu_s[y]
    for k in range(1, CHUNKS):
        first_hop(k)

    r = iota((512, 512), 0)
    pick = onehot(iota((512, 512), 1) == (r & 15) * 32 + (r >> 4))

    def second_hop(k):
        ret_x1[k].wait_recv()
        p_send[k] = mm(pick, q_recv[k].reshape(512, CW)).astype(BF16).reshape(8, 4, 16, CW)
        ret_x2[k].start(pending)
        ret[k, :, s] = p_send[k, s]

    place = {"y": y, "x": x, "z": z}
    device = {
        "y": lambda p: (2 * p + c, o),
        "x": lambda p: (s, 4 * p + z),
        "z": lambda p: (s, 4 * x + p),
    }

    def slab(i, core, known):
        at = dict(place)
        at.update(known)
        return ags[i].at[core, at["y"], at["x"], at["z"]]

    def gather_x(i, stage):
        order = AG_ORDERS[i]
        axis = order[stage]
        whole = {a: slice(None) for a in order[:stage]}
        block = lambda p: slab(i, c, {**whole, axis: p})
        return Exchange(
            4, place[axis], device[axis], lambda p: block(place[axis]), block,
            sem_ag.at[i, stage, 0], sem_ag.at[i, stage, 1],
        )

    def last_slab(i, core, p):
        order = AG_ORDERS[i]
        blk = slab(i, core, {order[0]: slice(None), order[1]: slice(None), order[2]: p})
        return to_sib(blk, blk, 3 + HEAD + i, p)

    gathers = [[gather_x(i, stage) for stage in range(3)] for i in range(3)]
    wu.wait_recv()
    pick_u = u.astype(F32)
    mine = total[0:16] * (1.0 - pick_u) + total[16:32] * pick_u + wu_r[...].astype(F32)
    mine = mine.astype(BF16)
    ag0[c, y, x, z] = mine[:, 0:256]
    ag1[c, y, x, z] = mine[:, 256:512]
    for i in range(2):
        gathers[i][0].start(pending)
    hot_x.wait_recv()
    ag2[c, y, x, z] = jnp.concatenate(
        [mine[:, 512:640], jnp.sum(hu_r[...].astype(F32), axis=0).astype(BF16)], axis=1
    )
    gathers[2][0].start(pending)
    second_hop(0)
    for stage in range(2):
        for i in range(3):
            gathers[i][stage].wait_recv()
            gathers[i][stage + 1].start(pending)
        if stage == 0:
            for k in range(1, CHUNKS):
                second_hop(k)
    for i in range(3):
        start_sib(last_slab(i, c, place[AG_ORDERS[i][2]]))
    for d in (1, 3, 2):
        for i in range(3):
            p = lax.rem(place[AG_ORDERS[i][2]] + d, 4)
            gathers[i][2].wait_from(p)
            start_sib(last_slab(i, c, p))
    for k in chunks:
        ret_x2[k].wait_recv()
    for i in range(3):
        for p in range(4):
            last_slab(i, 1 - c, p).wait_recv()

    for wait in pending:
        wait()


def finish_kernel(a0, a1, a2, ret, asked, gin, gout, ghot, gcold):
    g = pl.program_id(0)
    for yy in range(4):
        for core in range(2):
            user, head = yy // 2, (yy % 2) * 2 + core
            for zz in range(2):
                top = 32 * zz + 16 * user
                b0 = a0[core, yy, 0, zz].astype(F32)
                b1 = a1[core, yy, 0, zz].astype(F32)
                b2 = a2[core, yy, 0, zz].astype(F32)
                for b in range(4):
                    part = (b0, b1)[b // 2][:, (b % 2) * 128 : (b % 2) * 128 + 128]
                    gin[top : top + 16, b * 512 + head * 128 : b * 512 + head * 128 + 128] = part
                low = pl.multiple_of(head * 128 + 32 * (2 * lax.rem(g, 2) + zz) + 16 * user, 16)
                gout[pl.ds(low, 16), pl.ds(pl.multiple_of(g // 2 * 128, 128), 128)] = b2[:, 0:128]
                hot_top = 32 * zz + 16 * (yy // 2)
                left = 256 * core + 128 * (yy % 2)
                ghot[hot_top : hot_top + 16, left : left + 128] = b2[:, 128:256]
    hits = jnp.concatenate([onehot(iota((256, 128), 0) + g * 256 == asked[i : i + 1, :]) for i in range(4)], axis=1)
    for k in range(CHUNKS):
        sums = mm(hits, ret[k].reshape(512, CW))
        for half in range(2):
            left = half * 256 + k * HALF
            gcold[:, left : left + HALF] = sums[:, half * HALF : (half + 1) * HALF]


def on_device(
    d_out, weight_in, weight_out, hot_table, cold_table, cold_ids, cold_counts, event_slots, lengths
):
    vmem = pl.BlockSpec(memory_space=pltpu.VMEM)
    smem = pl.BlockSpec(memory_space=pltpu.SMEM)
    big = lambda *shape: pltpu.VMEM(shape, BF16)
    wide = lambda *shape: pltpu.VMEM(shape, F32)
    sems = pltpu.SemaphoreType.DMA
    outs = [pltpu.VMEM((2, 4, 4, 4, 16, 256), BF16)] * 3 + [
        pltpu.VMEM((CHUNKS, 4, 8, 16, CW), BF16),
        pltpu.VMEM((8, 128), jnp.int32),
    ]
    ints = lambda *shape: pltpu.VMEM(shape, jnp.int32)
    scratch = [
        ints(128, 128),
        ints(8, 16, 128),
        ints(16, 8, 128),
        ints(8, 16, 128),
        ints(2, 8, 256),
        ints(8, 8, 256),
        ints(512, 128),
        wide(512, 128),
        big(HEAD, 4, 8, 16, HW),
        big(HEAD, 8, 4, 16, HW),
        big(HEAD, 16, 32, HW),
        big(HEAD, 16, 32, HW),
        big(HEAD, 2, 256, HW),
        big(HEAD, 8, 256, HW),
        big(8, 256, 512),
        big(512, 512),
        big(512, 512),
        sems((4,)),
        wide(512, 2048),
        big(128, 2048),
        big(128, 2048),
        big(128, 2048),
        big(128, 2048),
        big(2048, 128),
        big(2048, 128),
        big(2048, 128),
        big(10, 512, 512),
        big(10, 512, 512),
        wide(128, 2048),
        wide(128, 2048),
        big(128, 2048),
        big(128, 2048),
        big(2048, 128),
        wide(128, 2048),
        wide(2048, 128),
        wide(2048, 128),
        big(512, 2048),
        wide(4, 4, 2048),
        big(CHUNKS, HALF, 2048),
        big(CHUNKS, HALF, 2048),
        big(CHUNKS, HALF, 2048),
        big(CHUNKS, 8, HALF, 256),
        big(CW, 512),
        big(16, 32, 256),
        big(16, 32, 256),
        big(16, 32, 640),
        big(16, 32, 640),
        big(2, 16, 640),
        big(16, 640),
        big(4, 16, 128),
        big(4, 16, 128),
        big(CHUNKS, 16, 32, CW),
        big(CHUNKS, 16, 32, CW),
        big(CHUNKS, 8, 4, 16, CW),
        big(2, 256, 512),
        big(512, 512),
        big(512, 512),
        big(2048, 512),
        sems((4,)),
        sems((3 + HEAD + CHUNKS, 2, 16)),
        sems((2 + HEAD + 2 * CHUNKS, 2, 8)),
        sems((3 + HEAD, 2, 4)),
        sems((3, 3, 2, 4)),
        sems((6 + HEAD, 2, 4)),
    ]
    a0, a1, a2, ret, asked = pl.pallas_call(
        main_kernel,
        out_shape=outs,
        in_specs=[vmem] * 3 + [smem] + [pl.BlockSpec(memory_space=pl.ANY)] * 5,
        out_specs=[vmem] * 5,
        scratch_shapes=scratch,
        compiler_params=pltpu.CompilerParams(
            collective_id=0, has_side_effects=True, vmem_limit_bytes=56 * 1024 * 1024
        ),
        name="layer",
    )(
        cold_ids.T, cold_counts.reshape(1, 128), event_slots, lengths,
        d_out, weight_out, hot_table, cold_table, weight_in,
    )

    part = pl.BlockSpec((2, 4, 1, 2, 16, 256), lambda g: (0, 0, g // 2, lax.rem(g, 2), 0, 0))
    return pl.pallas_call(
        finish_kernel,
        grid=(8,),
        out_shape=[
            jax.ShapeDtypeStruct((512, 2048), F32),
            jax.ShapeDtypeStruct((512, 512), F32),
            jax.ShapeDtypeStruct((512, 512), F32),
            jax.ShapeDtypeStruct((2048, 512), F32),
        ],
        in_specs=[part] * 3
        + [
            pl.BlockSpec((CHUNKS, 4, 8, 16, CW), lambda g: (0, 0, 0, 0, 0)),
            pl.BlockSpec((8, 128), lambda g: (0, 0)),
        ],
        out_specs=[
            pl.BlockSpec((64, 2048), lambda g: (g, 0)),
            pl.BlockSpec((512, 512), lambda g: (0, 0)),
            pl.BlockSpec((64, 512), lambda g: (g, 0)),
            pl.BlockSpec((256, 512), lambda g: (g, 0)),
        ],
        compiler_params=pltpu.CompilerParams(vmem_limit_bytes=24 * 1024 * 1024),
        name="finish",
    )(a0, a1, a2, ret, asked)


def solution(mesh):
    placed = (
        P("own", "seq", None),
        P(),
        P(),
        P(),
        P(("seq", "own"), None),
        P(("seq", "own"), None),
        P(("seq", "own")),
        P("own", "seq"),
        P("own"),
    )
    return jax.shard_map(
        on_device,
        mesh=mesh,
        in_specs=placed,
        out_specs=(P(), P(), P(), P(("seq", "own"), None)),
        check_vma=False,
    )
```

```python
import functools

import jax
import jax.numpy as jnp
from jax import lax
from jax.experimental import pallas as pl
from jax.experimental.pallas import tpu as pltpu
from jax.sharding import PartitionSpec as P

F32 = jnp.float32
BF16 = jnp.bfloat16
MESH = pl.DeviceIdType.MESH
SCALE = 128 ** (-0.5)
AG_ORDERS = (("z", "x", "y"), ("x", "y", "z"), ("y", "z", "x"))
HEAD = 2
HW = 512 // HEAD
CHUNKS = 2
CW = 512 // CHUNKS
HALF = 256 // CHUNKS


def mm(a, b):
    return jnp.dot(a, b, preferred_element_type=F32)


def mm_nt(a, b):
    return lax.dot_general(a, b, (((1,), (1,)), ((), ())), preferred_element_type=F32)


def iota(shape, dim):
    return lax.broadcasted_iota(jnp.int32, shape, dim)


def onehot(hit):
    return hit.astype(F32).astype(BF16)


def hops(step):
    return sum(min(d, 4 - d) for d in step[:2])


STEPS = {
    4: [(2,), (1,), (3,)],
    16: sorted(((dx, dz) for dx in range(4) for dz in range(4) if dx or dz), key=hops, reverse=True),
    8: [(2, 0), (2, 1), (1, 0), (1, 1), (3, 0), (3, 1), (0, 1)],
}


def away(n, me, step):
    if n == 4:
        return lax.rem(me + step[0], 4)
    if n == 16:
        return lax.rem(me // 4 + step[0], 4) * 4 + lax.rem(lax.rem(me, 4) + step[1], 4)
    return lax.rem(me // 2 + step[0], 4) * 2 + lax.rem(lax.rem(me, 2) + step[1], 2)


class Exchange:
    def __init__(self, n, me, device, src, dst, send_sem, recv_sem):
        self.n, self.me, self.device, self.src, self.dst = n, me, device, src, dst
        self.send_sem, self.recv_sem = send_sem, recv_sem

    def _out(self, p):
        return pltpu.make_async_remote_copy(
            src_ref=self.src(p),
            dst_ref=self.dst(self.me),
            send_sem=self.send_sem.at[p],
            recv_sem=self.recv_sem.at[self.me],
            device_id=self.device(p),
            device_id_type=MESH,
        )

    def _in(self, p):
        return pltpu.make_async_remote_copy(
            src_ref=self.src(p),
            dst_ref=self.dst(p),
            send_sem=self.send_sem.at[p],
            recv_sem=self.recv_sem.at[p],
            device_id=self.device(p),
            device_id_type=MESH,
        )

    def peers(self):
        return [away(self.n, self.me, step) for step in STEPS[self.n]]

    def _each(self, f, near_first=False):
        peers = self.peers()
        for p in peers[::-1] if near_first else peers:
            f(p)

    def start(self, pending):
        pending.append(self.wait_send)
        self._each(lambda p: self._out(p).start())

    def start_to(self, p, pending):
        pending.append(lambda: self._out(p).wait_send())
        self._out(p).start()

    def wait_from(self, p):
        self._in(p).wait_recv()

    def wait_recv(self):
        self._each(lambda p: self._in(p).wait_recv(), near_first=True)

    def wait_send(self):
        self._each(lambda p: self._out(p).wait_send())


def main_kernel(
    idst_ref, counts_ref, ev_ref, len_ref, dout_any, wout_any, hot_any, table_any, win_ref,
    ag0, ag1, ag2, ret, asked,
    id_pad, id_loc, id_a, id_b, ev_loc, ev_all, code_col, valid_col,
    got, rows, perm, fetched, e_loc, e_all, c_all,
    wh, wht, wh_sem, slope_pre, u_t, q_t, k_t, v_t, q_n, k_n, v_n,
    w_st, sl_st, att, gg, gat, ga_t, ga_n, gq, gk, gv, g_t, stat,
    hot_hit, hot_acc, sib_s, sib_r, tot, g_r, grad, w1_send, w1_recv, w2_send, w2_recv, wu_s, wu_r, hu_s, hu_r,
    s_send, q_recv, p_send, dout_ref, wout_ref, hot_ref, table_ref, load_sem,
    sem16, sem8, sem4, sem_ag, sem_sib,
):
    s, o = lax.axis_index("seq"), lax.axis_index("own")
    y, c = s // 2, lax.rem(s, 2)
    u, h = s // 4, lax.rem(s, 4)
    x, z = o // 4, lax.rem(o, 4)
    sib = (2 * y + 1 - c, o)
    ags = (ag0, ag1, ag2)
    chunks = range(CHUNKS)
    heads = range(HEAD)
    pending = []

    barrier = pltpu.get_barrier_semaphore()

    for step in STEPS[16]:
        pl.semaphore_signal(barrier, inc=1, device_id=(s, away(16, o, step)), device_id_type=MESH)
    for step in STEPS[8]:
        pl.semaphore_signal(barrier, inc=1, device_id=(away(8, s, step), o), device_id_type=MESH)

    def load_w(b):
        return pltpu.make_async_copy(
            win_ref.at[:, pl.ds(pl.multiple_of(b * 512 + h * 128, 128), 128)],
            wh.at[:, pl.ds(b * 128, 128)],
            wh_sem.at[b],
        )

    loads = [
        pltpu.make_async_copy(a, b, load_sem.at[i])
        for i, (a, b) in enumerate(
            ((dout_any, dout_ref), (table_any, table_ref), (hot_any, hot_ref), (wout_any, wout_ref))
        )
    ]
    for copy in loads:
        copy.start()
    for b in range(4):
        load_w(b).start()

    def own_x(i, src, dst):
        return Exchange(16, o, lambda p: (s, p), src, dst, sem16.at[i, 0], sem16.at[i, 1])

    def seq_x(i, src, dst):
        return Exchange(8, s, lambda p: (p, o), src, dst, sem8.at[i, 0], sem8.at[i, 1])

    def y_x(i, src, dst):
        return Exchange(4, y, lambda p: (2 * p + c, o), src, dst, sem4.at[i, 0], sem4.at[i, 1])

    def head_x(i, src, dst):
        return Exchange(4, h, lambda p: (4 * u + p, o), src, dst, sem4.at[i, 0], sem4.at[i, 1])

    def to_sib(src, dst, i, j):
        return pltpu.make_async_remote_copy(
            src_ref=src, dst_ref=dst, send_sem=sem_sib.at[i, 0, j], recv_sem=sem_sib.at[i, 1, j],
            device_id=sib, device_id_type=MESH,
        )

    def start_sib(copy):
        pending.append(copy.wait_send)
        copy.start()

    ids_x1 = own_x(0, lambda p: id_loc.at[:, p], lambda p: id_a.at[p])
    ids_x2 = seq_x(0, lambda p: id_a.at[:, p], lambda p: id_b.at[p])
    ev_x = seq_x(1, lambda p: ev_loc.at[p // 4], lambda p: ev_all.at[p])
    rows_x1 = [seq_x(2 + k, lambda p, k=k: got.at[k, :, p], lambda p, k=k: rows.at[k, p]) for k in heads]
    ret_x2 = [
        seq_x(2 + HEAD + k, lambda p, k=k: p_send.at[k, p], lambda p, k=k: ret.at[k, :, p]) for k in chunks
    ]
    w1_x = own_x(1, lambda p: w1_send.at[p], lambda p: w1_recv.at[p])
    w2_x = own_x(2, lambda p: w2_send.at[p], lambda p: w2_recv.at[p])
    rows_x2 = [own_x(3 + k, lambda p, k=k: perm.at[k, p], lambda p, k=k: fetched.at[k, p]) for k in heads]
    ret_x1 = [
        own_x(3 + HEAD + k, lambda p, k=k: s_send.at[k, p], lambda p, k=k: q_recv.at[k, p]) for k in chunks
    ]
    cot_x = y_x(0, lambda p: dout_ref.at[p // 2], lambda p: c_all.at[2 * p + c])
    stat_x = head_x(1, lambda p: stat.at[h], lambda p: stat.at[p])
    emb_x = [
        y_x(2 + k, lambda p, k=k: e_loc.at[k, p // 2], lambda p, k=k: e_all.at[k, 2 * p + c]) for k in heads
    ]
    hot_x = y_x(2 + HEAD, lambda p: hu_s.at[p], lambda p: hu_r.at[p])

    def positions(k, p):
        return tot.at[k, :, pl.ds(pl.multiple_of(p * 256, 256), 256)]

    grad_x = [
        seq_x(2 + HEAD + CHUNKS + k, lambda p, k=k: positions(k, p), lambda p, k=k: g_r.at[k, p]) for k in chunks
    ]

    def sib_block(buf, i, yy):
        return to_sib(buf.at[2 * yy + c], buf.at[2 * yy + c], i, yy)

    def sib_block_in(buf, i, yy):
        return to_sib(buf.at[2 * yy + 1 - c], buf.at[2 * yy + 1 - c], i, yy)

    id_pad[...] = jnp.zeros_like(id_pad)
    id_pad[0:4, :] = idst_ref[...]
    id_loc[...] = id_pad[...].T.reshape(8, 16, 128)

    pl.semaphore_wait(barrier, 22)

    ids_x1.start(pending)
    id_a[o] = id_loc[:, o, :]
    loads[0].wait()
    cot_x.start_to(lax.rem(y + 2, 4), pending)

    codes = []
    for uu in range(2):
        e = ev_ref[uu : uu + 1, :]
        cold = e - 512
        code = jnp.where(e < 512, e, 512 + ((cold >> 2) & 15) * 32 + (cold >> 6) * 4 + (cold & 3))
        ev_loc[uu] = jnp.broadcast_to(code, (8, 256))
        codes.append(code)
    code_row = jnp.concatenate(codes, axis=1)
    code_col[...] = jnp.broadcast_to(code_row, (128, 512)).T
    counts = counts_ref[...].astype(F32).astype(BF16)
    l = iota((128, 512), 1)
    pick = onehot(iota((128, 512), 0) == ((l >> 2) & 7) * 16 + (l >> 5))
    valid_row = (iota((8, 512), 1) & 3).astype(F32) < mm(jnp.broadcast_to(counts, (8, 128)), pick)
    valid_row = valid_row[0:1]
    l = iota((512, 128), 0)
    pick = onehot(iota((512, 128), 1) == ((l >> 2) & 7) * 16 + (l >> 5))
    valid_col[...] = (
        (l & 3).astype(F32) < mm_nt(pick, jnp.broadcast_to(counts, (128, 128)))
    ).astype(F32)
    for b in range(4):
        load_w(b).wait()
    wht[...] = wh[...].T
    for copy in loads[1:]:
        copy.wait()
    c_all[s] = dout_ref[u]

    ids_x1.wait_recv()
    ids_x2.start(pending)
    id_b[s] = id_a[:, s, :]
    ids_x2.wait_recv()

    asked_ids = id_b[...].reshape(128, 128)
    for i in range(4):
        hit = onehot(iota((128, 2048), 1) == asked_ids[:, i : i + 1])
        found = mm(hit, table_ref[...]).astype(BF16)
        for k in heads:
            got[k, i] = found[:, k * HW : (k + 1) * HW].reshape(8, 16, HW)
    for k in heads:
        rows_x1[k].start(pending)
        rows[k, s] = got[k, :, s]
    ev_x.start(pending)
    ev_all[s] = ev_loc[u]
    asked[...] = asked_ids.T[0:8, :]
    start_sib(sib_block(c_all, 0, y))
    hot_hits = [onehot(code_col[...] == iota((512, 128), 1) + b * 128) for b in range(4)]
    emb = mm(jnp.concatenate(hot_hits, axis=1), hot_ref[...])
    r = iota((512, 512), 0)
    pick = onehot(iota((512, 512), 1) == (r & 31) * 16 + (r >> 5))
    for k in heads:
        rows_x1[k].wait_recv()
        perm[k] = mm(pick, rows[k].reshape(512, HW)).astype(BF16).reshape(16, 32, HW)
        rows_x2[k].start(pending)
        fetched[k, o] = perm[k, o]
    for d in (1, 3):
        cot_x.start_to(lax.rem(y + d, 4), pending)
    cot_x.wait_from(lax.rem(y + 2, 4))
    start_sib(sib_block(c_all, 0, lax.rem(y + 2, 4)))
    cold_hits = [
        onehot(jnp.logical_and(
            code_col[...] == iota((512, 128), 1) + (512 + b * 128), valid_row[:, b * 128 : (b + 1) * 128]
        ))
        for b in range(4)
    ]
    cold_hits = jnp.concatenate(cold_hits, axis=1)
    for k in heads:
        rows_x2[k].wait_recv()
        part = emb[:, k * HW : (k + 1) * HW] + mm(cold_hits, fetched[k].reshape(512, HW))
        e_loc[k] = part.astype(BF16).reshape(2, 256, HW)
        emb_x[k].start(pending)
        e_all[k, s] = e_loc[k, u]
        start_sib(sib_block(e_all.at[k], 2 + k, y))

    def project(blk):
        cols = pl.ds(pl.multiple_of(blk * 256, 256), 256)
        pre = mm_nt(wht[...], jnp.concatenate([e_all[k, blk] for k in heads], axis=1))
        sig = 0.5 + 0.5 * jnp.tanh(0.5 * pre)
        act = pre * sig
        slope_pre[:, cols] = sig + act * (1.0 - sig)
        act = act.astype(BF16)
        u_t[:, cols] = act[0:128]
        q_t[:, cols] = act[128:256]
        k_t[:, cols] = act[256:384]
        keep = (blk * 256 + iota((1, 256), 1) < len_ref[u]).astype(F32)
        val = (act[384:512].astype(F32) * keep).astype(BF16)
        v_t[:, cols] = val
        q_n[cols, :] = act[128:256].T
        k_n[cols, :] = act[256:384].T
        v_n[cols, :] = val.T

    for d in (1, 3):
        cot_x.wait_from(lax.rem(y + d, 4))
        start_sib(sib_block(c_all, 0, lax.rem(y + d, 4)))
    def arrive(k, d):
        yy = lax.rem(y + d, 4)
        emb_x[k].wait_from(yy)
        start_sib(sib_block(e_all.at[k], 2 + k, yy))

    def project_sib(d):
        yy = lax.rem(y + d, 4)
        for k in heads:
            sib_block_in(e_all.at[k], 2 + k, yy).wait_recv()
        project(2 * yy + 1 - c)

    live = (iota((1, 2048), 1) < len_ref[u]).astype(F32)

    def gate_grad(blk):
        cols = pl.ds(pl.multiple_of(blk * 256, 256), 256)
        here = (blk * 256 + iota((1, 256), 1) < len_ref[u]).astype(F32)
        wo = wout_ref[pl.ds(pl.multiple_of(h * 128, 128), 128), :]
        gg[:, cols] = mm_nt(wo, c_all[blk]) * here

    project(s)
    for k in range(HEAD - 1):
        for d in (1, 3, 2):
            arrive(k, d)
    for d in (0, 2, 1, 3):
        yy = lax.rem(y + d, 4)
        sib_block_in(c_all, 0, yy).wait_recv()
        gate_grad(2 * yy + c)
        gate_grad(2 * yy + 1 - c)
    for d in (1, 3):
        arrive(HEAD - 1, d)
        project(2 * lax.rem(y + d, 4) + c)
    for d in (0, 1, 3):
        project_sib(d)
    arrive(HEAD - 1, 2)
    project(2 * lax.rem(y + 2, 4) + c)
    project_sib(2)

    att[...] = jnp.zeros_like(att)

    def forward(i, j, diag):
        keys = pl.multiple_of(j * 512, 512)
        qs = pl.ds(pl.multiple_of(i * 512, 512), 512)
        at = i * (i + 1) // 2 + j
        for m in range(4):
            half = mm(k_n[pl.ds(keys + m * 128, 128), :], q_t[:, qs]) * (0.5 * SCALE)
            t = jnp.tanh(half)
            a = 1.0 + t
            w = half * a
            slope = a + w * (2.0 - a)
            if diag:
                ok = iota((128, 512), 0) + m * 128 <= iota((128, 512), 1)
                w = jnp.where(ok, w, 0.0)
                slope = jnp.where(ok, slope, 0.0)
            w_st[at, m * 128 : (m + 1) * 128, :] = w.astype(BF16)
            sl_st[at, m * 128 : (m + 1) * 128, :] = slope.astype(BF16)
        att[:, qs] += mm(v_t[:, pl.ds(keys, 512)], w_st[at])

    @pl.loop(0, 4)
    def _(i):
        @pl.loop(0, i)
        def _(j):
            forward(i, j, False)

        forward(i, i, True)

    inv = 1.0 / jnp.full((1, 2048), len_ref[u], jnp.int32).astype(F32)
    mine = att[...] * inv
    m1 = jnp.sum(mine, axis=0, keepdims=True) * (1.0 / 128)
    dev = mine - m1
    gn = gg[...] * u_t[...].astype(F32)
    stat[h, 0:1, :] = m1
    stat[h, 1:2, :] = jnp.sum(dev * dev, axis=0, keepdims=True)
    stat[h, 2:3, :] = jnp.sum(gn, axis=0, keepdims=True)
    stat[h, 3:4, :] = jnp.sum(gn * dev, axis=0, keepdims=True)
    stat_x.start(pending)
    ev_x.wait_recv()
    for blk in range(8):
        hot_hit[:, blk * 256 : (blk + 1) * 256] = onehot(iota((512, 256), 0) == ev_all[blk, 0:1, :])
    part = pl.ds(pl.multiple_of(c * 256, 256), 256)
    sums = jnp.zeros((512, 256), F32)
    for b in range(4):
        blk = 4 * lax.rem(y, 2) + b
        here = (blk * 256 + iota((256, 1), 0) < len_ref[u]).astype(F32)
        kept = (c_all[blk, :, part].astype(F32) * here).astype(BF16)
        sums += mm(hot_hit[:, pl.ds(pl.multiple_of(blk * 256, 256), 256)], kept)
    hot_acc[...] = sums
    stat_x.wait_recv()
    both = stat[...]
    mean = jnp.sum(both[:, 0, :], axis=0, keepdims=True) * 0.25
    off = both[:, 0, :] - mean
    var = (jnp.sum(both[:, 1, :], axis=0, keepdims=True) + 128.0 * jnp.sum(off * off, axis=0, keepdims=True)) * (
        1.0 / 512
    )
    rstd = lax.rsqrt(var + 1e-05)
    mean1 = jnp.sum(both[:, 2, :], axis=0, keepdims=True) * (1.0 / 512)
    mean2 = jnp.sum(both[:, 3, :] + off * both[:, 2, :], axis=0, keepdims=True) * (rstd * (1.0 / 512))
    normed = (att[...] * inv - mean) * rstd
    att[...] = normed
    gn = gg[...] * u_t[...].astype(F32)
    ga_t[...] = ((gn - mean1 - normed * mean2) * (rstd * inv)).astype(BF16)
    for b in range(8):
        ga_n[b * 256 : (b + 1) * 256, :] = ga_t[:, b * 256 : (b + 1) * 256].T

    def to_rows(rows_by_cols):
        n = rows_by_cols.shape[1]
        return rows_by_cols.astype(BF16).reshape(-1, 32, n)

    gat[...] = (att[...] * u_t[...].astype(F32) * live).astype(BF16)
    gw_out = mm(gat[...], c_all[...].reshape(2048, 512))
    for b in range(4):
        w1_send[4 * b : 4 * b + 4, :, 0:128] = to_rows(gw_out[:, b * 128 : (b + 1) * 128])
    g_t[0:128, :] = (gg[...] * att[...] * slope_pre[0:128, :]).astype(BF16)
    n = HW // 32
    for k in heads:
        w1_send[k * n : (k + 1) * n, :, 128:256] = to_rows(mm(g_t[0:128, :], e_all[k].reshape(2048, HW)).T)
    w1_x.start(pending)
    w1_recv[o] = w1_send[o]

    gq[...] = jnp.zeros_like(gq)
    gk[...] = jnp.zeros_like(gk)
    gv[...] = jnp.zeros_like(gv)

    def backward(i, j):
        keys = pl.multiple_of(j * 512, 512)
        qs = pl.ds(pl.multiple_of(i * 512, 512), 512)
        at = i * (i + 1) // 2 + j
        for m in range(4):
            gw = mm(v_n[pl.ds(keys + m * 128, 128), :], ga_t[:, qs])
            ds = gw * sl_st[at, m * 128 : (m + 1) * 128, :].astype(F32)
            sl_st[at, m * 128 : (m + 1) * 128, :] = ds.astype(BF16)
        gk[pl.ds(keys, 512), :] += mm(sl_st[at], q_n[qs, :])
        gv[pl.ds(keys, 512), :] += mm(w_st[at], ga_n[qs, :])
        gq[:, qs] += mm(k_t[:, pl.ds(keys, 512)], sl_st[at])

    @pl.loop(0, 4)
    def _(i):
        @pl.loop(0, i + 1)
        def _(j):
            backward(i, j)

    keep = (iota((1, 2048), 1) < len_ref[u]).astype(F32)
    g_t[128:256, :] = (gq[...] * (0.5 * SCALE) * slope_pre[128:256, :]).astype(BF16)
    for b in range(8):
        cols = slice(b * 256, (b + 1) * 256)
        g_t[256:384, cols] = (gk[cols, :].T * (0.5 * SCALE) * slope_pre[256:384, cols]).astype(BF16)
        g_t[384:512, cols] = (gv[cols, :].T * keep[:, cols] * slope_pre[384:512, cols]).astype(BF16)

    def partial(k, half):
        return mm(wh[pl.ds(pl.multiple_of(half * 256 + k * HALF, HALF), HALF), :], g_t[...])

    def sib_grad(k):
        return to_sib(sib_s.at[k], sib_r.at[k], 2 + HEAD, k)

    for k in chunks:
        sib_s[k] = partial(k, 1 - c).astype(BF16)
        start_sib(sib_grad(k))
    for k in heads:
        w2_send[k * n : (k + 1) * n, :, 0:384] = to_rows(mm(g_t[128:512, :], e_all[k].reshape(2048, HW)).T)
    for k in chunks:
        total = partial(k, c)
        sib_grad(k).wait_recv()
        tot[k] = (total + sib_r[k].astype(F32)).astype(BF16)
        grad_x[k].start(pending)
        g_r[k, s] = positions(k, s)[...]

    sums = hot_acc[...] + mm_nt(hot_hit[...], tot[...].reshape(256, 2048))
    w2_send[:, :, 384:640] = to_rows(sums)
    w2_x.start(pending)
    w2_recv[o] = w2_send[o]

    cots = []
    for uu in range(2):
        here = (s * 256 + iota((256, 1), 0) < len_ref[uu]).astype(F32)
        cots.append((dout_ref[uu].astype(F32) * here).astype(BF16))
    cot = jnp.concatenate(cots, axis=0)
    hits = []
    for uu in range(2):
        hit = iota((512, 256), 0) + 512 == ev_loc[uu, 0:1, :]
        hits.append(onehot(jnp.logical_and(hit, jnp.concatenate([valid_col[...]] * 2, axis=1) > 0)))
    hits = jnp.concatenate(hits, axis=1)
    def first_hop(k):
        grad_x[k].wait_recv()
        here = []
        for half in range(2):
            rows_k = slice(half * HALF, (half + 1) * HALF)
            for uu in range(2):
                grad[rows_k, uu * 256 : (uu + 1) * 256] = (
                    g_r[k, 4 * uu + half].astype(F32) + g_r[k, 4 * uu + 2 + half].astype(F32)
                ).astype(BF16)
            here.append(cot[:, half * 256 + k * HALF : half * 256 + (k + 1) * HALF])
        sums = mm_nt(hits, grad[...]) + mm(hits, jnp.concatenate(here, axis=1))
        s_send[k] = to_rows(sums)
        ret_x1[k].start(pending)
        q_recv[k, o] = s_send[k, o]

    first_hop(0)

    w1_x.wait_recv()
    total1 = jnp.sum(w1_recv[...].astype(F32), axis=0)
    w2_x.wait_recv()
    total2 = jnp.sum(w2_recv[...].astype(F32), axis=0)
    total = jnp.concatenate([total1[:, 128:256], total2[:, 0:384], total1[:, 0:128]], axis=1)
    wu_s[...] = total.astype(BF16).reshape(2, 16, 640)
    for i in range(4):
        left = 384 + 128 * (i % 2)
        hu_s[i] = total2[16 * (i // 2) : 16 * (i // 2) + 16, left : left + 128].astype(BF16)
    wu = pltpu.make_async_remote_copy(
        src_ref=wu_s.at[1 - u],
        dst_ref=wu_r,
        send_sem=sem_sib.at[1, 0, 0],
        recv_sem=sem_sib.at[1, 1, 0],
        device_id=(lax.rem(s + 4, 8), o),
        device_id_type=MESH,
    )
    start_sib(wu)
    hot_x.start(pending)
    hu_r[y] = hu_s[y]
    for k in range(1, CHUNKS):
        first_hop(k)

    r = iota((512, 512), 0)
    pick = onehot(iota((512, 512), 1) == (r & 15) * 32 + (r >> 4))

    def second_hop(k):
        ret_x1[k].wait_recv()
        p_send[k] = mm(pick, q_recv[k].reshape(512, CW)).astype(BF16).reshape(8, 4, 16, CW)
        ret_x2[k].start(pending)
        ret[k, :, s] = p_send[k, s]

    place = {"y": y, "x": x, "z": z}
    device = {
        "y": lambda p: (2 * p + c, o),
        "x": lambda p: (s, 4 * p + z),
        "z": lambda p: (s, 4 * x + p),
    }

    def slab(i, core, known):
        at = dict(place)
        at.update(known)
        return ags[i].at[core, at["y"], at["x"], at["z"]]

    def gather_x(i, stage):
        order = AG_ORDERS[i]
        axis = order[stage]
        whole = {a: slice(None) for a in order[:stage]}
        block = lambda p: slab(i, c, {**whole, axis: p})
        return Exchange(
            4, place[axis], device[axis], lambda p: block(place[axis]), block,
            sem_ag.at[i, stage, 0], sem_ag.at[i, stage, 1],
        )

    def last_slab(i, core, p):
        order = AG_ORDERS[i]
        blk = slab(i, core, {order[0]: slice(None), order[1]: slice(None), order[2]: p})
        return to_sib(blk, blk, 3 + HEAD + i, p)

    gathers = [[gather_x(i, stage) for stage in range(3)] for i in range(3)]
    wu.wait_recv()
    pick_u = u.astype(F32)
    mine = total[0:16] * (1.0 - pick_u) + total[16:32] * pick_u + wu_r[...].astype(F32)
    mine = mine.astype(BF16)
    ag0[c, y, x, z] = mine[:, 0:256]
    ag1[c, y, x, z] = mine[:, 256:512]
    for i in range(2):
        gathers[i][0].start(pending)
    hot_x.wait_recv()
    ag2[c, y, x, z] = jnp.concatenate(
        [mine[:, 512:640], jnp.sum(hu_r[...].astype(F32), axis=0).astype(BF16)], axis=1
    )
    gathers[2][0].start(pending)
    second_hop(0)
    for stage in range(2):
        for i in range(3):
            gathers[i][stage].wait_recv()
            gathers[i][stage + 1].start(pending)
        if stage == 0:
            for k in range(1, CHUNKS):
                second_hop(k)
    for i in range(3):
        start_sib(last_slab(i, c, place[AG_ORDERS[i][2]]))
    for d in (1, 3, 2):
        for i in range(3):
            p = lax.rem(place[AG_ORDERS[i][2]] + d, 4)
            gathers[i][2].wait_from(p)
            start_sib(last_slab(i, c, p))
    for k in chunks:
        ret_x2[k].wait_recv()
    for i in range(3):
        for p in range(4):
            last_slab(i, 1 - c, p).wait_recv()

    for wait in pending:
        wait()


def finish_kernel(a0, a1, a2, ret, asked, gin, gout, ghot, gcold):
    g = pl.program_id(0)
    for yy in range(4):
        for core in range(2):
            user, head = yy // 2, (yy % 2) * 2 + core
            for zz in range(2):
                top = 32 * zz + 16 * user
                b0 = a0[core, yy, 0, zz].astype(F32)
                b1 = a1[core, yy, 0, zz].astype(F32)
                b2 = a2[core, yy, 0, zz].astype(F32)
                for b in range(4):
                    part = (b0, b1)[b // 2][:, (b % 2) * 128 : (b % 2) * 128 + 128]
                    gin[top : top + 16, b * 512 + head * 128 : b * 512 + head * 128 + 128] = part
                low = pl.multiple_of(head * 128 + 32 * (2 * lax.rem(g, 2) + zz) + 16 * user, 16)
                gout[pl.ds(low, 16), pl.ds(pl.multiple_of(g // 2 * 128, 128), 128)] = b2[:, 0:128]
                hot_top = 32 * zz + 16 * (yy // 2)
                left = 256 * core + 128 * (yy % 2)
                ghot[hot_top : hot_top + 16, left : left + 128] = b2[:, 128:256]
    hits = jnp.concatenate([onehot(iota((256, 128), 0) + g * 256 == asked[i : i + 1, :]) for i in range(4)], axis=1)
    for k in range(CHUNKS):
        sums = mm(hits, ret[k].reshape(512, CW))
        for half in range(2):
            left = half * 256 + k * HALF
            gcold[:, left : left + HALF] = sums[:, half * HALF : (half + 1) * HALF]


def on_device(
    d_out, weight_in, weight_out, hot_table, cold_table, cold_ids, cold_counts, event_slots, lengths
):
    vmem = pl.BlockSpec(memory_space=pltpu.VMEM)
    smem = pl.BlockSpec(memory_space=pltpu.SMEM)
    big = lambda *shape: pltpu.VMEM(shape, BF16)
    wide = lambda *shape: pltpu.VMEM(shape, F32)
    sems = pltpu.SemaphoreType.DMA
    outs = [pltpu.VMEM((2, 4, 4, 4, 16, 256), BF16)] * 3 + [
        pltpu.VMEM((CHUNKS, 4, 8, 16, CW), BF16),
        pltpu.VMEM((8, 128), jnp.int32),
    ]
    ints = lambda *shape: pltpu.VMEM(shape, jnp.int32)
    scratch = [
        ints(128, 128),
        ints(8, 16, 128),
        ints(16, 8, 128),
        ints(8, 16, 128),
        ints(2, 8, 256),
        ints(8, 8, 256),
        ints(512, 128),
        wide(512, 128),
        big(HEAD, 4, 8, 16, HW),
        big(HEAD, 8, 4, 16, HW),
        big(HEAD, 16, 32, HW),
        big(HEAD, 16, 32, HW),
        big(HEAD, 2, 256, HW),
        big(HEAD, 8, 256, HW),
        big(8, 256, 512),
        big(512, 512),
        big(512, 512),
        sems((4,)),
        wide(512, 2048),
        big(128, 2048),
        big(128, 2048),
        big(128, 2048),
        big(128, 2048),
        big(2048, 128),
        big(2048, 128),
        big(2048, 128),
        big(10, 512, 512),
        big(10, 512, 512),
        wide(128, 2048),
        wide(128, 2048),
        big(128, 2048),
        big(128, 2048),
        big(2048, 128),
        wide(128, 2048),
        wide(2048, 128),
        wide(2048, 128),
        big(512, 2048),
        wide(4, 4, 2048),
        big(512, 2048),
        wide(512, 256),
        big(CHUNKS, HALF, 2048),
        big(CHUNKS, HALF, 2048),
        big(CHUNKS, HALF, 2048),
        big(CHUNKS, 8, HALF, 256),
        big(CW, 512),
        big(16, 32, 256),
        big(16, 32, 256),
        big(16, 32, 640),
        big(16, 32, 640),
        big(2, 16, 640),
        big(16, 640),
        big(4, 16, 128),
        big(4, 16, 128),
        big(CHUNKS, 16, 32, CW),
        big(CHUNKS, 16, 32, CW),
        big(CHUNKS, 8, 4, 16, CW),
        big(2, 256, 512),
        big(512, 512),
        big(512, 512),
        big(2048, 512),
        sems((4,)),
        sems((3 + HEAD + CHUNKS, 2, 16)),
        sems((2 + HEAD + 2 * CHUNKS, 2, 8)),
        sems((3 + HEAD, 2, 4)),
        sems((3, 3, 2, 4)),
        sems((6 + HEAD, 2, 4)),
    ]
    a0, a1, a2, ret, asked = pl.pallas_call(
        main_kernel,
        out_shape=outs,
        in_specs=[vmem] * 3 + [smem] + [pl.BlockSpec(memory_space=pl.ANY)] * 5,
        out_specs=[vmem] * 5,
        scratch_shapes=scratch,
        compiler_params=pltpu.CompilerParams(
            collective_id=0, has_side_effects=True, vmem_limit_bytes=56 * 1024 * 1024
        ),
        name="layer",
    )(
        cold_ids.T, cold_counts.reshape(1, 128), event_slots, lengths,
        d_out, weight_out, hot_table, cold_table, weight_in,
    )

    part = pl.BlockSpec((2, 4, 1, 2, 16, 256), lambda g: (0, 0, g // 2, lax.rem(g, 2), 0, 0))
    return pl.pallas_call(
        finish_kernel,
        grid=(8,),
        out_shape=[
            jax.ShapeDtypeStruct((512, 2048), F32),
            jax.ShapeDtypeStruct((512, 512), F32),
            jax.ShapeDtypeStruct((512, 512), F32),
            jax.ShapeDtypeStruct((2048, 512), F32),
        ],
        in_specs=[part] * 3
        + [
            pl.BlockSpec((CHUNKS, 4, 8, 16, CW), lambda g: (0, 0, 0, 0, 0)),
            pl.BlockSpec((8, 128), lambda g: (0, 0)),
        ],
        out_specs=[
            pl.BlockSpec((64, 2048), lambda g: (g, 0)),
            pl.BlockSpec((512, 512), lambda g: (0, 0)),
            pl.BlockSpec((64, 512), lambda g: (g, 0)),
            pl.BlockSpec((256, 512), lambda g: (g, 0)),
        ],
        compiler_params=pltpu.CompilerParams(vmem_limit_bytes=24 * 1024 * 1024),
        name="finish",
    )(a0, a1, a2, ret, asked)


def solution(mesh):
    placed = (
        P("own", "seq", None),
        P(),
        P(),
        P(),
        P(("seq", "own"), None),
        P(("seq", "own"), None),
        P(("seq", "own")),
        P("own", "seq"),
        P("own"),
    )
    return jax.shard_map(
        on_device,
        mesh=mesh,
        in_specs=placed,
        out_specs=(P(), P(), P(), P(("seq", "own"), None)),
        check_vma=False,
    )
```

```python
import functools

import jax
import jax.numpy as jnp
from jax import lax
from jax.experimental import pallas as pl
from jax.experimental.pallas import tpu as pltpu
from jax.sharding import PartitionSpec as P

F32 = jnp.float32
BF16 = jnp.bfloat16
MESH = pl.DeviceIdType.MESH
SCALE = 128 ** (-0.5)
AG_ORDERS = (("z", "x", "y"), ("x", "y", "z"), ("y", "z", "x"))
HEAD = 2
HW = 512 // HEAD
CHUNKS = 2
CW = 512 // CHUNKS
HALF = 256 // CHUNKS


def mm(a, b):
    return jnp.dot(a, b, preferred_element_type=F32)


def mm_nt(a, b):
    return lax.dot_general(a, b, (((1,), (1,)), ((), ())), preferred_element_type=F32)


def iota(shape, dim):
    return lax.broadcasted_iota(jnp.int32, shape, dim)


def onehot(hit):
    return hit.astype(F32).astype(BF16)


def hops(step):
    return sum(min(d, 4 - d) for d in step[:2])


STEPS = {
    4: [(2,), (1,), (3,)],
    16: sorted(((dx, dz) for dx in range(4) for dz in range(4) if dx or dz), key=hops, reverse=True),
    8: [(2, 0), (2, 1), (1, 0), (1, 1), (3, 0), (3, 1), (0, 1)],
}


def away(n, me, step):
    if n == 4:
        return lax.rem(me + step[0], 4)
    if n == 16:
        return lax.rem(me // 4 + step[0], 4) * 4 + lax.rem(lax.rem(me, 4) + step[1], 4)
    return lax.rem(me // 2 + step[0], 4) * 2 + lax.rem(lax.rem(me, 2) + step[1], 2)


class Exchange:
    def __init__(self, n, me, device, src, dst, send_sem, recv_sem):
        self.n, self.me, self.device, self.src, self.dst = n, me, device, src, dst
        self.send_sem, self.recv_sem = send_sem, recv_sem

    def _out(self, p):
        return pltpu.make_async_remote_copy(
            src_ref=self.src(p),
            dst_ref=self.dst(self.me),
            send_sem=self.send_sem.at[p],
            recv_sem=self.recv_sem.at[self.me],
            device_id=self.device(p),
            device_id_type=MESH,
        )

    def _in(self, p):
        return pltpu.make_async_remote_copy(
            src_ref=self.src(p),
            dst_ref=self.dst(p),
            send_sem=self.send_sem.at[p],
            recv_sem=self.recv_sem.at[p],
            device_id=self.device(p),
            device_id_type=MESH,
        )

    def peers(self):
        return [away(self.n, self.me, step) for step in STEPS[self.n]]

    def _each(self, f, near_first=False):
        peers = self.peers()
        for p in peers[::-1] if near_first else peers:
            f(p)

    def start(self, pending):
        pending.append(self.wait_send)
        self._each(lambda p: self._out(p).start())

    def start_to(self, p, pending):
        pending.append(lambda: self._out(p).wait_send())
        self._out(p).start()

    def wait_from(self, p):
        self._in(p).wait_recv()

    def wait_recv(self):
        self._each(lambda p: self._in(p).wait_recv(), near_first=True)

    def wait_send(self):
        self._each(lambda p: self._out(p).wait_send())


def main_kernel(
    idst_ref, counts_ref, ev_ref, len_ref, dout_any, wout_any, hot_any, table_any, win_ref,
    ag0, ag1, ag2, ret, asked,
    id_pad, id_loc, id_a, id_b, ev_loc, ev_all, code_col, valid_col,
    got, rows, perm, fetched, e_loc, e_all, c_all,
    wh, wht, wh_sem, slope_pre, u_t, q_t, k_t, v_t, q_n, k_n, v_n,
    w_st, sl_st, att, gg, gat, ga_t, ga_n, gq, gk, gv, g_t, stat,
    hot_hit, hot_acc, sib_s, sib_r, tot, g_r, grad, w1_send, w1_recv, w2_send, w2_recv, wu_s, wu_r, hu_s, hu_r,
    s_send, q_recv, p_send, dout_ref, wout_ref, hot_ref, table_ref, load_sem,
    sem16, sem8, sem4, sem_ag, sem_sib,
):
    s, o = lax.axis_index("seq"), lax.axis_index("own")
    y, c = s // 2, lax.rem(s, 2)
    u, h = s // 4, lax.rem(s, 4)
    x, z = o // 4, lax.rem(o, 4)
    sib = (2 * y + 1 - c, o)
    ags = (ag0, ag1, ag2)
    chunks = range(CHUNKS)
    heads = range(HEAD)
    pending = []

    barrier = pltpu.get_barrier_semaphore()

    for step in STEPS[16]:
        pl.semaphore_signal(barrier, inc=1, device_id=(s, away(16, o, step)), device_id_type=MESH)
    for step in STEPS[8]:
        pl.semaphore_signal(barrier, inc=1, device_id=(away(8, s, step), o), device_id_type=MESH)

    def load_w(b):
        return pltpu.make_async_copy(
            win_ref.at[:, pl.ds(pl.multiple_of(b * 512 + h * 128, 128), 128)],
            wh.at[:, pl.ds(b * 128, 128)],
            wh_sem.at[b],
        )

    loads = [
        pltpu.make_async_copy(a, b, load_sem.at[i])
        for i, (a, b) in enumerate(
            ((dout_any, dout_ref), (table_any, table_ref), (hot_any, hot_ref), (wout_any, wout_ref))
        )
    ]
    for copy in loads:
        copy.start()
    for b in range(4):
        load_w(b).start()

    def own_x(i, src, dst):
        return Exchange(16, o, lambda p: (s, p), src, dst, sem16.at[i, 0], sem16.at[i, 1])

    def seq_x(i, src, dst):
        return Exchange(8, s, lambda p: (p, o), src, dst, sem8.at[i, 0], sem8.at[i, 1])

    def y_x(i, src, dst):
        return Exchange(4, y, lambda p: (2 * p + c, o), src, dst, sem4.at[i, 0], sem4.at[i, 1])

    def head_x(i, src, dst):
        return Exchange(4, h, lambda p: (4 * u + p, o), src, dst, sem4.at[i, 0], sem4.at[i, 1])

    def to_sib(src, dst, i, j):
        return pltpu.make_async_remote_copy(
            src_ref=src, dst_ref=dst, send_sem=sem_sib.at[i, 0, j], recv_sem=sem_sib.at[i, 1, j],
            device_id=sib, device_id_type=MESH,
        )

    def start_sib(copy):
        pending.append(copy.wait_send)
        copy.start()

    ids_x1 = own_x(0, lambda p: id_loc.at[:, p], lambda p: id_a.at[p])
    ids_x2 = seq_x(0, lambda p: id_a.at[:, p], lambda p: id_b.at[p])
    ev_x = seq_x(1, lambda p: ev_loc.at[p // 4], lambda p: ev_all.at[p])
    rows_x1 = [seq_x(2 + k, lambda p, k=k: got.at[k, :, p], lambda p, k=k: rows.at[k, p]) for k in heads]
    ret_x2 = [
        seq_x(2 + HEAD + k, lambda p, k=k: p_send.at[k, p], lambda p, k=k: ret.at[k, :, p]) for k in chunks
    ]
    w1_x = own_x(1, lambda p: w1_send.at[p], lambda p: w1_recv.at[p])
    w2_x = own_x(2, lambda p: w2_send.at[p], lambda p: w2_recv.at[p])
    rows_x2 = [own_x(3 + k, lambda p, k=k: perm.at[k, p], lambda p, k=k: fetched.at[k, p]) for k in heads]
    ret_x1 = [
        own_x(3 + HEAD + k, lambda p, k=k: s_send.at[k, p], lambda p, k=k: q_recv.at[k, p]) for k in chunks
    ]
    cot_x = y_x(0, lambda p: dout_ref.at[p // 2], lambda p: c_all.at[2 * p + c])
    stat_x = head_x(1, lambda p: stat.at[h], lambda p: stat.at[p])
    emb_x = [
        y_x(2 + k, lambda p, k=k: e_loc.at[k, p // 2], lambda p, k=k: e_all.at[k, 2 * p + c]) for k in heads
    ]
    hot_x = y_x(2 + HEAD, lambda p: hu_s.at[p], lambda p: hu_r.at[p])

    def positions(k, p):
        return tot.at[k, :, pl.ds(pl.multiple_of(p * 256, 256), 256)]

    grad_x = [
        seq_x(2 + HEAD + CHUNKS + k, lambda p, k=k: positions(k, p), lambda p, k=k: g_r.at[k, p]) for k in chunks
    ]

    def sib_block(buf, i, yy):
        return to_sib(buf.at[2 * yy + c], buf.at[2 * yy + c], i, yy)

    def sib_block_in(buf, i, yy):
        return to_sib(buf.at[2 * yy + 1 - c], buf.at[2 * yy + 1 - c], i, yy)

    id_pad[...] = jnp.zeros_like(id_pad)
    id_pad[0:4, :] = idst_ref[...]
    id_loc[...] = id_pad[...].T.reshape(8, 16, 128)

    pl.semaphore_wait(barrier, 22)

    ids_x1.start(pending)
    id_a[o] = id_loc[:, o, :]
    loads[0].wait()
    cot_x.start_to(lax.rem(y + 2, 4), pending)

    codes = []
    for uu in range(2):
        e = ev_ref[uu : uu + 1, :]
        cold = e - 512
        code = jnp.where(e < 512, e, 512 + ((cold >> 2) & 15) * 32 + (cold >> 6) * 4 + (cold & 3))
        ev_loc[uu] = jnp.broadcast_to(code, (8, 256))
        codes.append(code)
    code_row = jnp.concatenate(codes, axis=1)
    code_col[...] = jnp.broadcast_to(code_row, (128, 512)).T
    counts = counts_ref[...].astype(F32).astype(BF16)
    l = iota((128, 512), 1)
    pick = onehot(iota((128, 512), 0) == ((l >> 2) & 7) * 16 + (l >> 5))
    valid_row = (iota((8, 512), 1) & 3).astype(F32) < mm(jnp.broadcast_to(counts, (8, 128)), pick)
    valid_row = valid_row[0:1]
    l = iota((512, 128), 0)
    pick = onehot(iota((512, 128), 1) == ((l >> 2) & 7) * 16 + (l >> 5))
    valid_col[...] = (
        (l & 3).astype(F32) < mm_nt(pick, jnp.broadcast_to(counts, (128, 128)))
    ).astype(F32)
    for b in range(4):
        load_w(b).wait()
    wht[...] = wh[...].T
    for copy in loads[1:]:
        copy.wait()
    c_all[s] = dout_ref[u]

    ids_x1.wait_recv()
    ids_x2.start(pending)
    id_b[s] = id_a[:, s, :]
    ids_x2.wait_recv()

    asked_ids = id_b[...].reshape(128, 128)
    for i in range(4):
        hit = onehot(iota((128, 2048), 1) == asked_ids[:, i : i + 1])
        found = mm(hit, table_ref[...]).astype(BF16)
        for k in heads:
            got[k, i] = found[:, k * HW : (k + 1) * HW].reshape(8, 16, HW)
    for k in heads:
        rows_x1[k].start(pending)
        rows[k, s] = got[k, :, s]
    ev_x.start(pending)
    ev_all[s] = ev_loc[u]
    asked[...] = asked_ids.T[0:8, :]
    start_sib(sib_block(c_all, 0, y))
    hot_hits = [onehot(code_col[...] == iota((512, 128), 1) + b * 128) for b in range(4)]
    emb = mm(jnp.concatenate(hot_hits, axis=1), hot_ref[...])
    r = iota((512, 512), 0)
    pick = onehot(iota((512, 512), 1) == (r & 31) * 16 + (r >> 5))
    for k in heads:
        rows_x1[k].wait_recv()
        perm[k] = mm(pick, rows[k].reshape(512, HW)).astype(BF16).reshape(16, 32, HW)
        rows_x2[k].start(pending)
        fetched[k, o] = perm[k, o]
    for d in (1, 3):
        cot_x.start_to(lax.rem(y + d, 4), pending)
    cot_x.wait_from(lax.rem(y + 2, 4))
    start_sib(sib_block(c_all, 0, lax.rem(y + 2, 4)))
    cold_hits = [
        onehot(jnp.logical_and(
            code_col[...] == iota((512, 128), 1) + (512 + b * 128), valid_row[:, b * 128 : (b + 1) * 128]
        ))
        for b in range(4)
    ]
    cold_hits = jnp.concatenate(cold_hits, axis=1)
    for k in heads:
        rows_x2[k].wait_recv()
        part = emb[:, k * HW : (k + 1) * HW] + mm(cold_hits, fetched[k].reshape(512, HW))
        e_loc[k] = part.astype(BF16).reshape(2, 256, HW)
        emb_x[k].start(pending)
        e_all[k, s] = e_loc[k, u]
        start_sib(sib_block(e_all.at[k], 2 + k, y))

    def project(blk):
        cols = pl.ds(pl.multiple_of(blk * 256, 256), 256)
        pre = mm_nt(wht[...], jnp.concatenate([e_all[k, blk] for k in heads], axis=1))
        sig = 0.5 + 0.5 * jnp.tanh(0.5 * pre)
        act = pre * sig
        slope_pre[:, cols] = sig + act * (1.0 - sig)
        act = act.astype(BF16)
        u_t[:, cols] = act[0:128]
        q_t[:, cols] = act[128:256]
        k_t[:, cols] = act[256:384]
        keep = (blk * 256 + iota((1, 256), 1) < len_ref[u]).astype(F32)
        val = (act[384:512].astype(F32) * keep).astype(BF16)
        v_t[:, cols] = val
        q_n[cols, :] = act[128:256].T
        k_n[cols, :] = act[256:384].T
        v_n[cols, :] = val.T

    for d in (1, 3):
        cot_x.wait_from(lax.rem(y + d, 4))
        start_sib(sib_block(c_all, 0, lax.rem(y + d, 4)))
    def arrive(k, d):
        yy = lax.rem(y + d, 4)
        emb_x[k].wait_from(yy)
        start_sib(sib_block(e_all.at[k], 2 + k, yy))

    def project_sib(d):
        yy = lax.rem(y + d, 4)
        for k in heads:
            sib_block_in(e_all.at[k], 2 + k, yy).wait_recv()
        project(2 * yy + 1 - c)

    live = (iota((1, 2048), 1) < len_ref[u]).astype(F32)

    def gate_grad(blk):
        cols = pl.ds(pl.multiple_of(blk * 256, 256), 256)
        here = (blk * 256 + iota((1, 256), 1) < len_ref[u]).astype(F32)
        wo = wout_ref[pl.ds(pl.multiple_of(h * 128, 128), 128), :]
        gg[:, cols] = mm_nt(wo, c_all[blk]) * here

    project(s)
    for k in range(HEAD - 1):
        for d in (1, 3, 2):
            arrive(k, d)
    for d in (0, 2, 1, 3):
        yy = lax.rem(y + d, 4)
        sib_block_in(c_all, 0, yy).wait_recv()
        gate_grad(2 * yy + c)
        gate_grad(2 * yy + 1 - c)
    for d in (1, 3):
        arrive(HEAD - 1, d)
        project(2 * lax.rem(y + d, 4) + c)
    for d in (0, 1, 3):
        project_sib(d)
    arrive(HEAD - 1, 2)
    project(2 * lax.rem(y + 2, 4) + c)
    project_sib(2)

    att[...] = jnp.zeros_like(att)

    def forward(i, j, diag):
        keys = pl.multiple_of(j * 512, 512)
        qs = pl.ds(pl.multiple_of(i * 512, 512), 512)
        at = i * (i + 1) // 2 + j
        for m in range(4):
            half = mm(k_n[pl.ds(keys + m * 128, 128), :], q_t[:, qs]) * (0.5 * SCALE)
            t = jnp.tanh(half)
            a = 1.0 + t
            w = half * a
            slope = a + w * (2.0 - a)
            if diag:
                ok = iota((128, 512), 0) + m * 128 <= iota((128, 512), 1)
                w = jnp.where(ok, w, 0.0)
                slope = jnp.where(ok, slope, 0.0)
            w_st[at, m * 128 : (m + 1) * 128, :] = w.astype(BF16)
            sl_st[at, m * 128 : (m + 1) * 128, :] = slope.astype(BF16)
        att[:, qs] += mm(v_t[:, pl.ds(keys, 512)], w_st[at])

    @pl.loop(0, 4)
    def _(i):
        @pl.loop(0, i)
        def _(j):
            forward(i, j, False)

        forward(i, i, True)

    inv = 1.0 / jnp.full((1, 2048), len_ref[u], jnp.int32).astype(F32)
    mine = att[...] * inv
    m1 = jnp.sum(mine, axis=0, keepdims=True) * (1.0 / 128)
    dev = mine - m1
    gn = gg[...] * u_t[...].astype(F32)
    stat[h, 0:1, :] = m1
    stat[h, 1:2, :] = jnp.sum(dev * dev, axis=0, keepdims=True)
    stat[h, 2:3, :] = jnp.sum(gn, axis=0, keepdims=True)
    stat[h, 3:4, :] = jnp.sum(gn * dev, axis=0, keepdims=True)
    stat_x.start(pending)
    ev_x.wait_recv()
    for blk in range(8):
        hot_hit[:, blk * 256 : (blk + 1) * 256] = onehot(iota((512, 256), 0) == ev_all[blk, 0:1, :])
    part = pl.ds(pl.multiple_of(c * 256, 256), 256)
    sums = jnp.zeros((512, 256), F32)
    for b in range(4):
        blk = 4 * lax.rem(y, 2) + b
        here = (blk * 256 + iota((256, 1), 0) < len_ref[u]).astype(F32)
        kept = (c_all[blk, :, part].astype(F32) * here).astype(BF16)
        sums += mm(hot_hit[:, pl.ds(pl.multiple_of(blk * 256, 256), 256)], kept)
    hot_acc[...] = sums
    stat_x.wait_recv()
    both = stat[...]
    mean = jnp.sum(both[:, 0, :], axis=0, keepdims=True) * 0.25
    off = both[:, 0, :] - mean
    var = (jnp.sum(both[:, 1, :], axis=0, keepdims=True) + 128.0 * jnp.sum(off * off, axis=0, keepdims=True)) * (
        1.0 / 512
    )
    rstd = lax.rsqrt(var + 1e-05)
    mean1 = jnp.sum(both[:, 2, :], axis=0, keepdims=True) * (1.0 / 512)
    mean2 = jnp.sum(both[:, 3, :] + off * both[:, 2, :], axis=0, keepdims=True) * (rstd * (1.0 / 512))
    normed = (att[...] * inv - mean) * rstd
    att[...] = normed
    gn = gg[...] * u_t[...].astype(F32)
    ga_t[...] = ((gn - mean1 - normed * mean2) * (rstd * inv)).astype(BF16)
    for b in range(8):
        ga_n[b * 256 : (b + 1) * 256, :] = ga_t[:, b * 256 : (b + 1) * 256].T

    def to_rows(rows_by_cols):
        n = rows_by_cols.shape[1]
        return rows_by_cols.astype(BF16).reshape(-1, 32, n)

    gat[...] = (att[...] * u_t[...].astype(F32) * live).astype(BF16)
    gw_out = mm(gat[...], c_all[...].reshape(2048, 512))
    for b in range(4):
        w1_send[4 * b : 4 * b + 4, :, 0:128] = to_rows(gw_out[:, b * 128 : (b + 1) * 128])
    g_t[0:128, :] = (gg[...] * att[...] * slope_pre[0:128, :]).astype(BF16)
    n = HW // 32
    for k in heads:
        w1_send[k * n : (k + 1) * n, :, 128:256] = to_rows(mm(g_t[0:128, :], e_all[k].reshape(2048, HW)).T)
    w1_x.start(pending)
    w1_recv[o] = w1_send[o]

    gq[...] = jnp.zeros_like(gq)
    gk[...] = jnp.zeros_like(gk)
    gv[...] = jnp.zeros_like(gv)

    def backward(i, j):
        keys = pl.multiple_of(j * 512, 512)
        qs = pl.ds(pl.multiple_of(i * 512, 512), 512)
        at = i * (i + 1) // 2 + j
        for m in range(4):
            gw = mm(v_n[pl.ds(keys + m * 128, 128), :], ga_t[:, qs])
            ds = gw * sl_st[at, m * 128 : (m + 1) * 128, :].astype(F32)
            sl_st[at, m * 128 : (m + 1) * 128, :] = ds.astype(BF16)
        gk[pl.ds(keys, 512), :] += mm(sl_st[at], q_n[qs, :])
        gv[pl.ds(keys, 512), :] += mm(w_st[at], ga_n[qs, :])
        gq[:, qs] += mm(k_t[:, pl.ds(keys, 512)], sl_st[at])

    @pl.loop(0, 4)
    def _(i):
        @pl.loop(0, i + 1)
        def _(j):
            backward(i, j)

    keep = (iota((1, 2048), 1) < len_ref[u]).astype(F32)
    g_t[128:256, :] = (gq[...] * (0.5 * SCALE) * slope_pre[128:256, :]).astype(BF16)
    for b in range(8):
        cols = slice(b * 256, (b + 1) * 256)
        g_t[256:384, cols] = (gk[cols, :].T * (0.5 * SCALE) * slope_pre[256:384, cols]).astype(BF16)
        g_t[384:512, cols] = (gv[cols, :].T * keep[:, cols] * slope_pre[384:512, cols]).astype(BF16)

    head_sends = list(pending)
    pending.clear()

    def partial(k, half):
        return mm(wh[pl.ds(pl.multiple_of(half * 256 + k * HALF, HALF), HALF), :], g_t[...])

    def sib_grad(k):
        return to_sib(sib_s.at[k], sib_r.at[k], 2 + HEAD, k)

    for k in chunks:
        sib_s[k] = partial(k, 1 - c).astype(BF16)
        start_sib(sib_grad(k))
    for k in chunks:
        total = partial(k, c)
        sib_grad(k).wait_recv()
        tot[k] = (total + sib_r[k].astype(F32)).astype(BF16)
        grad_x[k].start(pending)
        g_r[k, s] = positions(k, s)[...]
        if k == 0:
            for b in heads:
                w2_send[b * n : (b + 1) * n, :, 0:384] = to_rows(mm(g_t[128:512, :], e_all[b].reshape(2048, HW)).T)

    sums = hot_acc[...] + mm_nt(hot_hit[...], tot[...].reshape(256, 2048))
    w2_send[:, :, 384:640] = to_rows(sums)
    w2_x.start(pending)
    w2_recv[o] = w2_send[o]
    for wait in head_sends:
        wait()
    grad_sends = list(pending)
    pending.clear()

    cots = []
    for uu in range(2):
        here = (s * 256 + iota((256, 1), 0) < len_ref[uu]).astype(F32)
        cots.append((dout_ref[uu].astype(F32) * here).astype(BF16))
    cot = jnp.concatenate(cots, axis=0)
    hits = []
    for uu in range(2):
        hit = iota((512, 256), 0) + 512 == ev_loc[uu, 0:1, :]
        hits.append(onehot(jnp.logical_and(hit, jnp.concatenate([valid_col[...]] * 2, axis=1) > 0)))
    hits = jnp.concatenate(hits, axis=1)
    def first_hop(k):
        grad_x[k].wait_recv()
        here = []
        for half in range(2):
            rows_k = slice(half * HALF, (half + 1) * HALF)
            for uu in range(2):
                grad[rows_k, uu * 256 : (uu + 1) * 256] = (
                    g_r[k, 4 * uu + half].astype(F32) + g_r[k, 4 * uu + 2 + half].astype(F32)
                ).astype(BF16)
            here.append(cot[:, half * 256 + k * HALF : half * 256 + (k + 1) * HALF])
        sums = mm_nt(hits, grad[...]) + mm(hits, jnp.concatenate(here, axis=1))
        s_send[k] = to_rows(sums)
        ret_x1[k].start(pending)
        q_recv[k, o] = s_send[k, o]

    first_hop(0)

    w1_x.wait_recv()
    total1 = jnp.sum(w1_recv[...].astype(F32), axis=0)
    w2_x.wait_recv()
    total2 = jnp.sum(w2_recv[...].astype(F32), axis=0)
    total = jnp.concatenate([total1[:, 128:256], total2[:, 0:384], total1[:, 0:128]], axis=1)
    wu_s[...] = total.astype(BF16).reshape(2, 16, 640)
    for i in range(4):
        left = 384 + 128 * (i % 2)
        hu_s[i] = total2[16 * (i // 2) : 16 * (i // 2) + 16, left : left + 128].astype(BF16)
    wu = pltpu.make_async_remote_copy(
        src_ref=wu_s.at[1 - u],
        dst_ref=wu_r,
        send_sem=sem_sib.at[1, 0, 0],
        recv_sem=sem_sib.at[1, 1, 0],
        device_id=(lax.rem(s + 4, 8), o),
        device_id_type=MESH,
    )
    start_sib(wu)
    hot_x.start(pending)
    hu_r[y] = hu_s[y]
    for k in range(1, CHUNKS):
        first_hop(k)

    r = iota((512, 512), 0)
    pick = onehot(iota((512, 512), 1) == (r & 15) * 32 + (r >> 4))

    def second_hop(k):
        ret_x1[k].wait_recv()
        p_send[k] = mm(pick, q_recv[k].reshape(512, CW)).astype(BF16).reshape(8, 4, 16, CW)
        ret_x2[k].start(pending)
        ret[k, :, s] = p_send[k, s]

    place = {"y": y, "x": x, "z": z}
    device = {
        "y": lambda p: (2 * p + c, o),
        "x": lambda p: (s, 4 * p + z),
        "z": lambda p: (s, 4 * x + p),
    }

    def slab(i, core, known):
        at = dict(place)
        at.update(known)
        return ags[i].at[core, at["y"], at["x"], at["z"]]

    def gather_x(i, stage):
        order = AG_ORDERS[i]
        axis = order[stage]
        whole = {a: slice(None) for a in order[:stage]}
        block = lambda p: slab(i, c, {**whole, axis: p})
        return Exchange(
            4, place[axis], device[axis], lambda p: block(place[axis]), block,
            sem_ag.at[i, stage, 0], sem_ag.at[i, stage, 1],
        )

    def last_slab(i, core, p):
        order = AG_ORDERS[i]
        blk = slab(i, core, {order[0]: slice(None), order[1]: slice(None), order[2]: p})
        return to_sib(blk, blk, 3 + HEAD + i, p)

    gathers = [[gather_x(i, stage) for stage in range(3)] for i in range(3)]
    wu.wait_recv()
    pick_u = u.astype(F32)
    mine = total[0:16] * (1.0 - pick_u) + total[16:32] * pick_u + wu_r[...].astype(F32)
    mine = mine.astype(BF16)
    ag0[c, y, x, z] = mine[:, 0:256]
    ag1[c, y, x, z] = mine[:, 256:512]
    for i in range(2):
        gathers[i][0].start(pending)
    hot_x.wait_recv()
    ag2[c, y, x, z] = jnp.concatenate(
        [mine[:, 512:640], jnp.sum(hu_r[...].astype(F32), axis=0).astype(BF16)], axis=1
    )
    gathers[2][0].start(pending)
    for wait in grad_sends:
        wait()
    hop_sends = list(pending)
    pending.clear()
    second_hop(0)
    for stage in range(2):
        for i in range(3):
            gathers[i][stage].wait_recv()
            gathers[i][stage + 1].start(pending)
        if stage == 0:
            for k in range(1, CHUNKS):
                second_hop(k)
    for i in range(3):
        start_sib(last_slab(i, c, place[AG_ORDERS[i][2]]))
    for wait in hop_sends:
        wait()
    for d in (1, 3, 2):
        for i in range(3):
            p = lax.rem(place[AG_ORDERS[i][2]] + d, 4)
            gathers[i][2].wait_from(p)
            start_sib(last_slab(i, c, p))
    for k in chunks:
        ret_x2[k].wait_recv()
    for i in range(3):
        for p in range(4):
            last_slab(i, 1 - c, p).wait_recv()

    for wait in pending:
        wait()


def finish_kernel(a0, a1, a2, ret, asked, gin, gout, ghot, gcold):
    g = pl.program_id(0)
    for yy in range(4):
        for core in range(2):
            user, head = yy // 2, (yy % 2) * 2 + core
            for zz in range(4):
                top = 32 * zz + 16 * user
                b0 = a0[core, yy, 0, zz].astype(F32)
                b1 = a1[core, yy, 0, zz].astype(F32)
                b2 = a2[core, yy, 0, zz].astype(F32)
                for b in range(4):
                    part = (b0, b1)[b // 2][:, (b % 2) * 128 : (b % 2) * 128 + 128]
                    gin[top : top + 16, b * 512 + head * 128 : b * 512 + head * 128 + 128] = part
                low = head * 128 + 32 * zz + 16 * user
                gout[low : low + 16, pl.ds(pl.multiple_of(g * 128, 128), 128)] = b2[:, 0:128]
                hot_top = 32 * zz + 16 * (yy // 2)
                left = 256 * core + 128 * (yy % 2)
                ghot[hot_top : hot_top + 16, left : left + 128] = b2[:, 128:256]
    hits = jnp.concatenate([onehot(iota((512, 128), 0) + g * 512 == asked[i : i + 1, :]) for i in range(4)], axis=1)
    for k in range(CHUNKS):
        sums = mm(hits, ret[k].reshape(512, CW))
        for half in range(2):
            left = half * 256 + k * HALF
            gcold[:, left : left + HALF] = sums[:, half * HALF : (half + 1) * HALF]


def on_device(
    d_out, weight_in, weight_out, hot_table, cold_table, cold_ids, cold_counts, event_slots, lengths
):
    vmem = pl.BlockSpec(memory_space=pltpu.VMEM)
    smem = pl.BlockSpec(memory_space=pltpu.SMEM)
    big = lambda *shape: pltpu.VMEM(shape, BF16)
    wide = lambda *shape: pltpu.VMEM(shape, F32)
    sems = pltpu.SemaphoreType.DMA
    outs = [pltpu.VMEM((2, 4, 4, 4, 16, 256), BF16)] * 3 + [
        pltpu.VMEM((CHUNKS, 4, 8, 16, CW), BF16),
        pltpu.VMEM((8, 128), jnp.int32),
    ]
    ints = lambda *shape: pltpu.VMEM(shape, jnp.int32)
    scratch = [
        ints(128, 128),
        ints(8, 16, 128),
        ints(16, 8, 128),
        ints(8, 16, 128),
        ints(2, 8, 256),
        ints(8, 8, 256),
        ints(512, 128),
        wide(512, 128),
        big(HEAD, 4, 8, 16, HW),
        big(HEAD, 8, 4, 16, HW),
        big(HEAD, 16, 32, HW),
        big(HEAD, 16, 32, HW),
        big(HEAD, 2, 256, HW),
        big(HEAD, 8, 256, HW),
        big(8, 256, 512),
        big(512, 512),
        big(512, 512),
        sems((4,)),
        wide(512, 2048),
        big(128, 2048),
        big(128, 2048),
        big(128, 2048),
        big(128, 2048),
        big(2048, 128),
        big(2048, 128),
        big(2048, 128),
        big(10, 512, 512),
        big(10, 512, 512),
        wide(128, 2048),
        wide(128, 2048),
        big(128, 2048),
        big(128, 2048),
        big(2048, 128),
        wide(128, 2048),
        wide(2048, 128),
        wide(2048, 128),
        big(512, 2048),
        wide(4, 4, 2048),
        big(512, 2048),
        wide(512, 256),
        big(CHUNKS, HALF, 2048),
        big(CHUNKS, HALF, 2048),
        big(CHUNKS, HALF, 2048),
        big(CHUNKS, 8, HALF, 256),
        big(CW, 512),
        big(16, 32, 256),
        big(16, 32, 256),
        big(16, 32, 640),
        big(16, 32, 640),
        big(2, 16, 640),
        big(16, 640),
        big(4, 16, 128),
        big(4, 16, 128),
        big(CHUNKS, 16, 32, CW),
        big(CHUNKS, 16, 32, CW),
        big(CHUNKS, 8, 4, 16, CW),
        big(2, 256, 512),
        big(512, 512),
        big(512, 512),
        big(2048, 512),
        sems((4,)),
        sems((3 + HEAD + CHUNKS, 2, 16)),
        sems((2 + HEAD + 2 * CHUNKS, 2, 8)),
        sems((3 + HEAD, 2, 4)),
        sems((3, 3, 2, 4)),
        sems((6 + HEAD, 2, 4)),
    ]
    a0, a1, a2, ret, asked = pl.pallas_call(
        main_kernel,
        out_shape=outs,
        in_specs=[vmem] * 3 + [smem] + [pl.BlockSpec(memory_space=pl.ANY)] * 5,
        out_specs=[vmem] * 5,
        scratch_shapes=scratch,
        compiler_params=pltpu.CompilerParams(
            collective_id=0, has_side_effects=True, vmem_limit_bytes=56 * 1024 * 1024
        ),
        name="layer",
    )(
        cold_ids.T, cold_counts.reshape(1, 128), event_slots, lengths,
        d_out, weight_out, hot_table, cold_table, weight_in,
    )

    part = pl.BlockSpec((2, 4, 1, 4, 16, 256), lambda g: (0, 0, g, 0, 0, 0))
    return pl.pallas_call(
        finish_kernel,
        grid=(4,),
        out_shape=[
            jax.ShapeDtypeStruct((512, 2048), F32),
            jax.ShapeDtypeStruct((512, 512), F32),
            jax.ShapeDtypeStruct((512, 512), F32),
            jax.ShapeDtypeStruct((2048, 512), F32),
        ],
        in_specs=[part] * 3
        + [
            pl.BlockSpec((CHUNKS, 4, 8, 16, CW), lambda g: (0, 0, 0, 0, 0)),
            pl.BlockSpec((8, 128), lambda g: (0, 0)),
        ],
        out_specs=[
            pl.BlockSpec((128, 2048), lambda g: (g, 0)),
            pl.BlockSpec((512, 512), lambda g: (0, 0)),
            pl.BlockSpec((128, 512), lambda g: (g, 0)),
            pl.BlockSpec((512, 512), lambda g: (g, 0)),
        ],
        compiler_params=pltpu.CompilerParams(vmem_limit_bytes=24 * 1024 * 1024),
        name="finish",
    )(a0, a1, a2, ret, asked)


def solution(mesh):
    placed = (
        P("own", "seq", None),
        P(),
        P(),
        P(),
        P(("seq", "own"), None),
        P(("seq", "own"), None),
        P(("seq", "own")),
        P("own", "seq"),
        P("own"),
    )
    return jax.shard_map(
        on_device,
        mesh=mesh,
        in_specs=placed,
        out_specs=(P(), P(), P(), P(("seq", "own"), None)),
        check_vma=False,
    )
```
